32 devices in a mesh: dp: 16 (over z, x, core), tensor: 2 (over y).
Axes of the slice: x: 2, y: 2, z: 4, core: 2. Of those that a mesh axis runs over, the one named last changes fastest.
Arguments:
- block_input: bfloat16 [16384, 1536], P('dp'), may hold values from -6 to 6
- norm_gain: float32 [1536], replicated, may hold values from 0.5 to 1.5
- z_weight: bfloat16 [1536, 3072], P(None, 'tensor'), may hold values from -0.15625 to 0.15625
- x_weight: bfloat16 [1536, 3072], P(None, 'tensor'), may hold values from -0.15625 to 0.15625
- bc_weight: bfloat16 [1536, 256], replicated, may hold values from -0.15625 to 0.15625
- dt_weight: bfloat16 [1536, 48], P(None, 'tensor'), may hold values from -0.15625 to 0.15625
- x_conv: float32 [4, 3072], P(None, 'tensor'), may hold values from -0.5 to 0.5
- x_conv_bias: float32 [3072], P('tensor'), may hold values from -0.5 to 0.5
- bc_conv: float32 [4, 256], replicated, may hold values from -0.5 to 0.5
- bc_conv_bias: float32 [256], replicated, may hold values from -0.5 to 0.5
- dt_bias: float32 [48], P('tensor'), may hold values from -7 to -2.3
- a_log: float32 [48], P('tensor'), may hold values from 0 to 2.77
- d_skip: float32 [48], P('tensor'), may hold values from 0.5 to 1.5
- gated_gain: float32 [3072], P('tensor'), may hold values from 0.5 to 1.5
- out_weight: bfloat16 [3072, 1536], P('tensor'), may hold values from -0.109375 to 0.109375
- out_cotangent: bfloat16 [16384, 1536], P('dp'), may hold values from -6 to 6
Outputs:
- block_output: bfloat16 [16384, 1536], P('dp')
- input_grad: bfloat16 [16384, 1536], P('dp')
- norm_gain_grad: float32 [1536], P(('dp', 'tensor'))
- z_weight_grad: float32 [1536, 3072], P('dp', 'tensor')
- x_weight_grad: float32 [1536, 3072], P('dp', 'tensor')
- bc_weight_grad: float32 [1536, 256], P(('dp', 'tensor'))
- dt_weight_grad: float32 [1536, 48], P('dp', 'tensor')
- x_conv_grad: float32 [4, 3072], P(None, 'tensor')
- x_conv_bias_grad: float32 [3072], P('tensor')
- bc_conv_grad: float32 [4, 256], P(None, ('dp', 'tensor'))
- bc_conv_bias_grad: float32 [256], P(('dp', 'tensor'))
- dt_bias_grad: float32 [48], P('tensor')
- a_log_grad: float32 [48], P('tensor')
- d_skip_grad: float32 [48], P('tensor')
- gated_gain_grad: float32 [3072], P('tensor')
- out_weight_grad: float32 [3072, 1536], P('tensor', 'dp')
The draws below stay inside these ranges and needn't reach their ends.
All inputs are finite; a program needn't handle non-finite values.
Results may differ from the reference program's by a relative error of at most 0.0076.
Values sent between devices are 32-bit elements; how exact they have to be, the bound alone decides.
No kernel may reach another device: no remote copies, remote signals or barrier semaphores. Data moves between devices by JAX's collectives and lax.ppermute only.
A program may use at most 256 MiB of HBM per device.

```python
import math
import jax
import jax.numpy as jnp
from jax import lax

D = 1536
H = 48
P_SIZE = 64
N = 128
K = 4
SPAN = 256
LEN = 1024
DI = 3072
TOKENS = 16384
N_TENSOR = 2


def with_spikes(array, stream_key, source, target, blocks, factor):
    def block_of(position):
        return (jnp.arange(array.shape[position]) // (array.shape[position] // blocks)).reshape((-1,) + (1,) * (array.ndim - 1 - position))

    one_side = jax.random.permutation(stream_key, blocks)[block_of(target)]
    second = (block_of(target) + blocks // 2) % blocks
    return jnp.where((block_of(source) == one_side) | (block_of(source) == second), factor * array, array)


def levels(stream_key, shape, cuts, low, top_value):
    gain = 1.0
    for axis_at, blocks in cuts:
        heights = jax.random.uniform(jax.random.fold_in(jax.random.fold_in(stream_key, 6), axis_at), (blocks,), jnp.float32, low / len(cuts), top_value / len(cuts))
        gain = gain * jnp.repeat(jnp.exp(heights), shape[axis_at] // blocks).reshape((-1,) + (1,) * (len(shape) - 1 - axis_at))
    return gain


def centred(own_key, shape, deviation, most, shards=(), kind=jnp.bfloat16):
    factor_of = levels(own_key, shape, shards, -0.22, 0.18) if shards else 1.0
    values = jax.random.normal(own_key, shape, jnp.float32) * deviation * factor_of
    return jnp.minimum(jnp.maximum(values, -most), most).astype(kind)


def bell_draw_with(stream_key, shape, width, reach, cuts, heavy, held_as=jnp.bfloat16):
    array = width * jax.random.normal(stream_key, shape, jnp.float32)
    if cuts:
        array = array * levels(stream_key, shape, cuts, -0.22, 0.18)
    return jnp.clip(with_spikes(array, jax.random.fold_in(stream_key, 3), *heavy), -reach, reach).astype(held_as)


def setup_inputs(seed: int = 0) -> dict:
    streams_of = jax.random.split(jax.random.key(seed), 17)
    return {
        "block_input": bell_draw_with(streams_of[0], (TOKENS, D), 1.0, 6.0, ((0, 16),), (0, 1, 16, 2.0)),
        "norm_gain": jnp.clip(1.0 + 0.1 * jax.random.normal(streams_of[1], (D,), jnp.float32), 0.5, 1.5),
        "z_weight": centred(streams_of[2], (D, DI), D ** -0.5, 0.15625, ((1, 2),)),
        "x_weight": centred(streams_of[3], (D, DI), D ** -0.5, 0.15625, ((1, 2),)),
        "bc_weight": centred(streams_of[4], (D, 2 * N), D ** -0.5, 0.15625),
        "dt_weight": centred(streams_of[5], (D, H), D ** -0.5, 0.15625, ((1, 2),)),
        "x_conv": jnp.clip(jax.random.uniform(streams_of[6], (K, DI), jnp.float32, -0.5, 0.5) * levels(streams_of[6], (K, DI), ((1, 2),), -0.4, 0.0), -0.5, 0.5),
        "x_conv_bias": jnp.clip(jax.random.uniform(streams_of[7], (DI,), jnp.float32, -0.5, 0.5) * levels(streams_of[7], (DI,), ((0, 2),), -0.4, 0.0), -0.5, 0.5),
        "bc_conv": jnp.clip(jax.random.uniform(streams_of[8], (K, 2 * N), jnp.float32, -0.5, 0.5), -0.5, 0.5),
        "bc_conv_bias": jnp.clip(jax.random.uniform(streams_of[9], (2 * N,), jnp.float32, -0.5, 0.5), -0.5, 0.5),
        "dt_bias": jnp.clip(-7.0 + 4.7 * jax.random.uniform(streams_of[10], (H,), jnp.float32) ** levels(streams_of[10], (H,), ((0, 2),), -0.2, 0.2), -7.0, -2.3),
        "a_log": jnp.clip(2.77 * jax.random.uniform(streams_of[11], (H,), jnp.float32) ** levels(streams_of[11], (H,), ((0, 2),), -0.2, 0.2), 0.0, 2.77),
        "d_skip": jnp.clip(0.5 + 1.0 * jax.random.uniform(streams_of[12], (H,), jnp.float32) ** levels(streams_of[12], (H,), ((0, 2),), -0.2, 0.2), 0.5, 1.5),
        "gated_gain": jnp.clip(1.0 + 0.1 * jax.random.normal(streams_of[13], (DI,), jnp.float32), 0.5, 1.5),
        "out_weight": centred(streams_of[14], (DI, D), DI ** -0.5, 0.109375, ((0, 2),)),
        "out_cotangent": bell_draw_with(streams_of[15], (TOKENS, D), 1.0, 6.0, ((0, 16),), (0, 1, 16, 2.0)),
    }


EPS = 1e-05
HIGH = lax.Precision.HIGHEST

def scan_heads(inputs_x, steps_dt, decay_a, skip_d, b_mat, c_mat):
    seq_count, length, head_count, head_dim = inputs_x.shape
    span_count = length // SPAN
    state_dim = b_mat.shape[-1]
    weighted = (inputs_x * steps_dt[..., None]).reshape(seq_count, span_count, SPAN, head_count, head_dim)
    rates = (steps_dt * decay_a).reshape(seq_count, span_count, SPAN, head_count)
    within = jnp.cumsum(rates, axis=2)
    b_blocks = b_mat.reshape(seq_count, span_count, SPAN, state_dim)
    c_blocks = c_mat.reshape(seq_count, span_count, SPAN, state_dim)
    scores = jnp.einsum('acln,acsn->acls', c_blocks, b_blocks, precision=HIGH)
    row_index = lax.broadcasted_iota(jnp.int32, (SPAN, SPAN), 0)
    col_index = lax.broadcasted_iota(jnp.int32, (SPAN, SPAN), 1)
    causal = row_index >= col_index
    within_heads = jnp.moveaxis(within, 3, 2)
    log_gaps = within_heads[..., :, None] - within_heads[..., None, :]
    decays = jnp.exp(jnp.where(causal, log_gaps, -jnp.inf))
    mixing = decays * scores[:, :, None]
    diag_out = jnp.einsum('achls,acshp->aclhp', mixing, weighted, precision=HIGH)
    to_end = jnp.exp(within[:, :, -1:, :] - within)
    scaled = weighted * to_end[..., None]
    states = jnp.einsum('acsn,acshp->achpn', b_blocks, scaled, precision=HIGH)
    span_decay = jnp.exp(within[:, :, -1, :])

    def carry_step(carried, pieces):
        decay_now, state_now = pieces
        return (decay_now[:, :, None, None] * carried + state_now, carried)
    initial = jnp.zeros((seq_count, head_count, head_dim, state_dim), jnp.float32)
    last_state, before = lax.scan(carry_step, initial, (jnp.moveaxis(span_decay, 1, 0), jnp.moveaxis(states, 1, 0)))
    before = jnp.moveaxis(before, 0, 1)
    off_out = jnp.einsum('acln,achpn->aclhp', c_blocks, before, precision=HIGH) * jnp.exp(within)[..., None]
    result = (diag_out + off_out).reshape(seq_count, length, head_count, head_dim)
    return result + skip_d[:, None] * inputs_x

def take_heads(values, group_index, head_block, along):
    return lax.dynamic_slice_in_dim(values, group_index * head_block, head_block, along)

def join_heads(stacked):
    moved = jnp.moveaxis(stacked, 0, 2)
    return moved.reshape(moved.shape[:2] + (-1,) + moved.shape[4:])

def ssd_forward(x_heads, steps_dt, decay_a, d_skip, b_mat, c_mat, head_block):
    head_count = x_heads.shape[2]

    def one_group(group_index):
        return scan_heads(take_heads(x_heads, group_index, head_block, 2), take_heads(steps_dt, group_index, head_block, 2), take_heads(decay_a, group_index, head_block, 0), take_heads(d_skip, group_index, head_block, 0), b_mat, c_mat)
    stacked = lax.map(one_group, jnp.arange(head_count // head_block, dtype=jnp.int32))
    return join_heads(stacked)

def ssd_backward(x_heads, steps_dt, decay_a, d_skip, b_mat, c_mat, y_grad, head_block):
    head_count = x_heads.shape[2]

    def one_group(carried, group_index):
        inputs = (take_heads(x_heads, group_index, head_block, 2), take_heads(steps_dt, group_index, head_block, 2), take_heads(decay_a, group_index, head_block, 0), take_heads(d_skip, group_index, head_block, 0))
        outputs, pull = jax.vjp(scan_heads, *inputs, b_mat, c_mat)
        grads = pull(take_heads(y_grad, group_index, head_block, 2))
        return ((carried[0] + grads[4], carried[1] + grads[5]), grads[:4])
    initial = (jnp.zeros_like(b_mat), jnp.zeros_like(c_mat))
    summed, stacked = lax.scan(one_group, initial, jnp.arange(head_count // head_block, dtype=jnp.int32))
    return (join_heads(stacked[0]), join_heads(stacked[1]), stacked[2].reshape(-1), stacked[3].reshape(-1), summed[0], summed[1])

def causal_conv(values, kernel, offsets):
    taps = kernel.shape[0]
    length = values.shape[1]
    padded = jnp.pad(values, ((0, 0), (taps - 1, 0), (0, 0)))
    summed = offsets + jnp.zeros_like(values)
    for offset in range(taps):
        summed = summed + kernel[offset] * padded[:, offset:offset + length]
    return jax.nn.silu(summed)

def conv_section(x_pre, bc_pre, x_conv, x_conv_bias, bc_conv, bc_conv_bias):
    return (causal_conv(x_pre, x_conv, x_conv_bias), causal_conv(bc_pre, bc_conv, bc_conv_bias))

def times_transposed(left, right):
    return lax.dot_general(left, right, (((1,), (1,)), ((), ())), preferred_element_type=jnp.float32)

def over_rows(left, right):
    return lax.dot_general(left, right, (((0,), (0,)), ((), ())), preferred_element_type=jnp.float32)

def reference(block_input, norm_gain, z_weight, x_weight, bc_weight, dt_weight, x_conv, x_conv_bias, bc_conv, bc_conv_bias, dt_bias, a_log, d_skip, gated_gain, out_weight, out_cotangent):
    inner_dim = H * P_SIZE
    group_inner = inner_dim // N_TENSOR
    group_heads = H // N_TENSOR
    head_block = math.gcd(8, group_heads)
    seq_total = block_input.shape[0] // LEN
    inputs_seq = block_input.reshape(seq_total, LEN, D)
    cot_seq = out_cotangent.reshape(seq_total, LEN, D)

    def one_sequence(totals, pieces):
        seq_input, seq_cot = pieces
        residual = seq_input.astype(jnp.float32)
        inv_rms = lax.rsqrt(lax.optimization_barrier(jnp.mean(residual * residual, axis=1, keepdims=True)) + EPS)
        unit_in = residual * inv_rms
        normed = (unit_in * norm_gain).astype(jnp.bfloat16)
        z_pre = jnp.dot(normed, z_weight, preferred_element_type=jnp.float32)
        x_pre = jnp.dot(normed, x_weight, preferred_element_type=jnp.float32).reshape(1, LEN, inner_dim)
        bc_pre = jnp.dot(normed, bc_weight, preferred_element_type=jnp.float32).reshape(1, LEN, 2 * N)
        dt_pre = jnp.dot(normed, dt_weight, preferred_element_type=jnp.float32).reshape(1, LEN, H)
        x_act, bc_act = conv_section(x_pre, bc_pre, x_conv, x_conv_bias, bc_conv, bc_conv_bias)
        dt_sum = dt_pre + dt_bias
        steps_dt = jax.nn.softplus(dt_sum)
        decay_a = -jnp.exp(a_log)
        x_heads = x_act.reshape(1, LEN, H, P_SIZE)
        b_mat = bc_act[..., :N]
        c_mat = bc_act[..., N:]
        mixed = ssd_forward(x_heads, steps_dt, decay_a, d_skip, b_mat, c_mat, head_block).reshape(LEN, inner_dim)
        gate_act = jax.nn.silu(z_pre)
        gated = mixed * gate_act
        gate_rms = lax.rsqrt(lax.optimization_barrier(jnp.mean(gated * gated, axis=1, keepdims=True)) + EPS)
        gated_unit = gated * gate_rms
        mixer_out = (gated_unit * gated_gain).astype(jnp.bfloat16)
        block_output = (residual + jnp.dot(mixer_out, out_weight, preferred_element_type=jnp.float32)).astype(jnp.bfloat16)
        mixer_grad = times_transposed(seq_cot, out_weight)
        out_weight_part = over_rows(mixer_out, seq_cot)
        gated_gain_part = lax.optimization_barrier(jnp.sum(mixer_grad * gated_unit, axis=0))
        unit_grad = mixer_grad * gated_gain
        row_dot = lax.optimization_barrier(jnp.mean(unit_grad * gated_unit, axis=1, keepdims=True))
        gated_grad = gate_rms * (unit_grad - gated_unit * row_dot)
        mixed_grad = (gated_grad * gate_act).reshape(1, LEN, H, P_SIZE)
        gate_sig = jax.nn.sigmoid(z_pre)
        z_grad = (gated_grad * mixed * (gate_sig + z_pre * gate_sig * (1.0 - gate_sig))).astype(jnp.bfloat16)
        normed_grad = times_transposed(z_grad, z_weight)
        z_weight_part = over_rows(normed, z_grad)
        bc_low_total = jnp.zeros((LEN, 2 * N), jnp.float32)
        bc_conv_part = jnp.zeros_like(bc_conv)
        bc_conv_bias_part = jnp.zeros_like(bc_conv_bias)
        x_parts, dt_parts, xc_parts, xcb_parts, dtb_parts, alog_parts, skip_parts = ([], [], [], [], [], [], [])
        for group_index in range(N_TENSOR):
            column_range = slice(group_index * group_inner, (group_index + 1) * group_inner)
            head_range = slice(group_index * group_heads, (group_index + 1) * group_heads)
            outputs, conv_pull = jax.vjp(conv_section, x_pre[..., column_range], bc_pre, x_conv[:, column_range], x_conv_bias[column_range], bc_conv, bc_conv_bias)
            x_heads_grad, dt_grad, a_grad, skip_part, b_grad, c_grad = ssd_backward(x_heads[:, :, head_range], steps_dt[:, :, head_range], decay_a[head_range], d_skip[head_range], b_mat, c_mat, mixed_grad[:, :, head_range], head_block)
            dt_pre_grad = dt_grad * jax.nn.sigmoid(dt_sum[:, :, head_range])
            conv_grads = conv_pull((x_heads_grad.reshape(1, LEN, group_inner), jnp.concatenate((b_grad, c_grad), axis=2)))
            x_pre_low = conv_grads[0].reshape(LEN, group_inner).astype(jnp.bfloat16)
            bc_pre_low = conv_grads[1].reshape(LEN, 2 * N).astype(jnp.bfloat16)
            dt_pre_low = dt_pre_grad.reshape(LEN, group_heads).astype(jnp.bfloat16)
            normed_grad = normed_grad + times_transposed(x_pre_low, x_weight[:, column_range]) + times_transposed(bc_pre_low, bc_weight) + times_transposed(dt_pre_low, dt_weight[:, head_range])
            bc_low_total = bc_low_total + bc_pre_low.astype(jnp.float32)
            bc_conv_part = bc_conv_part + conv_grads[4]
            bc_conv_bias_part = bc_conv_bias_part + conv_grads[5]
            x_parts.append(over_rows(normed, x_pre_low))
            dt_parts.append(over_rows(normed, dt_pre_low))
            xc_parts.append(conv_grads[2])
            xcb_parts.append(conv_grads[3])
            dtb_parts.append(lax.optimization_barrier(jnp.sum(dt_pre_grad, axis=(0, 1))))
            alog_parts.append(a_grad * decay_a[head_range])
            skip_parts.append(skip_part)
        bc_weight_part = lax.dot_general(normed.astype(jnp.float32), bc_low_total, (((0,), (0,)), ((), ())), precision=HIGH)
        norm_gain_part = lax.optimization_barrier(jnp.sum(normed_grad * unit_in, axis=0))
        in_unit_grad = normed_grad * norm_gain
        input_part = inv_rms * (in_unit_grad - unit_in * lax.optimization_barrier(jnp.mean(in_unit_grad * unit_in, axis=1, keepdims=True)))
        input_grad = (seq_cot.astype(jnp.float32) + input_part).astype(jnp.bfloat16)
        parts = (norm_gain_part, z_weight_part, jnp.concatenate(x_parts, axis=1), bc_weight_part, jnp.concatenate(dt_parts, axis=1), jnp.concatenate(xc_parts, axis=1), jnp.concatenate(xcb_parts), bc_conv_part, bc_conv_bias_part, jnp.concatenate(dtb_parts), jnp.concatenate(alog_parts), jnp.concatenate(skip_parts), gated_gain_part, out_weight_part)
        return (tuple((total + part for total, part in zip(totals, parts))), (block_output, input_grad))
    shapes = (norm_gain.shape, z_weight.shape, x_weight.shape, bc_weight.shape, dt_weight.shape, x_conv.shape, x_conv_bias.shape, bc_conv.shape, bc_conv_bias.shape, dt_bias.shape, a_log.shape, d_skip.shape, gated_gain.shape, out_weight.shape)
    initial = tuple((jnp.zeros(shape, jnp.float32) for shape in shapes))
    totals, outputs = lax.scan(one_sequence, initial, (inputs_seq, cot_seq))
    block_output = outputs[0].reshape(seq_total * LEN, D)
    input_grad = outputs[1].reshape(seq_total * LEN, D)
    return (block_output, input_grad, totals[0], totals[1], totals[2], totals[3], totals[4], totals[5], totals[6], totals[7], totals[8], totals[9], totals[10], totals[11], totals[12], totals[13])
```

```python
import functools
import math

import jax
import jax.numpy as jnp
from jax import lax
from jax.experimental import pallas as pl
from jax.experimental.pallas import tpu as pltpu
from jax.sharding import PartitionSpec as P

SPAN = 256
LEN = 1024
EPS = 1e-05
HIGH = lax.Precision.HIGHEST
LOG2E = math.log2(math.e)
F32 = jnp.float32
BF16 = jnp.bfloat16
HALO = 8
GROUP = 32
VMEM = 56 * 1024 * 1024


class Named(dict):
    __getattr__ = dict.get
    __setattr__ = dict.__setitem__


def mm(a, b):
    return lax.dot_general(a, b, (((1,), (0,)), ((), ())), preferred_element_type=F32)


def mm_nt(a, b):
    return lax.dot_general(a, b, (((1,), (1,)), ((), ())), preferred_element_type=F32)


def mm_tn(a, b):
    return lax.dot_general(a, b, (((0,), (0,)), ((), ())), preferred_element_type=F32)


def split3(x):
    hi = x.astype(BF16)
    rest = x - hi.astype(F32)
    mid = rest.astype(BF16)
    low = (rest - mid.astype(F32)).astype(BF16)
    return hi, mid, low


def split2(x):
    hi = x.astype(BF16)
    return hi, (x - hi.astype(F32)).astype(BF16)


def side(a, b):
    return jnp.concatenate((a, b), axis=1)


def folded(x):
    half = x.shape[1] // 2
    return x[:, :half] + x[:, half:]


def fine_nn(left_pair, b):
    bh, bl = split2(b)
    depth = b.shape[0]
    return mm(left_pair, jnp.concatenate((bh, bh), axis=0)) + mm(left_pair[:, :depth], bl)


def fine_rows(left_stack, b):
    bh, bl = split2(b)
    rows = left_stack.shape[0] // 2
    both = mm(left_stack, bh)
    return both[:rows] + both[rows:] + mm(left_stack[:rows], bl)


def fine_nt(a, b):
    ah, al = split2(a)
    bh, bl = split2(b)
    return folded(mm_nt(ah, jnp.concatenate((bh, bl), axis=0))) + mm_nt(al, bh)


def iota(shape, axis):
    return lax.broadcasted_iota(jnp.int32, shape, axis)


def softplus(v):
    return jnp.maximum(v, 0.0) + jnp.log1p(jnp.exp(-jnp.abs(v)))


def three_parts(x):
    hi, mid, low = split3(x)
    lane = iota(x.shape, 1)
    parts = jnp.where(
        lane < GROUP, hi.astype(F32), jnp.where(lane < 2 * GROUP, mid.astype(F32), low.astype(F32))
    )
    return parts.astype(BF16)


def spread_matrix(block, heads, head_dim, lanes):
    shape = (lanes, heads * head_dim)
    row, col = iota(shape, 0), iota(shape, 1)
    head = block * heads + col // head_dim
    hit = (row == head) | (row == head + GROUP) | (row == head + 2 * GROUP)
    return jnp.where(hit, 1.0, 0.0).astype(BF16)


def gather_matrix(block, heads, head_dim, lanes):
    shape = (heads * head_dim, lanes)
    row, col = iota(shape, 0), iota(shape, 1)
    return jnp.where(col == block * heads + row // head_dim, 1.0, 0.0).astype(BF16)


def triangle(n, lower):
    row, col = iota((n, n), 0), iota((n, n), 1)
    return jnp.where(row >= col if lower else row <= col, 1.0, 0.0)


def pair_masks(head_dim):
    lane = iota((1, 4 * head_dim), 1) // head_dim % 2
    return [jnp.where(lane == k, 1.0, 0.0).astype(BF16) for k in range(2)]


def pair_parts(parts, head_dim, pair):
    at = slice(2 * pair * head_dim, 2 * (pair + 1) * head_dim)
    return side(parts[0][:, at], parts[1][:, at])


def conv_of(buf, taps_ref, bias_ref, rows):
    taps = taps_ref.shape[0]
    total = bias_ref[...] + taps_ref[0:1, :] * buf[HALO - taps + 1 : HALO - taps + 1 + rows, :]
    for k in range(1, taps):
        start = HALO - taps + 1 + k
        total = total + taps_ref[k : k + 1, :] * buf[start : start + rows, :]
    return total


def silu_slope(v, s):
    return s + v * s * (1.0 - s)


def steps_of(dt_pre, dt_bias_ref, a_log_ref):
    dt = softplus(dt_pre + dt_bias_ref[...])
    decay = -jnp.exp(a_log_ref[...])
    rates = dt * (decay * LOG2E)
    cum = jnp.dot(triangle(dt.shape[0], True), rates, precision=HIGH, preferred_element_type=F32)
    return dt, decay, cum


def fwd_kernel(first, heads, head_dim, refs):
    j = pl.program_id(0)
    r = refs
    rows = r.xin.shape[0]
    half = rows // 2
    states = r.bc_w.shape[1] // 2
    lanes = r.dt_w.shape[1]

    @pl.when(j == 0)
    def _():
        res = r.xin[...].astype(F32)
        inv = lax.rsqrt(jnp.mean(res * res, axis=1, keepdims=True) + EPS)
        normed = (res * inv * r.norm_gain[...]).astype(BF16)
        r.normed[...] = normed
        bc_pre = mm(normed, r.bc_w[...])
        r.bc_pre[...] = bc_pre
        buf = r.bc_buf
        buf[0:HALO, :] = jnp.zeros((HALO, 2 * states), F32) if first else r.bc_halo[...]
        buf[HALO : HALO + rows, :] = bc_pre
        r.bc_halo_out[...] = bc_pre[rows - HALO :, :]
        u = conv_of(buf, r.bc_conv, r.bc_conv_bias, rows)
        act = u * jax.nn.sigmoid(u)
        b, c = act[:, :states], act[:, states:]
        r.cb[...] = side(*split2(c))
        r.bt[...] = jnp.concatenate(split2(b.T), axis=0)
        r.scores[...] = fine_nt(c, b) * triangle(rows, True)
        dt_pre = mm(normed, r.dt_w[...])
        r.dt_pre[...] = dt_pre
        dt, decay, cum = steps_of(dt_pre, r.dt_bias, r.a_log)
        r.cum_t[...] = cum.T
        r.parts[0:rows, :] = three_parts(cum)
        r.parts[rows : 2 * rows, :] = three_parts(dt)
        r.u_out[...] = jnp.zeros_like(r.u_out)
        r.acc[...] = jnp.zeros_like(r.acc)

    width = heads * head_dim
    normed = r.normed[...]
    xp = mm(normed, r.x_w[...])
    zp = mm(normed, r.z_w[...])
    mg = mm_nt(r.cot[...], r.out_w[...])
    r.x_pre[...] = xp
    r.z_pre[...] = zp
    r.mg[...] = mg
    buf = r.x_buf
    buf[0:HALO, :] = jnp.zeros((HALO, width), F32) if first else r.x_halo[...]
    buf[HALO : HALO + rows, :] = xp
    r.x_halo_out[...] = xp[rows - HALO :, :]
    u = conv_of(buf, r.x_conv, r.x_conv_bias, rows)
    xa = u * jax.nn.sigmoid(u)
    spread = mm(r.parts[...], spread_matrix(j, heads, head_dim, lanes))
    cum_e, dt_e = spread[:rows], spread[rows:]
    w = xa * dt_e
    last = cum_e[rows - 1 : rows, :]
    scaled = w * jnp.exp2(last - cum_e)
    masks = pair_masks(head_dim)
    parts = split2(w)
    cols = []
    for pair in range(heads // 2):
        both = pair_parts(parts, head_dim, pair)
        top = bot = 0.0
        for k in range(2):
            head = 2 * pair + k
            row = r.cum_t[pl.ds(j * heads + head, 1), :]
            col = cum_e[:, head * head_dim : head * head_dim + 1]
            wk = both * masks[k]
            m = jnp.exp2(jnp.minimum(col[:half] - row[:, :half], 0.0)) * r.scores[:half, :half]
            hi, low = split2(m)
            top = top + mm(hi, wk[:half]) + mm(low, wk[:half])
            m = jnp.exp2(jnp.minimum(col[half:] - row, 0.0)) * r.scores[half:, :]
            hi, low = split2(m)
            bot = bot + mm(hi, wk) + mm(low, wk)
        cols.append(folded(jnp.concatenate((top, bot), axis=0)))
    y = side(*cols)
    if first:
        r.state_out[...] = fine_rows(r.bt[...], scaled)
    else:
        state = r.state[...]
        y = y + jnp.exp2(cum_e) * fine_nn(r.cb[...], state)
        r.state_out[...] = jnp.exp2(last) * state + fine_rows(r.bt[...], scaled)
    r.y[...] = y
    mixed = y + r.d_skip[...] * xa
    gated = mixed * (zp * jax.nn.sigmoid(zp))
    gain = gated * r.gated_gain[...]
    gb = gain.astype(BF16)
    r.gb[...] = gb
    r.u_out[...] += mm(gb, r.out_w[...])
    r.acc[0:rows, :] += gated * gated
    r.acc[rows : 2 * rows, :] += mg * gain

    @pl.when(j == pl.num_programs(0) - 1)
    def _():
        ones = jnp.ones((HALO, width), F32)
        sums = lax.dot_general(
            ones, r.acc[...], (((1,), (1,)), ((), ())), precision=HIGH, preferred_element_type=F32
        )
        r.sums[0:1, :] = sums[0:1, :rows]
        r.sums[1:2, :] = sums[0:1, rows:]
        r.sums[2:HALO, :] = jnp.zeros((HALO - 2, rows), F32)


def bwd_kernel(first, last_chunk, heads, head_dim, inner_total, refs):
    j = pl.program_id(0)
    r = refs
    rows = r.xin.shape[0]
    half = rows // 2
    states = r.bc_w.shape[1] // 2
    lanes = r.dt_w.shape[1]
    width = heads * head_dim
    taps = r.x_conv.shape[0]

    def fill(buf, halo, values, columns):
        buf[0:HALO, :] = jnp.zeros((HALO, columns), F32) if first else halo[...]
        buf[HALO : HALO + rows, :] = values

    def conv_back(buf, halo, grad, taps_ref, columns):
        buf[0:rows, :] = grad
        buf[rows : rows + HALO, :] = jnp.zeros((HALO, columns), F32) if last_chunk else halo[...]
        total = taps_ref[taps - 1 : taps, :] * grad
        for k in range(taps - 1):
            total = total + taps_ref[k : k + 1, :] * buf[taps - 1 - k : taps - 1 - k + rows, :]
        return total

    def column_sum(v):
        return jnp.sum(v, axis=0, keepdims=True)

    @pl.when(j == 0)
    def _():
        bc_pre = r.bc_pre[...]
        fill(r.bc_buf, r.bc_halo, bc_pre, 2 * states)
        u = conv_of(r.bc_buf, r.bc_conv, r.bc_conv_bias, rows)
        s = jax.nn.sigmoid(u)
        act = u * s
        r.bc_slope[...] = silu_slope(u, s)
        b, c = act[:, :states], act[:, states:]
        r.bb[...] = side(*split2(b))
        r.cb[...] = side(*split2(c))
        r.ct[...] = jnp.concatenate(split2(c.T), axis=0)
        r.scores[...] = fine_nt(b, c) * triangle(rows, False)
        dt, decay, cum = steps_of(r.dt_pre[...], r.dt_bias, r.a_log)
        r.dt[...] = dt
        r.cum_t[...] = cum.T
        r.parts[0:rows, :] = three_parts(cum)
        r.parts[rows : 2 * rows, :] = three_parts(dt)
        for ref in (r.d_scores, r.db, r.dc, r.d_cum, r.d_dt, r.ng):
            ref[...] = jnp.zeros_like(ref)
        sums = (r.sums[...] + r.sums_other[...]).T
        rms = lax.rsqrt(sums[:, 0:1] / inner_total + EPS)
        r.rows[:, 0:1] = rms
        r.rows[:, 1:2] = sums[:, 1:2] * rms / inner_total

    xp = r.x_pre[...]
    fill(r.x_buf, r.x_halo, xp, width)
    u = conv_of(r.x_buf, r.x_conv, r.x_conv_bias, rows)
    su = jax.nn.sigmoid(u)
    xa = u * su
    spread = mm(r.parts[...], spread_matrix(j, heads, head_dim, lanes))
    cum_e, dt_e = spread[:rows], spread[rows:]
    w = xa * dt_e
    last = cum_e[rows - 1 : rows, :]
    rms, row_dot = r.rows[:, 0:1], r.rows[:, 1:2]
    zp, mg, y = r.z_pre[...], r.mg[...], r.y[...]
    sz = jax.nn.sigmoid(zp)
    gate = zp * sz
    d_skip = r.d_skip[...]
    mixed = y + d_skip * xa
    gated_unit = mixed * gate * rms
    gg = rms * (mg * r.gated_gain[...] - gated_unit * row_dot)
    dy = gg * gate
    zl = (gg * mixed * silu_slope(zp, sz)).astype(BF16)
    r.z_low[...] = zl
    sums = [column_sum(mg * gated_unit), column_sum(dy * xa)]
    masks = pair_masks(head_dim)
    w_parts = split2(w)
    dy_parts = split2(dy)
    cols = []
    for pair in range(heads // 2):
        at = slice(2 * pair * head_dim, 2 * (pair + 1) * head_dim)
        w_both = pair_parts(w_parts, head_dim, pair)
        w_high = w_parts[0][:, at]
        dy_both = pair_parts(dy_parts, head_dim, pair)
        dy_high = side(dy_parts[0][:, at], dy_parts[0][:, at])
        dy_low = dy_parts[1][:, at]
        top = bot = 0.0
        for k in range(2):
            head = 2 * pair + k
            row = r.cum_t[pl.ds(j * heads + head, 1), :]
            col = cum_e[:, head * head_dim : head * head_dim + 1]
            dk, dk_high = dy_both * masks[k], dy_high * masks[k]
            dk_low = dy_low * masks[k][:, : 2 * head_dim]
            decay = jnp.exp2(jnp.minimum(row - col[:half], 0.0))
            grad = mm_nt(w_both[:half], dk_high) + mm_nt(w_high[:half], dk_low)
            r.d_scores[:half, :] += grad * decay
            hi, low = split2(decay * r.scores[:half, :])
            top = top + mm(hi, dk) + mm(low, dk)
            decay = jnp.exp2(jnp.minimum(row[:, half:] - col[half:], 0.0))
            grad = mm_nt(w_both[half:], dk_high[half:]) + mm_nt(w_high[half:], dk_low[half:])
            r.d_scores[half:, half:] += grad * decay
            hi, low = split2(decay * r.scores[half:, half:])
            bot = bot + mm(hi, dk[half:]) + mm(low, dk[half:])
        cols.append(folded(jnp.concatenate((top, bot), axis=0)))
    dw = side(*cols)
    extra = None
    if not last_chunk:
        to_end = jnp.exp2(last - cum_e)
        d_state = r.d_state[...]
        ds = fine_nn(r.bb[...], d_state) * to_end
        r.db[...] += fine_nt(w * to_end, d_state)
        dw = dw + ds
        extra = column_sum(w * ds)
    if not first:
        state = r.state[...]
        g = jnp.exp2(cum_e) * dy
        r.dc[...] += fine_nt(g, state)
        d_state_out = fine_rows(r.ct[...], g)
        if not last_chunk:
            kept = jnp.exp2(last) * d_state
            extra = extra + column_sum(kept * state)
            d_state_out = d_state_out + kept
        r.d_state_out[...] = d_state_out
    q = dy * y - w * dw
    if extra is not None:
        q = q + jnp.where(iota((rows, 1), 0) == rows - 1, 1.0, 0.0) * extra
    gather = gather_matrix(j, heads, head_dim, lanes)
    hi, mid, low = split3(q)
    r.d_cum[...] += mm(hi, gather) + mm(mid, gather) + mm(low, gather)
    hi, mid, low = split3(dw * xa)
    r.d_dt[...] += mm(hi, gather) + mm(mid, gather)
    du = (d_skip * dy + dw * dt_e) * silu_slope(u, su)
    xg = conv_back(r.x_grad_buf, r.du_halo, du, r.x_conv, width)
    r.du_halo_out[...] = du[:HALO, :]
    for k in range(taps):
        start = HALO - taps + 1 + k
        sums.append(column_sum(du * r.x_buf[start : start + rows, :]))
    sums.append(column_sum(du))
    for at, value in enumerate(sums):
        before = 0.0 if last_chunk else r.x_sums_in[at : at + 1, :]
        r.x_sums[at : at + 1, :] = value + before
    r.x_sums[len(sums) : HALO, :] = jnp.zeros((HALO - len(sums), width), F32)
    xl = xg.astype(BF16)
    r.x_low[...] = xl
    r.ng[...] += mm_nt(zl, r.z_w[...]) + mm_nt(xl, r.x_w[...])

    @pl.when(j == pl.num_programs(0) - 1)
    def _():
        hi, low = split2(r.d_scores[...] * triangle(rows, False))
        cb, bb = r.cb[...], r.bb[...]
        db = r.db[...] + folded(mm(hi, cb)) + mm(low, cb[:, :states])
        dc = r.dc[...] + folded(mm_tn(hi, bb)) + mm_tn(low, bb[:, :states])
        d_rates = jnp.dot(
            triangle(rows, False), r.d_cum[...], precision=HIGH, preferred_element_type=F32
        )
        dt = r.dt[...]
        decay = -jnp.exp(r.a_log[...])
        d_dt = d_rates * decay + r.d_dt[...]
        dtg = d_dt * jax.nn.sigmoid(r.dt_pre[...] + r.dt_bias[...])
        dtl = jnp.where(iota(dtg.shape, 1) < GROUP, dtg, 0.0).astype(BF16)
        r.dt_low[...] = dtl
        head_sums = [column_sum(dtg), column_sum(d_rates * dt) * decay]
        for at, value in enumerate(head_sums):
            before = 0.0 if last_chunk else r.head_sums_in[at : at + 1, :]
            r.head_sums[at : at + 1, :] = value + before
        r.head_sums[2:HALO, :] = jnp.zeros((HALO - 2, lanes), F32)
        du_bc = jnp.concatenate((db, dc), axis=1) * r.bc_slope[...]
        bg = conv_back(r.bc_grad_buf, r.du_bc_halo, du_bc, r.bc_conv, 2 * states)
        r.du_bc_halo_out[...] = du_bc[:HALO, :]
        bc_sums = []
        for k in range(taps):
            start = HALO - taps + 1 + k
            bc_sums.append(column_sum(du_bc * r.bc_buf[start : start + rows, :]))
        bc_sums.append(column_sum(du_bc))
        for at, value in enumerate(bc_sums):
            before = 0.0 if last_chunk else r.bc_sums_in[at : at + 1, :]
            r.bc_sums[at : at + 1, :] = value + before
        r.bc_sums[len(bc_sums) : HALO, :] = jnp.zeros((HALO - len(bc_sums), 2 * states), F32)
        bl = bg.astype(BF16)
        r.bc_low[...] = bl
        ng = r.ng[...] + mm_nt(bl, r.bc_w[...]) + mm_nt(dtl, r.dt_w[...])
        res = r.xin[...].astype(F32)
        inv = lax.rsqrt(jnp.mean(res * res, axis=1, keepdims=True) + EPS)
        unit = res * inv
        gain_sum = column_sum(ng * unit)
        r.gain_sums[0:1, :] = gain_sum if last_chunk else gain_sum + r.gain_sums_in[0:1, :]
        r.gain_sums[1:HALO, :] = jnp.zeros((HALO - 1, gain_sum.shape[1]), F32)
        iu = ng * r.norm_gain[...]
        r.in_part[...] = inv * (iu - unit * jnp.mean(iu * unit, axis=1, keepdims=True))


def run_kernel(body, grid, operands, outs, scratch, carried, flops, moved):
    names, arrays, specs = [], [], []
    for name, (array, block, index) in operands.items():
        names.append(name)
        arrays.append(array)
        specs.append(pl.BlockSpec(block, index))
    aliases = {}
    out_names = list(outs)
    for at, name in enumerate(out_names):
        if name in carried:
            aliases[len(arrays)] = at
            names.append(name + "_old")
            arrays.append(carried[name])
            specs.append(pl.BlockSpec(memory_space=pl.ANY))
    scratch_names = list(scratch)

    def kernel(*refs):
        body(Named(zip(names + out_names + scratch_names, refs)))

    given = pl.pallas_call(
        kernel,
        grid=(grid,),
        in_specs=specs,
        out_specs=[pl.BlockSpec(block, index) for _, block, index in outs.values()],
        out_shape=[shape for shape, _, _ in outs.values()],
        scratch_shapes=[pltpu.VMEM(shape, kind) for shape, kind in scratch.values()],
        input_output_aliases=aliases,
        compiler_params=pltpu.CompilerParams(
            dimension_semantics=("arbitrary",), vmem_limit_bytes=VMEM
        ),
        cost_estimate=pl.CostEstimate(flops=flops, bytes_accessed=moved, transcendentals=0),
    )(*arrays)
    return Named(zip(out_names, given))


def shape(*dims, kind=F32):
    return jax.ShapeDtypeStruct(dims, kind)


def stage_sizes(n):
    sizes = []
    while n > 1 and len(sizes) < 2 and n % 2 == 0:
        sizes.append(2)
        n //= 2
    while n > 1:
        part = 4 if n % 4 == 0 else (2 if n % 2 == 0 else n)
        sizes.append(part)
        n //= part
    return sizes


def hops(n, stride, size, step, keep):
    pairs = []
    for d in range(n):
        place = d // stride % size
        if keep(place) and 0 <= place + step < size:
            pairs.append((d, d + step * stride))
    return pairs


def line_sum(values, n, stride, size):
    place = lax.axis_index("dp") // stride % size

    def block(at):
        return lax.dynamic_index_in_dim(values, jnp.clip(at, 0, size - 1), 0, keepdims=False)

    if size == 2:
        other = lax.ppermute(
            block(1 - place), "dp", hops(n, stride, size, 1, lambda p: True)
            + hops(n, stride, size, -1, lambda p: True)
        )
        return block(place) + other
    right = left = None
    for step in range(1, size):
        send = block(size - step + place)
        send = send if right is None else send + right
        right = lax.ppermute(send, "dp", hops(n, stride, size, 1, lambda p: p <= step - 1))
        send = block(step + place - size)
        send = send if left is None else send + left
        left = lax.ppermute(send, "dp", hops(n, stride, size, -1, lambda p: p >= size - step))
    return block(place) + right + left


def doubling_sum(values, n):
    step = 1
    while step < n:
        if n % (2 * step):
            return lax.psum(values, "dp")
        values = values + lax.ppermute(values, "dp", [(d, d ^ step) for d in range(n)])
        step *= 2
    return values


def by_stage(left, n):
    sizes = stage_sizes(n)
    rows, depth = left.shape
    cut = left.reshape(tuple(reversed(sizes)) + (rows // n, depth))
    k = len(sizes)
    return jnp.transpose(cut, tuple(range(k - 1, -1, -1)) + (k, k + 1))


def scattered_product(left, right, n):
    sizes = stage_sizes(n)
    rest, depth = left.shape[-2:]
    if not sizes:
        return jnp.dot(left.reshape(-1, depth), right, preferred_element_type=F32)
    if sizes[0] != 2:
        total = jnp.dot(left.reshape(-1, depth), right, preferred_element_type=F32)
        total = total.reshape(left.shape[:-1] + (right.shape[1],))
        stride = 1
        for size in sizes:
            total = line_sum(total, n, stride, size)
            stride *= size
        return total
    place = lax.axis_index("dp") % 2

    def share(at):
        mine = lax.dynamic_index_in_dim(left, at, 0, keepdims=False).reshape(-1, depth)
        return jnp.dot(mine, right, preferred_element_type=F32)

    other = lax.ppermute(share(1 - place), "dp", [(d, d ^ 1) for d in range(n)])
    total = share(place) + other
    total = total.reshape(left.shape[1:-1] + (right.shape[1],))
    stride = 2
    for size in sizes[1:]:
        total = line_sum(total, n, stride, size)
        stride *= size
    return total


def swap_tensor(values, n):
    return lax.ppermute(values, "tensor", [(t, t ^ 1) for t in range(n)])


def body(
    block_input,
    norm_gain,
    z_weight,
    x_weight,
    bc_weight,
    dt_weight,
    x_conv,
    x_conv_bias,
    bc_conv,
    bc_conv_bias,
    dt_bias,
    a_log,
    d_skip,
    gated_gain,
    out_weight,
    out_cotangent,
):
    n_dp, n_tensor = lax.axis_size("dp"), lax.axis_size("tensor")
    rows, model = block_input.shape
    inner = x_weight.shape[1]
    head_count = dt_weight.shape[1]
    head_dim = inner // head_count
    states = bc_weight.shape[1] // 2
    taps = x_conv.shape[0]
    heads = 4
    width = heads * head_dim
    blocks = inner // width
    chunks = rows // SPAN
    per_seq = LEN // SPAN
    inner_total = inner * n_tensor
    lanes = 128

    def tripled(v):
        one = jnp.pad(v, ((0, 0), (0, GROUP - head_count)))
        return jnp.pad(jnp.concatenate((one, one, one), axis=1), ((0, 0), (0, lanes - 3 * GROUP)))

    dt_w = tripled(dt_weight)
    dt_b = tripled(dt_bias[None])
    a_l = tripled(a_log[None])
    skip = jnp.repeat(d_skip, head_dim)[None]
    gain_in = norm_gain[None]
    gain_gated = gated_gain[None]
    x_bias = x_conv_bias[None]
    bc_bias = bc_conv_bias[None]

    def whole(array):
        return (array, array.shape, lambda j: (0,) * array.ndim)

    def columns(array):
        return (array, (array.shape[0], width), lambda j: (0, j))

    shared = Named(
        norm_gain=whole(gain_in),
        x_w=columns(x_weight),
        z_w=columns(z_weight),
        bc_w=whole(bc_weight),
        dt_w=whole(dt_w),
        x_conv=columns(x_conv),
        x_conv_bias=columns(x_bias),
        bc_conv=whole(bc_conv),
        bc_conv_bias=whole(bc_bias),
        dt_bias=whole(dt_b),
        a_log=whole(a_l),
        d_skip=columns(skip),
        gated_gain=columns(gain_gated),
    )

    kept = Named()
    shares = []
    states_at = []
    x_halo = bc_halo = None
    for i in range(chunks):
        first = i % per_seq == 0

        def at_rows(j, i=i):
            return (i, 0)

        def at_block(j, i=i):
            return (i, j)

        operands = Named(shared)
        operands.xin = (block_input, (SPAN, model), at_rows)
        operands.cot = (out_cotangent, (SPAN, model), at_rows)
        operands.out_w = (out_weight, (width, model), lambda j: (j, 0))
        if not first:
            operands.x_halo = columns(x_halo)
            operands.bc_halo = whole(bc_halo)
            operands.state = columns(states_at[-1])
        outs = Named(
            u_out=(shape(SPAN, model), (SPAN, model), lambda j: (0, 0)),
            state_out=(shape(states, inner), (states, width), lambda j: (0, j)),
            x_halo_out=(shape(HALO, inner), (HALO, width), lambda j: (0, j)),
            bc_halo_out=(shape(HALO, 2 * states), (HALO, 2 * states), lambda j: (0, 0)),
            sums=(shape(HALO, rows), (HALO, SPAN), lambda j, i=i: (0, i)),
            normed=(shape(rows, model, kind=BF16), (SPAN, model), at_rows),
            bc_pre=(shape(rows, 2 * states), (SPAN, 2 * states), at_rows),
            dt_pre=(shape(rows, lanes), (SPAN, lanes), at_rows),
            x_pre=(shape(rows, inner), (SPAN, width), at_block),
            z_pre=(shape(rows, inner), (SPAN, width), at_block),
            mg=(shape(rows, inner), (SPAN, width), at_block),
            y=(shape(rows, inner), (SPAN, width), at_block),
            gb=(shape(rows, inner, kind=BF16), (SPAN, width), at_block),
        )
        scratch = Named(
            bc_buf=((SPAN + HALO, 2 * states), F32),
            x_buf=((SPAN + HALO, width), F32),
            cb=((SPAN, 2 * states), BF16),
            bt=((2 * states, SPAN), BF16),
            scores=((SPAN, SPAN), F32),
            cum_t=((lanes, SPAN), F32),
            parts=((2 * SPAN, lanes), BF16),
            acc=((2 * SPAN, width), F32),
        )
        given = run_kernel(
            functools.partial(fwd_kernel, first, heads, head_dim),
            blocks,
            operands,
            outs,
            scratch,
            kept,
            flops=2 * SPAN * model * inner * 5,
            moved=2 * 3 * model * inner + 24 * SPAN * inner,
        )
        shares.append(given.pop("u_out"))
        states_at.append(given.pop("state_out"))
        x_halo = given.pop("x_halo_out")
        bc_halo = given.pop("bc_halo_out")
        kept = given

    sums = kept.sums
    sums_other = swap_tensor(sums, n_tensor)
    shares_other = [swap_tensor(u, n_tensor) for u in shares]

    square_sum = sums[0] + sums_other[0]
    gate_rms = lax.rsqrt(square_sum / inner_total + EPS)

    cot_scaled = (out_cotangent.astype(F32) * gate_rms[:, None]).astype(BF16)
    out_part = scattered_product(by_stage(cot_scaled.T, n_dp), kept.gb, n_dp)

    lows = Named()
    carry = Named()
    in_parts = [None] * chunks
    for i in reversed(range(chunks)):
        first = i % per_seq == 0
        last_chunk = i % per_seq == per_seq - 1
        start = i == chunks - 1

        def at_rows(j, i=i):
            return (i, 0)

        def at_block(j, i=i):
            return (i, j)

        operands = Named(shared)
        operands.xin = (block_input, (SPAN, model), at_rows)
        for name in ("bc_pre", "dt_pre"):
            operands[name] = (kept[name], (SPAN, kept[name].shape[1]), at_rows)
        for name in ("x_pre", "z_pre", "mg", "y"):
            operands[name] = (kept[name], (SPAN, width), at_block)
        operands.sums = (sums, (HALO, SPAN), lambda j, i=i: (0, i))
        operands.sums_other = (sums_other, (HALO, SPAN), lambda j, i=i: (0, i))
        before = i * (SPAN // HALO) - 1
        if not first:
            operands.x_halo = (kept.x_pre, (HALO, width), lambda j, b=before: (b, j))
            operands.bc_halo = (kept.bc_pre, (HALO, 2 * states), lambda j, b=before: (b, 0))
            operands.state = columns(states_at[i - 1])
        if not last_chunk:
            operands.d_state = columns(carry.d_state_out)
            operands.du_halo = columns(carry.du_halo_out)
            operands.du_bc_halo = whole(carry.du_bc_halo_out)
            operands.x_sums_in = columns(carry.x_sums)
            for name in ("head_sums", "bc_sums", "gain_sums"):
                operands[name + "_in"] = whole(carry[name])
        outs = Named(
            in_part=(shape(SPAN, model), (SPAN, model), lambda j: (0, 0)),
            du_halo_out=(shape(HALO, inner), (HALO, width), lambda j: (0, j)),
            du_bc_halo_out=(shape(HALO, 2 * states), (HALO, 2 * states), lambda j: (0, 0)),
            x_sums=(shape(HALO, inner), (HALO, width), lambda j: (0, j)),
            head_sums=(shape(HALO, lanes), (HALO, lanes), lambda j: (0, 0)),
            bc_sums=(shape(HALO, 2 * states), (HALO, 2 * states), lambda j: (0, 0)),
            gain_sums=(shape(HALO, model), (HALO, model), lambda j: (0, 0)),
            z_low=(shape(rows, inner, kind=BF16), (SPAN, width), at_block),
            x_low=(shape(rows, inner, kind=BF16), (SPAN, width), at_block),
            bc_low=(shape(rows, 2 * states, kind=BF16), (SPAN, 2 * states), at_rows),
            dt_low=(shape(rows, lanes, kind=BF16), (SPAN, lanes), at_rows),
        )
        if not first:
            outs.d_state_out = (shape(states, inner), (states, width), lambda j: (0, j))
        scratch = Named(
            bc_buf=((SPAN + HALO, 2 * states), F32),
            x_buf=((SPAN + HALO, width), F32),
            bc_grad_buf=((SPAN + HALO, 2 * states), F32),
            x_grad_buf=((SPAN + HALO, width), F32),
            bc_slope=((SPAN, 2 * states), F32),
            bb=((SPAN, 2 * states), BF16),
            cb=((SPAN, 2 * states), BF16),
            ct=((2 * states, SPAN), BF16),
            scores=((SPAN, SPAN), F32),
            d_scores=((SPAN, SPAN), F32),
            dt=((SPAN, lanes), F32),
            cum_t=((lanes, SPAN), F32),
            parts=((2 * SPAN, lanes), BF16),
            db=((SPAN, states), F32),
            dc=((SPAN, states), F32),
            d_cum=((SPAN, lanes), F32),
            d_dt=((SPAN, lanes), F32),
            ng=((SPAN, model), F32),
            rows=((SPAN, lanes), F32),
        )
        given = run_kernel(
            functools.partial(bwd_kernel, first, last_chunk, heads, head_dim, inner_total),
            blocks,
            operands,
            outs,
            scratch,
            lows,
            flops=2 * SPAN * model * inner * 6,
            moved=2 * 2 * model * inner + 24 * SPAN * inner,
        )
        lows = Named(
            z_low=given.z_low, x_low=given.x_low, bc_low=given.bc_low, dt_low=given.dt_low
        )
        in_parts[i] = given.in_part
        if last_chunk and not start:
            for name in ("x_sums", "head_sums", "bc_sums", "gain_sums"):
                given[name] = given[name] + carry[name]
        carry = given

    shared_sums = jnp.concatenate(
        (carry.gain_sums[0], carry.bc_sums[: taps + 1].reshape(-1))
    )
    shared_sums = shared_sums + swap_tensor(shared_sums, n_tensor)
    in_other = [None] * chunks
    for i in reversed(range(chunks)):
        in_other[i] = swap_tensor(in_parts[i], n_tensor)

    by_head = carry.head_sums[:2, :head_count].reshape(-1)
    small = jnp.concatenate((carry.x_sums[: taps + 3].reshape(-1), by_head, shared_sums))
    length = small.shape[0]
    padded = -(-length // 1024) * 1024
    small = doubling_sum(jnp.pad(small, (0, padded - length)).reshape(8, -1), n_dp).reshape(-1)
    x_end = (taps + 3) * inner
    x_sums = small[:x_end].reshape(taps + 3, inner)
    gated_gain_grad = x_sums[0]
    d_skip_grad = x_sums[1].reshape(head_count, head_dim).sum(axis=1)
    x_conv_grad = x_sums[2 : taps + 2]
    x_conv_bias_grad = x_sums[taps + 2]
    dt_bias_grad = small[x_end : x_end + head_count]
    a_log_grad = small[x_end + head_count : x_end + 2 * head_count]
    gain_at = x_end + 2 * head_count
    bc_at = gain_at + model
    gain_total = small[gain_at:bc_at]
    bc_total = small[bc_at : bc_at + (taps + 1) * 2 * states].reshape(taps + 1, 2 * states)
    place = lax.axis_index("dp") * n_tensor + lax.axis_index("tensor")
    places = n_dp * n_tensor

    def own(values, axis):
        size = values.shape[axis] // places
        return lax.dynamic_slice_in_dim(values, place * size, size, axis)

    norm_gain_grad = own(gain_total, 0)
    bc_conv_grad = own(bc_total[:taps], 1)
    bc_conv_bias_grad = own(bc_total[taps], 0)

    normed_rows = by_stage(kept.normed.T, n_dp)
    z_side = jnp.concatenate((lows.z_low, lows.bc_low, lows.dt_low), axis=1)
    z_part = scattered_product(normed_rows, z_side, n_dp)
    x_weight_grad = scattered_product(normed_rows, lows.x_low, n_dp)
    z_weight_grad = z_part[:, :inner]
    bc_part = z_part[:, inner : inner + 2 * states]
    dt_weight_grad = z_part[:, inner + 2 * states : inner + 2 * states + head_count]
    bc_part = bc_part.reshape(n_tensor, -1, 2 * states)
    mine = lax.axis_index("tensor")
    bc_weight_grad = lax.dynamic_index_in_dim(bc_part, mine, 0, keepdims=False) + swap_tensor(
        lax.dynamic_index_in_dim(bc_part, 1 - mine, 0, keepdims=False), n_tensor
    )
    out_weight_grad = out_part.T

    block_output = jnp.zeros((rows, model), BF16)
    for i in range(chunks):
        at = slice(i * SPAN, (i + 1) * SPAN)
        total = (shares[i] + shares_other[i]) * gate_rms[at, None]
        block_output = block_output.at[at].set((block_input[at].astype(F32) + total).astype(BF16))
    input_grad = jnp.zeros((rows, model), BF16)
    for i in reversed(range(chunks)):
        at = slice(i * SPAN, (i + 1) * SPAN)
        total = out_cotangent[at].astype(F32) + (in_parts[i] + in_other[i])
        input_grad = input_grad.at[at].set(total.astype(BF16))
    return (
        block_output,
        input_grad,
        norm_gain_grad,
        z_weight_grad,
        x_weight_grad,
        bc_weight_grad,
        dt_weight_grad,
        x_conv_grad,
        x_conv_bias_grad,
        bc_conv_grad,
        bc_conv_bias_grad,
        dt_bias_grad,
        a_log_grad,
        d_skip_grad,
        gated_gain_grad,
        out_weight_grad,
    )


def solution(mesh):
    in_specs = (
        P("dp", None),
        P(),
        P(None, "tensor"),
        P(None, "tensor"),
        P(),
        P(None, "tensor"),
        P(None, "tensor"),
        P("tensor"),
        P(),
        P(),
        P("tensor"),
        P("tensor"),
        P("tensor"),
        P("tensor"),
        P("tensor", None),
        P("dp", None),
    )
    out_specs = (
        P("dp", None),
        P("dp", None),
        P(("dp", "tensor")),
        P("dp", "tensor"),
        P("dp", "tensor"),
        P(("dp", "tensor"), None),
        P("dp", "tensor"),
        P(None, "tensor"),
        P("tensor"),
        P(None, ("dp", "tensor")),
        P(("dp", "tensor")),
        P("tensor"),
        P("tensor"),
        P("tensor"),
        P("tensor"),
        P("tensor", "dp"),
    )
    return jax.shard_map(body, mesh=mesh, in_specs=in_specs, out_specs=out_specs, check_vma=False)
```

```python
import functools
import math

import jax
import jax.numpy as jnp
from jax import lax
from jax.experimental import pallas as pl
from jax.experimental.pallas import tpu as pltpu
from jax.sharding import PartitionSpec as P

SPAN = 256
LEN = 1024
EPS = 1e-05
HIGH = lax.Precision.HIGHEST
LOG2E = math.log2(math.e)
F32 = jnp.float32
BF16 = jnp.bfloat16
HALO = 8
GROUP = 32
VMEM = 56 * 1024 * 1024


class Named(dict):
    __getattr__ = dict.get
    __setattr__ = dict.__setitem__


def mm(a, b):
    return lax.dot_general(a, b, (((1,), (0,)), ((), ())), preferred_element_type=F32)


def mm_nt(a, b):
    return lax.dot_general(a, b, (((1,), (1,)), ((), ())), preferred_element_type=F32)


def mm_tn(a, b):
    return lax.dot_general(a, b, (((0,), (0,)), ((), ())), preferred_element_type=F32)


def split3(x):
    hi = x.astype(BF16)
    rest = x - hi.astype(F32)
    mid = rest.astype(BF16)
    low = (rest - mid.astype(F32)).astype(BF16)
    return hi, mid, low


def split2(x):
    hi = x.astype(BF16)
    return hi, (x - hi.astype(F32)).astype(BF16)


def side(a, b):
    return jnp.concatenate((a, b), axis=1)


def folded(x):
    half = x.shape[1] // 2
    return x[:, :half] + x[:, half:]


def fine_nn(left_pair, b):
    bh, bl = split2(b)
    depth = b.shape[0]
    return mm(left_pair, jnp.concatenate((bh, bh), axis=0)) + mm(left_pair[:, :depth], bl)


def fine_rows(left_stack, b):
    bh, bl = split2(b)
    rows = left_stack.shape[0] // 2
    both = mm(left_stack, bh)
    return both[:rows] + both[rows:] + mm(left_stack[:rows], bl)


def fine_nt(a, b):
    ah, al = split2(a)
    bh, bl = split2(b)
    return folded(mm_nt(ah, jnp.concatenate((bh, bl), axis=0))) + mm_nt(al, bh)


def iota(shape, axis):
    return lax.broadcasted_iota(jnp.int32, shape, axis)


def times_transposed(left, right):
    return lax.dot_general(left, right, (((1,), (1,)), ((), ())), preferred_element_type=F32)


def softplus(v):
    return jnp.maximum(v, 0.0) + jnp.log1p(jnp.exp(-jnp.abs(v)))


def three_parts(x):
    hi, mid, low = split3(x)
    lane = iota(x.shape, 1)
    parts = jnp.where(
        lane < GROUP, hi.astype(F32), jnp.where(lane < 2 * GROUP, mid.astype(F32), low.astype(F32))
    )
    return parts.astype(BF16)


def spread_matrix(block, heads, head_dim, lanes):
    shape = (lanes, heads * head_dim)
    row, col = iota(shape, 0), iota(shape, 1)
    head = block * heads + col // head_dim
    hit = (row == head) | (row == head + GROUP) | (row == head + 2 * GROUP)
    return jnp.where(hit, 1.0, 0.0).astype(BF16)


def gather_matrix(block, heads, head_dim, lanes):
    shape = (heads * head_dim, lanes)
    row, col = iota(shape, 0), iota(shape, 1)
    return jnp.where(col == block * heads + row // head_dim, 1.0, 0.0).astype(BF16)


def triangle(n, lower):
    row, col = iota((n, n), 0), iota((n, n), 1)
    return jnp.where(row >= col if lower else row <= col, 1.0, 0.0)


def pair_masks(head_dim):
    lane = iota((1, 4 * head_dim), 1) // head_dim % 2
    return [jnp.where(lane == k, 1.0, 0.0).astype(BF16) for k in range(2)]


def pair_parts(parts, head_dim, pair):
    at = slice(2 * pair * head_dim, 2 * (pair + 1) * head_dim)
    return side(parts[0][:, at], parts[1][:, at])


def earlier(x, halo, by):
    if by == 0:
        return x
    rolled = pltpu.roll(x, by, 0)
    head = iota((HALO, x.shape[1]), 0) < by
    front = pltpu.roll(halo, by, 0) if halo is not None else 0.0
    return jnp.concatenate((jnp.where(head, front, rolled[:HALO]), rolled[HALO:]), axis=0)


def later(x, halo, by):
    if by == 0:
        return x
    rows = x.shape[0]
    rolled = pltpu.roll(x, rows - by, 0)
    tail = iota((HALO, x.shape[1]), 0) >= HALO - by
    back = pltpu.roll(halo, HALO - by, 0) if halo is not None else 0.0
    end = jnp.where(tail, back, rolled[rows - HALO :])
    return jnp.concatenate((rolled[: rows - HALO], end), axis=0)


def conv_of(x, halo, taps, bias):
    count = taps.shape[0]
    shifted = [earlier(x, halo, count - 1 - k) for k in range(count)]
    total = bias + taps[0:1] * shifted[0]
    for k in range(1, count):
        total = total + taps[k : k + 1] * shifted[k]
    return total, shifted


def conv_back(grad, halo, taps):
    count = taps.shape[0]
    total = taps[count - 1 : count] * grad
    for k in range(count - 1):
        total = total + taps[k : k + 1] * later(grad, halo, count - 1 - k)
    return total


def unpacked(ref, taps):
    return ref[:taps], ref[taps : taps + 1], ref[taps + 1 : taps + 2], ref[taps + 2 : taps + 3]


def maybe(ref):
    return None if ref is None else ref[...]


def silu_slope(v, s):
    return s + v * s * (1.0 - s)


def triangle_sum(x, lower):
    lanes = x.shape[1]
    parts = mm(triangle(x.shape[0], lower).astype(BF16), jnp.concatenate(split3(x), axis=1))
    return parts[:, :lanes] + parts[:, lanes : 2 * lanes] + parts[:, 2 * lanes :]


def steps_of(dt_pre, dt_bias_ref, a_log_ref):
    dt = softplus(dt_pre + dt_bias_ref[...])
    decay = -jnp.exp(a_log_ref[...])
    rates = dt * (decay * LOG2E)
    cum = triangle_sum(rates, True)
    return dt, decay, cum


def row_sums(x):
    lanes = 128
    part = x[:, :lanes]
    for at in range(lanes, x.shape[1], lanes):
        part = part + x[:, at : at + lanes]
    return jnp.sum(part.T, axis=0, keepdims=True)


PIECE = 32


def slot_of(rel, n):
    bits = n.bit_length() - 1
    p = sum((rel >> b & 1) << (bits - 1 - b) for b in range(1, bits))
    first, half, quarter = rel & 1, n // 2, n // 4
    return jnp.where(first == 1, p, jnp.where(p >= quarter, half + p - quarter, n - quarter + p))


def arrange_rows(start, n, place, turned, target):
    block = target.shape[0] // n
    if n == 1 or block % PIECE:
        target[pl.ds(pl.multiple_of(start, PIECE), turned.shape[0]), :] = turned
        return
    for at in range(0, turned.shape[0], PIECE):
        begin = start + at
        owner = lax.div(begin, block)
        slot = slot_of(owner ^ place[0], n)
        to = pl.multiple_of(slot * block + begin - owner * block, PIECE)
        target[pl.ds(to, PIECE), :] = turned[at : at + PIECE]


def fwd_kernel(first, heads, head_dim, blocks, n_dp, refs):
    j = pl.program_id(0)
    r = refs
    rows = r.xin.shape[0]
    half = rows // 2
    states = r.bc_w.shape[1] // 2
    lanes = r.dt_w.shape[1]

    @pl.when(j == 0)
    def _():
        res = r.xin[...].astype(F32)
        inv = lax.rsqrt(jnp.mean(res * res, axis=1, keepdims=True) + EPS)
        normed = (res * inv * r.norm_gain[...]).astype(BF16)
        r.normed[...] = normed
        bc_pre = mm(normed, r.bc_w[...])
        r.bc_pre[...] = bc_pre
        r.bc_halo_out[...] = bc_pre[rows - HALO :, :]
        u, _ = conv_of(bc_pre, maybe(r.bc_halo), r.bc_conv[...], r.bc_conv_bias[...])
        act = u * jax.nn.sigmoid(u)
        b, c = act[:, :states], act[:, states:]
        r.cb[...] = side(*split2(c))
        r.bt[...] = jnp.concatenate(split2(b.T), axis=0)
        r.scores[...] = fine_nt(c, b) * triangle(rows, True)
        dt_pre = mm(normed, r.dt_w[...])
        r.dt_pre[...] = dt_pre
        dt, decay, cum = steps_of(dt_pre, r.dt_bias, r.a_log)
        r.cum_t[...] = cum.T
        r.parts[0:rows, :] = three_parts(cum)
        r.parts[rows : 2 * rows, :] = three_parts(dt)
        r.u_out[...] = jnp.zeros_like(r.u_out)
        r.acc[...] = jnp.zeros_like(r.acc)
        r.x_next[...] = mm(normed, r.x_w_first[...])
        r.z_next[...] = mm(normed, r.z_w_first[...])

    width = heads * head_dim
    xp, zp = r.x_next[...], r.z_next[...]
    gate = zp * jax.nn.sigmoid(zp)
    r.x_pre[...] = xp
    r.z_pre[...] = zp
    r.x_halo_out[...] = xp[rows - HALO :, :]
    columns = r.xin.shape[1] // blocks
    here = pl.ds(pl.multiple_of(j * columns, columns), columns)
    turned = r.normed[:, here].T
    arrange_rows(j * columns, n_dp, r.place, turned, r.normed_t)
    r.cot_t[here, :] = r.cot[:, here].T
    taps = r.bc_conv.shape[0]
    conv, conv_bias, d_skip, gated_gain = unpacked(r.packed, taps)
    u, _ = conv_of(xp, maybe(r.x_halo), conv, conv_bias)
    xa = u * jax.nn.sigmoid(u)
    spread = mm(r.parts[...], spread_matrix(j, heads, head_dim, lanes))
    cum_e, dt_e = spread[:rows], spread[rows:]
    w = xa * dt_e
    last = cum_e[rows - 1 : rows, :]
    scaled = w * jnp.exp2(last - cum_e)
    masks = pair_masks(head_dim)
    parts = split2(w)
    empty = jnp.zeros((half, half), BF16)
    cols = []
    for pair in range(heads // 2):
        both = pair_parts(parts, head_dim, pair)
        total = 0.0
        for k in range(2):
            head = 2 * pair + k
            row = r.cum_t[pl.ds(j * heads + head, 1), :]
            col = cum_e[:, head * head_dim : head * head_dim + 1]
            m = jnp.exp2(jnp.minimum(col[:half] - row[:, :half], 0.0)) * r.scores[:half, :half]
            top = [side(part, empty) for part in split2(m)]
            m = jnp.exp2(jnp.minimum(col[half:] - row, 0.0)) * r.scores[half:, :]
            bot = split2(m)
            stack = jnp.concatenate((top[0], bot[0], top[1], bot[1]), axis=0)
            total = total + mm(stack, both * masks[k])
        cols.append(folded(total[:rows] + total[rows:]))
    y = side(*cols)
    if first:
        r.state_out[...] = fine_rows(r.bt[...], scaled)
    else:
        state = r.state[...]
        y = y + jnp.exp2(cum_e) * fine_nn(r.cb[...], state)
        r.state_out[...] = jnp.exp2(last) * state + fine_rows(r.bt[...], scaled)
    mixed = y + d_skip * xa
    r.mixed[...] = mixed
    gated = mixed * gate
    gain = gated * gated_gain
    r.u_out[...] += mm(gain.astype(BF16), r.out_w[...])
    r.acc[...] += gated * gated
    r.x_next[...] = mm(r.normed[...], r.x_w[...])
    r.z_next[...] = mm(r.normed[...], r.z_w[...])

    @pl.when(j == pl.num_programs(0) - 1)
    def _():
        r.sums[0:1, :] = row_sums(r.acc[...])
        r.sums[1:2, :] = row_sums(r.cot[...].astype(F32) * r.u_out[...])
        r.sums[2:HALO, :] = jnp.zeros((HALO - 2, rows), F32)


def row_scales(r, inner_total):
    sums = (r.sums[...] + r.sums_other[...]).T
    rms = lax.rsqrt(sums[:, 0:1] / inner_total + EPS)
    return rms, sums[:, 1:2] * rms / inner_total


def gate_kernel(inner_total, taps, width, r):
    rms, row_dot = row_scales(r, inner_total)
    for start in range(0, r.z_pre.shape[1], width):
        at = slice(start, start + width)
        mg = mm_nt(r.cot[...], r.out_w[at, :])
        r.mg[:, at] = mg
        zp, mixed = r.z_pre[:, at], r.mixed[:, at]
        gain = r.packed[taps + 2 : taps + 3, at]
        sz = jax.nn.sigmoid(zp)
        gated_unit = mixed * (zp * sz) * rms
        r.mixer_out[:, at] = (gated_unit * gain).astype(BF16)
        gg = rms * (mg * gain - gated_unit * row_dot)
        r.z_low[:, at] = (gg * mixed * silu_slope(zp, sz)).astype(BF16)


def output_kernel(inner_total, r):
    rms, _ = row_scales(r, inner_total)
    total = (r.share[...] + r.share_other[...]) * rms
    r.out[...] = (r.xin[...].astype(F32) + total).astype(BF16)


def grad_kernel(r):
    total = r.share[...] + r.share_other[...]
    r.out[...] = (r.cot[...].astype(F32) + total).astype(BF16)


def bwd_kernel(first, last_chunk, heads, head_dim, inner_total, refs):
    j = pl.program_id(0)
    r = refs
    rows = r.xin.shape[0]
    half = rows // 2
    states = r.bc_w.shape[1] // 2
    lanes = r.dt_w.shape[1]
    width = heads * head_dim
    taps = r.bc_conv.shape[0]
    conv, conv_bias, d_skip, gated_gain = unpacked(r.packed, taps)

    def column_sum(v):
        return jnp.sum(v, axis=0, keepdims=True)

    @pl.when(j == 0)
    def _():
        bc_pre = r.bc_pre[...]
        u, _ = conv_of(bc_pre, maybe(r.bc_halo), r.bc_conv[...], r.bc_conv_bias[...])
        s = jax.nn.sigmoid(u)
        act = u * s
        r.bc_slope[...] = silu_slope(u, s)
        b, c = act[:, :states], act[:, states:]
        r.bb[...] = side(*split2(b))
        r.cb[...] = side(*split2(c))
        r.ct[...] = jnp.concatenate(split2(c.T), axis=0)
        r.scores[...] = fine_nt(b, c) * triangle(rows, False)
        dt, decay, cum = steps_of(r.dt_pre[...], r.dt_bias, r.a_log)
        r.dt[...] = dt
        r.cum_t[...] = cum.T
        r.parts[0:rows, :] = three_parts(cum)
        r.parts[rows : 2 * rows, :] = three_parts(dt)
        r.x_low_before[...] = jnp.zeros_like(r.x_low_before)
        for ref in (r.d_scores, r.db, r.dc, r.d_cum, r.d_dt, r.ng):
            ref[...] = jnp.zeros_like(ref)
        rms, row_dot = row_scales(r, inner_total)
        r.rows[:, 0:1] = rms
        r.rows[:, 1:2] = row_dot

    xp = r.x_pre[...]
    u, shifted = conv_of(xp, maybe(r.x_halo), conv, conv_bias)
    su = jax.nn.sigmoid(u)
    xa = u * su
    spread = mm(r.parts[...], spread_matrix(j, heads, head_dim, lanes))
    cum_e, dt_e = spread[:rows], spread[rows:]
    w = xa * dt_e
    last = cum_e[rows - 1 : rows, :]
    rms, row_dot = r.rows[:, 0:1], r.rows[:, 1:2]
    zp, mg, mixed = r.z_pre[...], r.mg[...], r.mixed[...]
    sz = jax.nn.sigmoid(zp)
    gate = zp * sz
    y = mixed - d_skip * xa
    gated_unit = mixed * gate * rms
    gg = rms * (mg * gated_gain - gated_unit * row_dot)
    dy = gg * gate
    sums = [column_sum(mg * gated_unit), column_sum(dy * xa)]
    masks = pair_masks(head_dim)
    w_parts = split2(w)
    dy_parts = split2(dy)
    empty = jnp.zeros((half, half), BF16)
    cols = []
    for pair in range(heads // 2):
        at = slice(2 * pair * head_dim, 2 * (pair + 1) * head_dim)
        w_both = pair_parts(w_parts, head_dim, pair)
        w_high = w_parts[0][:, at]
        dy_both = pair_parts(dy_parts, head_dim, pair)
        dy_high = side(dy_parts[0][:, at], dy_parts[0][:, at])
        dy_low = dy_parts[1][:, at]
        total = 0.0
        for k in range(2):
            head = 2 * pair + k
            row = r.cum_t[pl.ds(j * heads + head, 1), :]
            col = cum_e[:, head * head_dim : head * head_dim + 1]
            dk, dk_high = dy_both * masks[k], dy_high * masks[k]
            dk_low = dy_low * masks[k][:, : 2 * head_dim]
            grad = mm_nt(w_both, dk_high) + mm_nt(w_high, dk_low)
            decay = jnp.exp2(jnp.minimum(row - col[:half], 0.0))
            r.d_scores[:half, :] += grad[:half] * decay
            top = split2(decay * r.scores[:half, :])
            decay = jnp.exp2(jnp.minimum(row[:, half:] - col[half:], 0.0))
            r.d_scores[half:, half:] += grad[half:, half:] * decay
            bot = [side(empty, part) for part in split2(decay * r.scores[half:, half:])]
            stack = jnp.concatenate((top[0], bot[0], top[1], bot[1]), axis=0)
            total = total + mm(stack, dk)
        cols.append(folded(total[:rows] + total[rows:]))
    dw = side(*cols)
    extra = None
    if not last_chunk:
        to_end = jnp.exp2(last - cum_e)
        d_state = r.d_state[...]
        ds = fine_nn(r.bb[...], d_state) * to_end
        r.db[...] += fine_nt(w * to_end, d_state)
        dw = dw + ds
        extra = column_sum(w * ds)
    if not first:
        state = r.state[...]
        g = jnp.exp2(cum_e) * dy
        r.dc[...] += fine_nt(g, state)
        d_state_out = fine_rows(r.ct[...], g)
        if not last_chunk:
            kept = jnp.exp2(last) * d_state
            extra = extra + column_sum(kept * state)
            d_state_out = d_state_out + kept
        r.d_state_out[...] = d_state_out
    q = dy * y - w * dw
    if extra is not None:
        q = q + jnp.where(iota((rows, 1), 0) == rows - 1, 1.0, 0.0) * extra
    gather = gather_matrix(j, heads, head_dim, lanes)
    stack = split3(q) + split2(dw * xa)
    given = mm(jnp.concatenate(stack, axis=0), gather)
    given = [given[at * rows : (at + 1) * rows] for at in range(5)]
    r.d_cum[...] += given[0] + given[1] + given[2]
    r.d_dt[...] += given[3] + given[4]
    du = (d_skip * dy + dw * dt_e) * silu_slope(u, su)
    xg = conv_back(du, maybe(r.du_halo), conv)
    r.du_halo_out[...] = du[:HALO, :]
    for k in range(taps):
        sums.append(column_sum(du * shifted[k]))
    sums.append(column_sum(du))
    for at, value in enumerate(sums):
        before = 0.0 if last_chunk else r.x_sums_in[at : at + 1, :]
        r.x_sums[at : at + 1, :] = value + before
    r.x_sums[len(sums) : HALO, :] = jnp.zeros((HALO - len(sums), width), F32)
    xl = xg.astype(BF16)
    r.x_low[...] = xl
    r.ng[...] += mm_nt(r.z_low[...], r.z_w[...]) + mm_nt(r.x_low_before[...], r.x_w[...])
    r.x_low_before[...] = xl

    @pl.when(j == pl.num_programs(0) - 1)
    def _():
        hi, low = split2(r.d_scores[...] * triangle(rows, False))
        cb, bb = r.cb[...], r.bb[...]
        db = r.db[...] + folded(mm(hi, cb)) + mm(low, cb[:, :states])
        dc = r.dc[...] + folded(mm_tn(hi, bb)) + mm_tn(low, bb[:, :states])
        d_rates = triangle_sum(r.d_cum[...], False)
        dt = r.dt[...]
        decay = -jnp.exp(r.a_log[...])
        d_dt = d_rates * decay + r.d_dt[...]
        dtg = d_dt * jax.nn.sigmoid(r.dt_pre[...] + r.dt_bias[...])
        dtl = jnp.where(iota(dtg.shape, 1) < GROUP, dtg, 0.0).astype(BF16)
        r.side_low[:, 2 * states :] = dtl
        head_sums = [column_sum(dtg), column_sum(d_rates * dt) * decay]
        for at, value in enumerate(head_sums):
            before = 0.0 if last_chunk else r.head_sums_in[at : at + 1, :]
            r.head_sums[at : at + 1, :] = value + before
        r.head_sums[2:HALO, :] = jnp.zeros((HALO - 2, lanes), F32)
        du_bc = jnp.concatenate((db, dc), axis=1) * r.bc_slope[...]
        bg = conv_back(du_bc, maybe(r.du_bc_halo), r.bc_conv[...])
        r.du_bc_halo_out[...] = du_bc[:HALO, :]
        bc_sums = []
        for k in range(taps):
            near = earlier(r.bc_pre[...], maybe(r.bc_halo), taps - 1 - k)
            bc_sums.append(column_sum(du_bc * near))
        bc_sums.append(column_sum(du_bc))
        for at, value in enumerate(bc_sums):
            before = 0.0 if last_chunk else r.bc_sums_in[at : at + 1, :]
            r.bc_sums[at : at + 1, :] = value + before
        r.bc_sums[len(bc_sums) : HALO, :] = jnp.zeros((HALO - len(bc_sums), 2 * states), F32)
        bl = bg.astype(BF16)
        r.side_low[:, : 2 * states] = bl
        ng = r.ng[...] + mm_nt(bl, r.bc_w[...]) + mm_nt(dtl, r.dt_w[...])
        ng = ng + mm_nt(xl, r.x_w_last[...])
        res = r.xin[...].astype(F32)
        inv = lax.rsqrt(jnp.mean(res * res, axis=1, keepdims=True) + EPS)
        unit = res * inv
        gain_sum = column_sum(ng * unit)
        r.gain_sums[0:1, :] = gain_sum if last_chunk else gain_sum + r.gain_sums_in[0:1, :]
        r.gain_sums[1:HALO, :] = jnp.zeros((HALO - 1, gain_sum.shape[1]), F32)
        iu = ng * r.norm_gain[...]
        r.in_part[...] = inv * (iu - unit * jnp.mean(iu * unit, axis=1, keepdims=True))


def run_kernel(body, grid, operands, outs, scratch, carried, waits=(), flops=1):
    names, arrays, specs = [], [], []
    for name, (array, block, index) in operands.items():
        names.append(name)
        arrays.append(array)
        whole = pl.BlockSpec(memory_space=pltpu.SMEM)
        specs.append(whole if block is None else pl.BlockSpec(block, index))
    aliases = {}
    out_names = list(outs)
    for at, name in enumerate(out_names):
        if name in carried:
            aliases[len(arrays)] = at
            names.append(name + "_old")
            arrays.append(carried[name])
            specs.append(pl.BlockSpec(memory_space=pl.ANY))
    for at, array in enumerate(waits):
        names.append(at)
        arrays.append(array)
        specs.append(pl.BlockSpec(memory_space=pl.ANY))
    scratch_names = list(scratch)

    def kernel(*refs):
        body(Named(zip(names + out_names + scratch_names, refs)))

    given = pl.pallas_call(
        kernel,
        grid=grid,
        in_specs=specs,
        out_specs=[pl.BlockSpec(block, index) for _, block, index in outs.values()],
        out_shape=[shape for shape, _, _ in outs.values()],
        scratch_shapes=[pltpu.VMEM(shape, kind) for shape, kind in scratch.values()],
        input_output_aliases=aliases,
        compiler_params=pltpu.CompilerParams(
            dimension_semantics=("arbitrary",) * len(grid), vmem_limit_bytes=VMEM
        ),
        cost_estimate=pl.CostEstimate(flops=flops, bytes_accessed=1, transcendentals=0),
    )(*arrays)
    return Named(zip(out_names, given))


def shape(*dims, kind=F32):
    return jax.ShapeDtypeStruct(dims, kind)


def relative_masks(n, flip):
    bits = n.bit_length() - 1
    masks = []
    for p in range(n // 2):
        masks.append(flip + sum((p >> (bits - 1 - b) & 1) << b for b in range(1, bits)))
    return masks


def arranged(left, n):
    if n == 1:
        return None, left, left[:0]
    block = left.shape[0] // n
    me = lax.axis_index("dp")
    if block % PIECE == 0:
        half, quarter = left.shape[0] // 2, left.shape[0] // 4
        return left[:half], left[half : half + quarter], left[half + quarter :]

    def pick(masks):
        rows = [lax.dynamic_slice_in_dim(left, (me ^ mask) * block, block, 0) for mask in masks]
        return jnp.concatenate(rows, axis=0)

    kept = relative_masks(n, 0)
    half = len(kept) // 2
    if not half:
        return pick(relative_masks(n, 1)), pick(kept), left[:0]
    return pick(relative_masks(n, 1)), pick(kept[half:]), pick(kept[:half])


class ScatteredProduct:
    def __init__(self, left, right, n, extra=None):
        self.n, self.stride, self.left, self.right, self.extra = n, 1, left, right, extra
        if n == 1:
            self.total = mm(left[1], right)
        else:
            self.send = mm(left[0], right)

    def start(self, *others):
        pairs = [(p, p ^ self.stride) for p in range(self.n)]
        if self.stride == 1 and self.extra is not None:
            self.extra = self.extra + lax.ppermute(self.extra, "dp", pairs)
        self.came = lax.ppermute(after(self.send, *others), "dp", pairs)

    def settle(self, *others):
        came = after(self.came, *others)
        if self.stride == 1:
            rows = self.left[2].shape[0]
            keep = mm(self.left[2], self.right) + came[:rows]
            send = mm(self.left[1], self.right) + came[rows:]
        else:
            size = self.keep.shape[0]
            rows = size // 2 if 2 * self.stride < self.n else 0
            if self.extra is not None:
                self.extra = self.extra + came[size:]
            keep, send = self.keep[:rows] + came[:rows], self.keep[rows:] + came[rows:size]
        self.stride *= 2
        if self.stride == self.n:
            self.total = send
            return
        if self.extra is not None:
            send = jnp.concatenate((send, self.extra), axis=0)
        self.keep, self.send = keep, send

    def finish(self):
        while self.stride < self.n:
            self.start()
            self.settle()
        return self.total


def after(values, *others):
    return lax.optimization_barrier((values,) + others)[0]


def tied(array, *waits):
    def nothing(*refs):
        pass

    anywhere = pl.BlockSpec(memory_space=pl.ANY)
    out = pl.pallas_call(
        nothing,
        in_specs=[anywhere] * (1 + len(waits)),
        out_specs=anywhere,
        out_shape=jax.ShapeDtypeStruct(array.shape, array.dtype),
        input_output_aliases={0: 0},
        cost_estimate=pl.CostEstimate(flops=1, bytes_accessed=1, transcendentals=0),
    )(array, *waits)
    return out


def swap_tensor(values, n):
    return lax.ppermute(values, "tensor", [(t, t ^ 1) for t in range(n)])


def body(
    block_input,
    norm_gain,
    z_weight,
    x_weight,
    bc_weight,
    dt_weight,
    x_conv,
    x_conv_bias,
    bc_conv,
    bc_conv_bias,
    dt_bias,
    a_log,
    d_skip,
    gated_gain,
    out_weight,
    out_cotangent,
):
    n_dp, n_tensor = lax.axis_size("dp"), lax.axis_size("tensor")
    rows, model = block_input.shape
    inner = x_weight.shape[1]
    head_count = dt_weight.shape[1]
    head_dim = inner // head_count
    states = bc_weight.shape[1] // 2
    taps = x_conv.shape[0]
    heads = 4
    width = heads * head_dim
    blocks = inner // width
    chunks = rows // SPAN
    per_seq = LEN // SPAN
    inner_total = inner * n_tensor
    me = lax.axis_index("dp").astype(jnp.int32).reshape(1)
    lanes = 128
    side_width = 2 * states + lanes

    def tripled(v):
        one = jnp.pad(v, ((0, 0), (0, GROUP - head_count)))
        return jnp.pad(jnp.concatenate((one, one, one), axis=1), ((0, 0), (0, lanes - 3 * GROUP)))

    dt_w = tripled(dt_weight)
    dt_b = tripled(dt_bias[None])
    a_l = tripled(a_log[None])
    skip = jnp.repeat(d_skip, head_dim)[None]
    packed = jnp.concatenate((x_conv, x_conv_bias[None], skip, gated_gain[None]), axis=0)
    packed = jnp.pad(packed, ((0, HALO - packed.shape[0] % HALO), (0, 0)))
    gain_in = norm_gain[None]
    bc_bias = bc_conv_bias[None]

    def whole(array):
        return (array, array.shape, lambda j: (0,) * array.ndim)

    def columns(array):
        return (array, (array.shape[0], width), lambda j: (0, j))

    shared = Named(
        norm_gain=whole(gain_in),
        x_w=columns(x_weight),
        z_w=columns(z_weight),
        bc_w=whole(bc_weight),
        dt_w=whole(dt_w),
        packed=columns(packed),
        bc_conv=whole(bc_conv),
        bc_conv_bias=whole(bc_bias),
        dt_bias=whole(dt_b),
        a_log=whole(a_l),
    )

    kept = Named()
    shares = []
    shares_other = []
    states_at = []
    x_halo = bc_halo = None
    for i in range(chunks):
        first = i % per_seq == 0

        def at_rows(j, i=i):
            return (i, 0)

        def at_block(j, i=i):
            return (i, j)

        def at_turned(j, i=i):
            return (0, i)

        operands = Named(shared)
        operands.place = (me, None, None)
        operands.xin = (block_input, (SPAN, model), at_rows)
        operands.cot = (out_cotangent, (SPAN, model), at_rows)
        operands.out_w = (out_weight, (width, model), lambda j: (j, 0))
        following = ((model, width), lambda j: (0, jnp.minimum(j + 1, blocks - 1)))
        operands.x_w, operands.z_w = (x_weight,) + following, (z_weight,) + following
        beginning = ((model, width), lambda j: (0, 0))
        operands.x_w_first, operands.z_w_first = (x_weight,) + beginning, (z_weight,) + beginning
        if not first:
            operands.x_halo = columns(x_halo)
            operands.bc_halo = whole(bc_halo)
            operands.state = columns(states_at[-1])
        outs = Named(
            u_out=(shape(SPAN, model), (SPAN, model), lambda j: (0, 0)),
            state_out=(shape(states, inner), (states, width), lambda j: (0, j)),
            x_halo_out=(shape(HALO, inner), (HALO, width), lambda j: (0, j)),
            bc_halo_out=(shape(HALO, 2 * states), (HALO, 2 * states), lambda j: (0, 0)),
            sums=(shape(HALO, rows), (HALO, SPAN), lambda j, i=i: (0, i)),
            normed=(shape(rows, model, kind=BF16), (SPAN, model), at_rows),
            bc_pre=(shape(rows, 2 * states), (SPAN, 2 * states), at_rows),
            dt_pre=(shape(rows, lanes), (SPAN, lanes), at_rows),
            x_pre=(shape(rows, inner), (SPAN, width), at_block),
            z_pre=(shape(rows, inner), (SPAN, width), at_block),
            normed_t=(shape(model, rows, kind=BF16), (model, SPAN), at_turned),
            cot_t=(shape(model, rows, kind=BF16), (model, SPAN), at_turned),
            mixed=(shape(rows, inner), (SPAN, width), at_block),
        )
        waits = [shares_other[i - 3]] if i >= 3 else []
        scratch = Named(
            cb=((SPAN, 2 * states), BF16),
            bt=((2 * states, SPAN), BF16),
            scores=((SPAN, SPAN), F32),
            cum_t=((lanes, SPAN), F32),
            parts=((2 * SPAN, lanes), BF16),
            acc=((SPAN, width), F32),
            x_next=((SPAN, width), F32),
            z_next=((SPAN, width), F32),
        )
        given = run_kernel(
            functools.partial(fwd_kernel, first, heads, head_dim, blocks, n_dp),
            (blocks,),
            operands,
            outs,
            scratch,
            kept,
            waits,
        )
        shares.append(given.pop("u_out"))
        if i < chunks - 2:
            shares_other.append(swap_tensor(shares[-1], n_tensor))
        states_at.append(given.pop("state_out"))
        x_halo = given.pop("x_halo_out")
        bc_halo = given.pop("bc_halo_out")
        kept = given

    sums = kept.sums
    sums_other = swap_tensor(sums, n_tensor)

    def sums_at(rows_of, at=lambda i: i):
        block = (HALO, rows_of)
        return {
            "sums": (sums, block, lambda i: (0, at(i))),
            "sums_other": (sums_other, block, lambda i: (0, at(i))),
        }

    operands = Named(sums_at(SPAN))
    operands.packed = (packed, packed.shape, lambda i: (0, 0))
    for name, array in dict(z_pre=kept.z_pre, mixed=kept.mixed).items():
        operands[name] = (array, (SPAN, inner), lambda i: (i, 0))
    operands.cot = (out_cotangent, (SPAN, model), lambda i: (i, 0))
    operands.out_w = (out_weight, out_weight.shape, lambda i: (0, 0))
    outs = Named(
        mg=(shape(rows, inner), (SPAN, inner), lambda i: (i, 0)),
        mixer_out=(shape(rows, inner, kind=BF16), (SPAN, inner), lambda i: (i, 0)),
        z_low=(shape(rows, inner, kind=BF16), (SPAN, inner), lambda i: (i, 0)),
    )
    gates = run_kernel(
        functools.partial(gate_kernel, inner_total, taps, width),
        (chunks,),
        operands,
        outs,
        Named(),
        Named(),
        shares_other[: max(chunks - 2, 0)],
    )
    for i in range(len(shares_other), chunks):
        shares_other.append(swap_tensor(after(shares[i], sums_other), n_tensor))

    def finished(body, given, out, ours, theirs, i):
        operands = Named(given)
        for name, array in dict(share=ours[i], share_other=theirs[i]).items():
            operands[name] = (array, (part, model), lambda k: (k, 0))
        outs = Named(out=(shape(rows, model, kind=BF16), (part, model), lambda k: (i * 2 + k, 0)))
        carried = Named() if out is None else Named(out=out)
        return run_kernel(body, (SPAN // part,), operands, outs, Named(), carried).out

    def with_output(out, i):
        given = sums_at(part, lambda k, i=i: i * 2 + k)
        given["xin"] = (block_input, (part, model), lambda k, i=i: (i * 2 + k, 0))
        kernel = functools.partial(output_kernel, inner_total)
        return finished(kernel, given, out, shares, shares_other, i)

    part = SPAN // 2
    block_output = None
    for i in range(chunks - 2):
        block_output = with_output(block_output, i)

    out_product = mm(kept.cot_t, gates.mixer_out)
    z_low = gates.z_low
    kept.z_low, kept.mg = z_low, gates.mg
    normed_left = arranged(kept.normed_t, n_dp)
    z_sum = ScatteredProduct(normed_left, z_low, n_dp)
    if n_dp > 1:
        z_sum.start()
        z_sum.settle()
    y_waits = {0: [out_product], 2: shares_other[-2:-1], 3: shares_other[-1:]}
    if n_dp > 2:
        z_sum.start()
        y_waits[0] = [out_product, z_sum.send]


    lows = Named()
    carry = Named()
    in_parts = [None] * chunks
    in_other = [None] * chunks
    queue = [sums_other] + shares_other[-2:]
    for i in reversed(range(chunks)):
        first = i % per_seq == 0
        last_chunk = i % per_seq == per_seq - 1
        start = i == chunks - 1

        def at_rows(j, i=i):
            return (i, 0)

        def at_block(j, i=i):
            return (i, j)

        operands = Named(shared)
        operands.xin = (block_input, (SPAN, model), at_rows)
        for name in ("bc_pre", "dt_pre"):
            operands[name] = (kept[name], (SPAN, kept[name].shape[1]), at_rows)
        operands.x_w = (x_weight, (model, width), lambda j: (0, jnp.maximum(j - 1, 0)))
        operands.x_w_last = (x_weight, (model, width), lambda j: (0, blocks - 1))
        for name in ("x_pre", "z_pre", "mg", "mixed", "z_low"):
            operands[name] = (kept[name], (SPAN, width), at_block)
        operands.sums = (sums, (HALO, SPAN), lambda j, i=i: (0, i))
        operands.sums_other = (sums_other, (HALO, SPAN), lambda j, i=i: (0, i))
        before = i * (SPAN // HALO) - 1
        if not first:
            operands.x_halo = (kept.x_pre, (HALO, width), lambda j, b=before: (b, j))
            operands.bc_halo = (kept.bc_pre, (HALO, 2 * states), lambda j, b=before: (b, 0))
            operands.state = columns(states_at[i - 1])
        if not last_chunk:
            operands.d_state = columns(carry.d_state_out)
            operands.du_halo = columns(carry.du_halo_out)
            operands.du_bc_halo = whole(carry.du_bc_halo_out)
            operands.x_sums_in = columns(carry.x_sums)
            for name in ("head_sums", "bc_sums", "gain_sums"):
                operands[name + "_in"] = whole(carry[name])
        outs = Named(
            in_part=(shape(SPAN, model), (SPAN, model), lambda j: (0, 0)),
            du_halo_out=(shape(HALO, inner), (HALO, width), lambda j: (0, j)),
            du_bc_halo_out=(shape(HALO, 2 * states), (HALO, 2 * states), lambda j: (0, 0)),
            x_sums=(shape(HALO, inner), (HALO, width), lambda j: (0, j)),
            head_sums=(shape(HALO, lanes), (HALO, lanes), lambda j: (0, 0)),
            bc_sums=(shape(HALO, 2 * states), (HALO, 2 * states), lambda j: (0, 0)),
            gain_sums=(shape(HALO, model), (HALO, model), lambda j: (0, 0)),
            x_low=(shape(rows, inner, kind=BF16), (SPAN, width), at_block),
            side_low=(shape(rows, side_width, kind=BF16), (SPAN, side_width), at_rows),
        )
        waits = y_waits.get(chunks - 1 - i, [])
        if i == 0 and n_dp > 4:
            z_sum.settle(*([carry.head_sums] if carry else []))
            z_sum.start()
            waits = waits + [z_sum.send]
        if not first:
            outs.d_state_out = (shape(states, inner), (states, width), lambda j: (0, j))
        scratch = Named(
            bc_slope=((SPAN, 2 * states), F32),
            bb=((SPAN, 2 * states), BF16),
            cb=((SPAN, 2 * states), BF16),
            ct=((2 * states, SPAN), BF16),
            scores=((SPAN, SPAN), F32),
            d_scores=((SPAN, SPAN), F32),
            dt=((SPAN, lanes), F32),
            cum_t=((lanes, SPAN), F32),
            parts=((2 * SPAN, lanes), BF16),
            db=((SPAN, states), F32),
            dc=((SPAN, states), F32),
            d_cum=((SPAN, lanes), F32),
            d_dt=((SPAN, lanes), F32),
            ng=((SPAN, model), F32),
            x_low_before=((SPAN, width), BF16),
            rows=((SPAN, lanes), F32),
        )
        given = run_kernel(
            functools.partial(bwd_kernel, first, last_chunk, heads, head_dim, inner_total),
            (blocks,),
            operands,
            outs,
            scratch,
            lows,
            waits,
        )
        lows = Named(x_low=given.x_low, side_low=given.side_low)
        in_parts[i] = given.in_part
        queue.append(swap_tensor(in_parts[i], n_tensor))
        in_other[i] = queue[-1]
        if last_chunk and not start:
            for name in ("x_sums", "head_sums", "bc_sums", "gain_sums"):
                given[name] = given[name] + carry[name]
        carry = given

    cut = inner // 2
    if n_dp > 4:
        z_sum.settle(carry.head_sums)
        z_sum.start()
    x_low = tied(lows.x_low, queue[3], *([z_sum.send] if n_dp > 4 else []))
    small = jnp.concatenate(
        (
            carry.x_sums[: taps + 3].reshape(-1),
            carry.head_sums[:2, :head_count].reshape(-1),
            carry.gain_sums[0],
            carry.bc_sums[: taps + 1].reshape(-1),
        )
    )
    near_width = cut + side_width
    extra = jnp.pad(small, (0, -small.shape[0] % (16 * near_width))).reshape(-1, near_width)
    near_low = jnp.concatenate((x_low[:, :cut], lows.side_low), axis=1)
    near = ScatteredProduct(normed_left, near_low, n_dp, extra)
    far = ScatteredProduct(normed_left, x_low[:, cut:], n_dp)
    order = []
    for i in range(max(chunks - 2, 0), chunks):
        block_output = with_output(block_output, i)

    def with_grad(out, i):
        given = dict(cot=(out_cotangent, (part, model), lambda k, i=i: (i * 2 + k, 0)))
        return finished(grad_kernel, given, out, in_parts, in_other, i)

    input_grads = []
    for i in reversed(range(2, chunks)):
        input_grads.append(with_grad(input_grads[-1] if input_grads else None, i))
    input_grad = input_grads[-1] if input_grads else None
    starts = {(True, 4): queue[4:5], (False, 4): [block_output] + input_grads[-1:], (True, 8): queue[5:6]}

    def step(sum_of):
        if sum_of.stride < n_dp:
            sum_of.settle(*order)
            done = sum_of.stride == n_dp
            order[:] = [sum_of.total if done else sum_of.send]
            if not done:
                sum_of.start(*starts.get((sum_of is near, sum_of.stride), []))

    for one in (near, far):
        if n_dp > 1:
            one.start()
    for one in (near, far, near, z_sum, far, near, far, near, far) + (z_sum, near, far) * 8:
        step(one)
    z_weight_grad = z_sum.total
    out_part = lax.psum_scatter(out_product, "dp", scatter_dimension=0, tiled=True)
    near_part, far = near.total, far.total
    small = near.extra.reshape(-1)
    side_part = near_part[:, cut:]
    x_weight_grad = jnp.concatenate((near_part[:, :cut], far), axis=1)
    bc_part = side_part[:, : 2 * states]
    dt_weight_grad = side_part[:, 2 * states : 2 * states + head_count]

    bc_part = bc_part.reshape(n_tensor, -1, 2 * states)
    mine = lax.axis_index("tensor")
    theirs = lax.dynamic_index_in_dim(bc_part, 1 - mine, 0, keepdims=False)
    shared_at = (taps + 3) * inner + 2 * head_count
    shared_sums = small[shared_at : shared_at + model + (taps + 1) * 2 * states]
    shared_sums = jnp.pad(shared_sums, (0, -shared_sums.shape[0] % (HALO * 2 * states)))
    shared_sums = shared_sums.reshape(-1, 2 * states)
    ours = lax.dynamic_index_in_dim(bc_part, mine, 0, keepdims=False)
    came = swap_tensor(jnp.concatenate((theirs, shared_sums), axis=0), n_tensor)
    bc_weight_grad = ours + came[: ours.shape[0]]
    shared_sums = (shared_sums + came[ours.shape[0] :]).reshape(-1)

    x_end = (taps + 3) * inner
    x_sums = small[:x_end].reshape(taps + 3, inner)
    gated_gain_grad = x_sums[0]
    d_skip_grad = x_sums[1].reshape(head_count, head_dim).sum(axis=1)
    x_conv_grad = x_sums[2 : taps + 2]
    x_conv_bias_grad = x_sums[taps + 2]
    dt_bias_grad = small[x_end : x_end + head_count]
    a_log_grad = small[x_end + head_count : x_end + 2 * head_count]
    gain_total = shared_sums[:model]
    bc_total = shared_sums[model : model + (taps + 1) * 2 * states].reshape(taps + 1, 2 * states)
    place = lax.axis_index("dp") * n_tensor + lax.axis_index("tensor")
    places = n_dp * n_tensor

    def own(values, axis):
        size = values.shape[axis] // places
        return lax.dynamic_slice_in_dim(values, place * size, size, axis)

    norm_gain_grad = own(gain_total, 0)
    bc_conv_grad = own(bc_total[:taps], 1)
    bc_conv_bias_grad = own(bc_total[taps], 0)

    out_weight_grad = out_part.T

    for i in reversed(range(chunks - len(input_grads), )):
        input_grad = with_grad(input_grad, i)
    return (
        block_output,
        input_grad,
        norm_gain_grad,
        z_weight_grad,
        x_weight_grad,
        bc_weight_grad,
        dt_weight_grad,
        x_conv_grad,
        x_conv_bias_grad,
        bc_conv_grad,
        bc_conv_bias_grad,
        dt_bias_grad,
        a_log_grad,
        d_skip_grad,
        gated_gain_grad,
        out_weight_grad,
    )


def solution(mesh):
    in_specs = (
        P("dp", None),
        P(),
        P(None, "tensor"),
        P(None, "tensor"),
        P(),
        P(None, "tensor"),
        P(None, "tensor"),
        P("tensor"),
        P(),
        P(),
        P("tensor"),
        P("tensor"),
        P("tensor"),
        P("tensor"),
        P("tensor", None),
        P("dp", None),
    )
    out_specs = (
        P("dp", None),
        P("dp", None),
        P(("dp", "tensor")),
        P("dp", "tensor"),
        P("dp", "tensor"),
        P(("dp", "tensor"), None),
        P("dp", "tensor"),
        P(None, "tensor"),
        P("tensor"),
        P(None, ("dp", "tensor")),
        P(("dp", "tensor")),
        P("tensor"),
        P("tensor"),
        P("tensor"),
        P("tensor"),
        P("tensor", "dp"),
    )
    return jax.shard_map(body, mesh=mesh, in_specs=in_specs, out_specs=out_specs, check_vma=False)
```

```python
import functools
import math

import jax
import jax.numpy as jnp
from jax import lax
from jax.experimental import pallas as pl
from jax.experimental.pallas import tpu as pltpu
from jax.sharding import PartitionSpec as P

SPAN = 256
LEN = 1024
EPS = 1e-05
HIGH = lax.Precision.HIGHEST
LOG2E = math.log2(math.e)
F32 = jnp.float32
BF16 = jnp.bfloat16
HALO = 8
GROUP = 32
VMEM = 56 * 1024 * 1024


class Named(dict):
    __getattr__ = dict.get
    __setattr__ = dict.__setitem__


def mm(a, b):
    return lax.dot_general(a, b, (((1,), (0,)), ((), ())), preferred_element_type=F32)


def mm_nt(a, b):
    return lax.dot_general(a, b, (((1,), (1,)), ((), ())), preferred_element_type=F32)


def mm_tn(a, b):
    return lax.dot_general(a, b, (((0,), (0,)), ((), ())), preferred_element_type=F32)


def split3(x):
    hi = x.astype(BF16)
    rest = x - hi.astype(F32)
    mid = rest.astype(BF16)
    low = (rest - mid.astype(F32)).astype(BF16)
    return hi, mid, low


def split2(x):
    hi = x.astype(BF16)
    return hi, (x - hi.astype(F32)).astype(BF16)


def side(a, b):
    return jnp.concatenate((a, b), axis=1)


def folded(x):
    half = x.shape[1] // 2
    return x[:, :half] + x[:, half:]


def fine_nn(left_pair, b):
    bh, bl = split2(b)
    depth = b.shape[0]
    return mm(left_pair, jnp.concatenate((bh, bh), axis=0)) + mm(left_pair[:, :depth], bl)


def fine_rows(left_stack, b):
    bh, bl = split2(b)
    rows = left_stack.shape[0] // 2
    both = mm(left_stack, bh)
    return both[:rows] + both[rows:] + mm(left_stack[:rows], bl)


def fine_nt(a, b):
    ah, al = split2(a)
    bh, bl = split2(b)
    return folded(mm_nt(ah, jnp.concatenate((bh, bl), axis=0))) + mm_nt(al, bh)


def iota(shape, axis):
    return lax.broadcasted_iota(jnp.int32, shape, axis)


def times_transposed(left, right):
    return lax.dot_general(left, right, (((1,), (1,)), ((), ())), preferred_element_type=F32)


def softplus(v):
    return jnp.maximum(v, 0.0) + jnp.log1p(jnp.exp(-jnp.abs(v)))


def three_parts(x):
    hi, mid, low = split3(x)
    lane = iota(x.shape, 1)
    parts = jnp.where(
        lane < GROUP, hi.astype(F32), jnp.where(lane < 2 * GROUP, mid.astype(F32), low.astype(F32))
    )
    return parts.astype(BF16)


def spread_matrix(block, heads, head_dim, lanes):
    shape = (lanes, heads * head_dim)
    row, col = iota(shape, 0), iota(shape, 1)
    head = block * heads + col // head_dim
    hit = (row == head) | (row == head + GROUP) | (row == head + 2 * GROUP)
    return jnp.where(hit, 1.0, 0.0).astype(BF16)


def gather_matrix(block, heads, head_dim, lanes):
    shape = (heads * head_dim, lanes)
    row, col = iota(shape, 0), iota(shape, 1)
    return jnp.where(col == block * heads + row // head_dim, 1.0, 0.0).astype(BF16)


def triangle(n, lower):
    row, col = iota((n, n), 0), iota((n, n), 1)
    return jnp.where(row >= col if lower else row <= col, 1.0, 0.0)


def pair_masks(head_dim):
    lane = iota((1, 4 * head_dim), 1) // head_dim % 2
    return [jnp.where(lane == k, 1.0, 0.0).astype(BF16) for k in range(2)]


def pair_parts(parts, head_dim, pair):
    at = slice(2 * pair * head_dim, 2 * (pair + 1) * head_dim)
    return side(parts[0][:, at], parts[1][:, at])


def earlier(x, halo, by):
    if by == 0:
        return x
    rolled = pltpu.roll(x, by, 0)
    head = iota((HALO, x.shape[1]), 0) < by
    front = pltpu.roll(halo, by, 0) if halo is not None else 0.0
    return jnp.concatenate((jnp.where(head, front, rolled[:HALO]), rolled[HALO:]), axis=0)


def later(x, halo, by):
    if by == 0:
        return x
    rows = x.shape[0]
    rolled = pltpu.roll(x, rows - by, 0)
    tail = iota((HALO, x.shape[1]), 0) >= HALO - by
    back = pltpu.roll(halo, HALO - by, 0) if halo is not None else 0.0
    end = jnp.where(tail, back, rolled[rows - HALO :])
    return jnp.concatenate((rolled[: rows - HALO], end), axis=0)


def conv_of(x, halo, taps, bias):
    count = taps.shape[0]
    shifted = [earlier(x, halo, count - 1 - k) for k in range(count)]
    total = bias + taps[0:1] * shifted[0]
    for k in range(1, count):
        total = total + taps[k : k + 1] * shifted[k]
    return total, shifted


def conv_back(grad, halo, taps):
    count = taps.shape[0]
    total = taps[count - 1 : count] * grad
    for k in range(count - 1):
        total = total + taps[k : k + 1] * later(grad, halo, count - 1 - k)
    return total


def unpacked(ref, taps):
    return ref[:taps], ref[taps : taps + 1], ref[taps + 1 : taps + 2], ref[taps + 2 : taps + 3]


def maybe(ref):
    return None if ref is None else ref[...]


def silu_slope(v, s):
    return s + v * s * (1.0 - s)


def triangle_sum(x, lower):
    lanes = x.shape[1]
    parts = mm(triangle(x.shape[0], lower).astype(BF16), jnp.concatenate(split3(x), axis=1))
    return parts[:, :lanes] + parts[:, lanes : 2 * lanes] + parts[:, 2 * lanes :]


def steps_of(dt_pre, dt_bias_ref, a_log_ref):
    dt = softplus(dt_pre + dt_bias_ref[...])
    decay = -jnp.exp(a_log_ref[...])
    rates = dt * (decay * LOG2E)
    cum = triangle_sum(rates, True)
    return dt, decay, cum


def row_sums(x):
    lanes = 128
    part = x[:, :lanes]
    for at in range(lanes, x.shape[1], lanes):
        part = part + x[:, at : at + lanes]
    return jnp.sum(part.T, axis=0, keepdims=True)


PIECE = 32


def slot_of(rel, n):
    bits = n.bit_length() - 1
    p = sum((rel >> b & 1) << (bits - 1 - b) for b in range(1, bits))
    first, half, quarter = rel & 1, n // 2, n // 4
    return jnp.where(first == 1, p, jnp.where(p >= quarter, half + p - quarter, n - quarter + p))


def arrange_rows(start, n, place, turned, target):
    block = target.shape[0] // n
    if n == 1 or block % PIECE:
        target[pl.ds(pl.multiple_of(start, PIECE), turned.shape[0]), :] = turned
        return
    for at in range(0, turned.shape[0], PIECE):
        begin = start + at
        owner = lax.div(begin, block)
        slot = slot_of(owner ^ place[0], n)
        to = pl.multiple_of(slot * block + begin - owner * block, PIECE)
        target[pl.ds(to, PIECE), :] = turned[at : at + PIECE]


def fwd_kernel(first, heads, head_dim, blocks, n_dp, refs):
    j = pl.program_id(0)
    r = refs
    rows = r.normed.shape[0]
    half = rows // 2
    states = r.bc_pre.shape[1] // 2
    lanes = r.dt_pre.shape[1]

    @pl.when(j == 0)
    def _():
        bc_pre = r.bc_pre[...]
        u, _ = conv_of(bc_pre, maybe(r.bc_halo), r.bc_conv[...], r.bc_conv_bias[...])
        act = u * jax.nn.sigmoid(u)
        b, c = act[:, :states], act[:, states:]
        r.cb[...] = side(*split2(c))
        r.bt[...] = jnp.concatenate(split2(b.T), axis=0)
        r.scores[...] = fine_nt(c, b) * triangle(rows, True)
        dt, decay, cum = steps_of(r.dt_pre[...], r.dt_bias, r.a_log)
        r.cum_t[...] = cum.T
        r.parts[0:rows, :] = three_parts(cum)
        r.parts[rows : 2 * rows, :] = three_parts(dt)
        r.u_out[...] = jnp.zeros_like(r.u_out)
        r.acc[...] = jnp.zeros_like(r.acc)

    width = heads * head_dim
    xp, zp = r.x_pre[...], r.z_pre[...]
    gate = zp * jax.nn.sigmoid(zp)
    columns = r.normed.shape[1] // blocks
    here = pl.ds(pl.multiple_of(j * columns, columns), columns)
    turned = r.normed[:, here].T
    arrange_rows(j * columns, n_dp, r.place, turned, r.normed_t)
    r.cot_t[here, :] = r.cot[:, here].T
    taps = r.bc_conv.shape[0]
    conv, conv_bias, d_skip, gated_gain = unpacked(r.packed, taps)
    u, _ = conv_of(xp, maybe(r.x_halo), conv, conv_bias)
    xa = u * jax.nn.sigmoid(u)
    spread = mm(r.parts[...], spread_matrix(j, heads, head_dim, lanes))
    cum_e, dt_e = spread[:rows], spread[rows:]
    w = xa * dt_e
    last = cum_e[rows - 1 : rows, :]
    scaled = w * jnp.exp2(last - cum_e)
    masks = pair_masks(head_dim)
    parts = split2(w)
    empty = jnp.zeros((half, half), BF16)
    cols = []
    for pair in range(heads // 2):
        both = pair_parts(parts, head_dim, pair)
        total = 0.0
        for k in range(2):
            head = 2 * pair + k
            row = r.cum_t[pl.ds(j * heads + head, 1), :]
            col = cum_e[:, head * head_dim : head * head_dim + 1]
            m = jnp.exp2(jnp.minimum(col[:half] - row[:, :half], 0.0)) * r.scores[:half, :half]
            top = [side(part, empty) for part in split2(m)]
            m = jnp.exp2(jnp.minimum(col[half:] - row, 0.0)) * r.scores[half:, :]
            bot = split2(m)
            stack = jnp.concatenate((top[0], bot[0], top[1], bot[1]), axis=0)
            total = total + mm(stack, both * masks[k])
        cols.append(folded(total[:rows] + total[rows:]))
    y = side(*cols)
    if first:
        r.state_out[...] = fine_rows(r.bt[...], scaled)
    else:
        state = r.state[...]
        y = y + jnp.exp2(cum_e) * fine_nn(r.cb[...], state)
        r.state_out[...] = jnp.exp2(last) * state + fine_rows(r.bt[...], scaled)
    mixed = y + d_skip * xa
    r.mixed[...] = mixed
    gated = mixed * gate
    gain = gated * gated_gain
    r.u_out[...] += mm(gain.astype(BF16), r.out_w[...])
    r.acc[...] += gated * gated

    @pl.when(j == pl.num_programs(0) - 1)
    def _():
        r.sums[0:1, :] = row_sums(r.acc[...])
        r.sums[1:2, :] = row_sums(r.cot[...].astype(F32) * r.u_out[...])
        r.sums[2:HALO, :] = jnp.zeros((HALO - 2, rows), F32)


def row_scales(r, inner_total):
    sums = (r.sums[...] + r.sums_other[...]).T
    rms = lax.rsqrt(sums[:, 0:1] / inner_total + EPS)
    return rms, sums[:, 1:2] * rms / inner_total


def gate_kernel(inner_total, taps, width, r):
    rms, row_dot = row_scales(r, inner_total)
    for start in range(0, r.z_pre.shape[1], width):
        at = slice(start, start + width)
        mg = mm_nt(r.cot[...], r.out_w[at, :])
        r.mg[:, at] = mg
        zp, mixed = r.z_pre[:, at], r.mixed[:, at]
        gain = r.packed[taps + 2 : taps + 3, at]
        sz = jax.nn.sigmoid(zp)
        gated_unit = mixed * (zp * sz) * rms
        r.mixer_out[:, at] = (gated_unit * gain).astype(BF16)
        gg = rms * (mg * gain - gated_unit * row_dot)
        r.z_low[:, at] = (gg * mixed * silu_slope(zp, sz)).astype(BF16)


def output_kernel(inner_total, r):
    rms, _ = row_scales(r, inner_total)
    total = (r.share[...] + r.share_other[...]) * rms
    r.out[...] = (r.xin[...].astype(F32) + total).astype(BF16)


def grad_kernel(r):
    total = r.share[...] + r.share_other[...]
    r.out[...] = (r.cot[...].astype(F32) + total).astype(BF16)


def bwd_kernel(first, last_chunk, heads, head_dim, inner_total, refs):
    j = pl.program_id(0)
    r = refs
    rows = r.xin.shape[0]
    half = rows // 2
    states = r.bc_w.shape[1] // 2
    lanes = r.dt_w.shape[1]
    width = heads * head_dim
    taps = r.bc_conv.shape[0]
    conv, conv_bias, d_skip, gated_gain = unpacked(r.packed, taps)

    def column_sum(v):
        return jnp.sum(v, axis=0, keepdims=True)

    @pl.when(j == 0)
    def _():
        bc_pre = r.bc_pre[...]
        u, _ = conv_of(bc_pre, maybe(r.bc_halo), r.bc_conv[...], r.bc_conv_bias[...])
        s = jax.nn.sigmoid(u)
        act = u * s
        r.bc_slope[...] = silu_slope(u, s)
        b, c = act[:, :states], act[:, states:]
        r.bb[...] = side(*split2(b))
        r.cb[...] = side(*split2(c))
        r.ct[...] = jnp.concatenate(split2(c.T), axis=0)
        r.scores[...] = fine_nt(b, c) * triangle(rows, False)
        dt, decay, cum = steps_of(r.dt_pre[...], r.dt_bias, r.a_log)
        r.dt[...] = dt
        r.cum_t[...] = cum.T
        r.parts[0:rows, :] = three_parts(cum)
        r.parts[rows : 2 * rows, :] = three_parts(dt)
        r.x_low_before[...] = jnp.zeros_like(r.x_low_before)
        for ref in (r.d_scores, r.db, r.dc, r.d_cum, r.d_dt, r.ng):
            ref[...] = jnp.zeros_like(ref)
        rms, row_dot = row_scales(r, inner_total)
        r.rows[:, 0:1] = rms
        r.rows[:, 1:2] = row_dot

    xp = r.x_pre[...]
    u, shifted = conv_of(xp, maybe(r.x_halo), conv, conv_bias)
    su = jax.nn.sigmoid(u)
    xa = u * su
    spread = mm(r.parts[...], spread_matrix(j, heads, head_dim, lanes))
    cum_e, dt_e = spread[:rows], spread[rows:]
    w = xa * dt_e
    last = cum_e[rows - 1 : rows, :]
    rms, row_dot = r.rows[:, 0:1], r.rows[:, 1:2]
    zp, mg, mixed = r.z_pre[...], r.mg[...], r.mixed[...]
    sz = jax.nn.sigmoid(zp)
    gate = zp * sz
    y = mixed - d_skip * xa
    gated_unit = mixed * gate * rms
    gg = rms * (mg * gated_gain - gated_unit * row_dot)
    dy = gg * gate
    sums = [column_sum(mg * gated_unit), column_sum(dy * xa)]
    masks = pair_masks(head_dim)
    w_parts = split2(w)
    dy_parts = split2(dy)
    empty = jnp.zeros((half, half), BF16)
    cols = []
    for pair in range(heads // 2):
        at = slice(2 * pair * head_dim, 2 * (pair + 1) * head_dim)
        w_both = pair_parts(w_parts, head_dim, pair)
        w_high = w_parts[0][:, at]
        dy_both = pair_parts(dy_parts, head_dim, pair)
        dy_high = side(dy_parts[0][:, at], dy_parts[0][:, at])
        dy_low = dy_parts[1][:, at]
        total = 0.0
        for k in range(2):
            head = 2 * pair + k
            row = r.cum_t[pl.ds(j * heads + head, 1), :]
            col = cum_e[:, head * head_dim : head * head_dim + 1]
            dk, dk_high = dy_both * masks[k], dy_high * masks[k]
            dk_low = dy_low * masks[k][:, : 2 * head_dim]
            grad = mm_nt(w_both, dk_high) + mm_nt(w_high, dk_low)
            decay = jnp.exp2(jnp.minimum(row - col[:half], 0.0))
            r.d_scores[:half, :] += grad[:half] * decay
            top = split2(decay * r.scores[:half, :])
            decay = jnp.exp2(jnp.minimum(row[:, half:] - col[half:], 0.0))
            r.d_scores[half:, half:] += grad[half:, half:] * decay
            bot = [side(empty, part) for part in split2(decay * r.scores[half:, half:])]
            stack = jnp.concatenate((top[0], bot[0], top[1], bot[1]), axis=0)
            total = total + mm(stack, dk)
        cols.append(folded(total[:rows] + total[rows:]))
    dw = side(*cols)
    extra = None
    if not last_chunk:
        to_end = jnp.exp2(last - cum_e)
        d_state = r.d_state[...]
        ds = fine_nn(r.bb[...], d_state) * to_end
        r.db[...] += fine_nt(w * to_end, d_state)
        dw = dw + ds
        extra = column_sum(w * ds)
    if not first:
        state = r.state[...]
        g = jnp.exp2(cum_e) * dy
        r.dc[...] += fine_nt(g, state)
        d_state_out = fine_rows(r.ct[...], g)
        if not last_chunk:
            kept = jnp.exp2(last) * d_state
            extra = extra + column_sum(kept * state)
            d_state_out = d_state_out + kept
        r.d_state_out[...] = d_state_out
    q = dy * y - w * dw
    if extra is not None:
        q = q + jnp.where(iota((rows, 1), 0) == rows - 1, 1.0, 0.0) * extra
    gather = gather_matrix(j, heads, head_dim, lanes)
    stack = split3(q) + split2(dw * xa)
    given = mm(jnp.concatenate(stack, axis=0), gather)
    given = [given[at * rows : (at + 1) * rows] for at in range(5)]
    r.d_cum[...] += given[0] + given[1] + given[2]
    r.d_dt[...] += given[3] + given[4]
    du = (d_skip * dy + dw * dt_e) * silu_slope(u, su)
    xg = conv_back(du, maybe(r.du_halo), conv)
    r.du_halo_out[...] = du[:HALO, :]
    for k in range(taps):
        sums.append(column_sum(du * shifted[k]))
    sums.append(column_sum(du))
    for at, value in enumerate(sums):
        before = 0.0 if last_chunk else r.x_sums_in[at : at + 1, :]
        r.x_sums[at : at + 1, :] = value + before
    r.x_sums[len(sums) : HALO, :] = jnp.zeros((HALO - len(sums), width), F32)
    xl = xg.astype(BF16)
    r.x_low[...] = xl
    r.ng[...] += mm_nt(r.z_low[...], r.z_w[...]) + mm_nt(r.x_low_before[...], r.x_w[...])
    r.x_low_before[...] = xl

    @pl.when(j == pl.num_programs(0) - 1)
    def _():
        hi, low = split2(r.d_scores[...] * triangle(rows, False))
        cb, bb = r.cb[...], r.bb[...]
        db = r.db[...] + folded(mm(hi, cb)) + mm(low, cb[:, :states])
        dc = r.dc[...] + folded(mm_tn(hi, bb)) + mm_tn(low, bb[:, :states])
        d_rates = triangle_sum(r.d_cum[...], False)
        dt = r.dt[...]
        decay = -jnp.exp(r.a_log[...])
        d_dt = d_rates * decay + r.d_dt[...]
        dtg = d_dt * jax.nn.sigmoid(r.dt_pre[...] + r.dt_bias[...])
        dtl = jnp.where(iota(dtg.shape, 1) < GROUP, dtg, 0.0).astype(BF16)
        r.side_low[:, 2 * states :] = dtl
        head_sums = [column_sum(dtg), column_sum(d_rates * dt) * decay]
        for at, value in enumerate(head_sums):
            before = 0.0 if last_chunk else r.head_sums_in[at : at + 1, :]
            r.head_sums[at : at + 1, :] = value + before
        r.head_sums[2:HALO, :] = jnp.zeros((HALO - 2, lanes), F32)
        du_bc = jnp.concatenate((db, dc), axis=1) * r.bc_slope[...]
        bg = conv_back(du_bc, maybe(r.du_bc_halo), r.bc_conv[...])
        r.du_bc_halo_out[...] = du_bc[:HALO, :]
        bc_sums = []
        for k in range(taps):
            near = earlier(r.bc_pre[...], maybe(r.bc_halo), taps - 1 - k)
            bc_sums.append(column_sum(du_bc * near))
        bc_sums.append(column_sum(du_bc))
        for at, value in enumerate(bc_sums):
            before = 0.0 if last_chunk else r.bc_sums_in[at : at + 1, :]
            r.bc_sums[at : at + 1, :] = value + before
        r.bc_sums[len(bc_sums) : HALO, :] = jnp.zeros((HALO - len(bc_sums), 2 * states), F32)
        bl = bg.astype(BF16)
        r.side_low[:, : 2 * states] = bl
        ng = r.ng[...] + mm_nt(bl, r.bc_w[...]) + mm_nt(dtl, r.dt_w[...])
        ng = ng + mm_nt(xl, r.x_w_last[...])
        res = r.xin[...].astype(F32)
        inv = lax.rsqrt(jnp.mean(res * res, axis=1, keepdims=True) + EPS)
        unit = res * inv
        gain_sum = column_sum(ng * unit)
        r.gain_sums[0:1, :] = gain_sum if last_chunk else gain_sum + r.gain_sums_in[0:1, :]
        r.gain_sums[1:HALO, :] = jnp.zeros((HALO - 1, gain_sum.shape[1]), F32)
        iu = ng * r.norm_gain[...]
        r.in_part[...] = inv * (iu - unit * jnp.mean(iu * unit, axis=1, keepdims=True))


def run_kernel(body, grid, operands, outs, scratch, carried, waits=(), flops=1):
    names, arrays, specs = [], [], []
    for name, (array, block, index) in operands.items():
        names.append(name)
        arrays.append(array)
        whole = pl.BlockSpec(memory_space=pltpu.SMEM)
        specs.append(whole if block is None else pl.BlockSpec(block, index))
    aliases = {}
    out_names = list(outs)
    for at, name in enumerate(out_names):
        if name in carried:
            aliases[len(arrays)] = at
            names.append(name + "_old")
            arrays.append(carried[name])
            specs.append(pl.BlockSpec(memory_space=pl.ANY))
    for at, array in enumerate(waits):
        names.append(at)
        arrays.append(array)
        specs.append(pl.BlockSpec(memory_space=pl.ANY))
    scratch_names = list(scratch)

    def kernel(*refs):
        body(Named(zip(names + out_names + scratch_names, refs)))

    given = pl.pallas_call(
        kernel,
        grid=grid,
        in_specs=specs,
        out_specs=[pl.BlockSpec(block, index) for _, block, index in outs.values()],
        out_shape=[shape for shape, _, _ in outs.values()],
        scratch_shapes=[pltpu.VMEM(shape, kind) for shape, kind in scratch.values()],
        input_output_aliases=aliases,
        compiler_params=pltpu.CompilerParams(
            dimension_semantics=("arbitrary",) * len(grid), vmem_limit_bytes=VMEM
        ),
        cost_estimate=pl.CostEstimate(flops=flops, bytes_accessed=1, transcendentals=0),
    )(*arrays)
    return Named(zip(out_names, given))


def shape(*dims, kind=F32):
    return jax.ShapeDtypeStruct(dims, kind)


def relative_masks(n, flip):
    bits = n.bit_length() - 1
    masks = []
    for p in range(n // 2):
        masks.append(flip + sum((p >> (bits - 1 - b) & 1) << b for b in range(1, bits)))
    return masks


def arranged(left, n):
    if n == 1:
        return None, left, left[:0]
    block = left.shape[0] // n
    me = lax.axis_index("dp")
    if block % PIECE == 0:
        half, quarter = left.shape[0] // 2, left.shape[0] // 4
        return left[:half], left[half : half + quarter], left[half + quarter :]

    def pick(masks):
        rows = [lax.dynamic_slice_in_dim(left, (me ^ mask) * block, block, 0) for mask in masks]
        return jnp.concatenate(rows, axis=0)

    kept = relative_masks(n, 0)
    half = len(kept) // 2
    if not half:
        return pick(relative_masks(n, 1)), pick(kept), left[:0]
    return pick(relative_masks(n, 1)), pick(kept[half:]), pick(kept[:half])


def product(left, at, rows, right, came=None, came_at=0):
    depth, columns = right.shape
    step = next(size for size in (512, 384, 256, 128) if columns % size == 0)
    arrays, specs = [left, right], [
        pl.BlockSpec((rows, depth), lambda j: (at, 0)),
        pl.BlockSpec((depth, step), lambda j: (0, j)),
    ]
    if came is not None:
        arrays.append(came)
        specs.append(pl.BlockSpec((rows, step), lambda j: (came_at, j)))

    def kernel(*refs):
        given = mm(refs[0][...], refs[1][...])
        refs[-1][...] = given if came is None else given + refs[2][...]

    return pl.pallas_call(
        kernel,
        grid=(columns // step,),
        in_specs=specs,
        out_specs=pl.BlockSpec((rows, step), lambda j: (0, j)),
        out_shape=shape(rows, columns),
        compiler_params=pltpu.CompilerParams(
            dimension_semantics=("arbitrary",), vmem_limit_bytes=VMEM
        ),
        cost_estimate=pl.CostEstimate(flops=1, bytes_accessed=1, transcendentals=0),
    )(*arrays)


class ScatteredProduct:
    def __init__(self, left, right, n, extra=None):
        self.n, self.stride, self.left, self.right, self.extra = n, 1, left, right, extra
        if n == 1:
            self.total = mm(left[1], right)
        else:
            self.send = mm(left[0], right)

    def start(self, *others):
        pairs = [(p, p ^ self.stride) for p in range(self.n)]
        if self.stride == 1 and self.extra is not None:
            self.extra = self.extra + lax.ppermute(self.extra, "dp", pairs)
        self.came = lax.ppermute(after(self.send, *others), "dp", pairs)

    def settle(self, *others):
        came = after(self.came, *others)
        if self.stride == 1:
            rows = self.left[2].shape[0]
            keep = mm(self.left[2], self.right) + came[:rows]
            send = mm(self.left[1], self.right) + came[rows:]
        else:
            size = self.keep.shape[0]
            rows = size // 2 if 2 * self.stride < self.n else 0
            if self.extra is not None:
                self.extra = self.extra + came[size:]
            keep, send = self.keep[:rows] + came[:rows], self.keep[rows:] + came[rows:size]
        self.stride *= 2
        if self.stride == self.n:
            self.total = send
            return
        if self.extra is not None:
            send = jnp.concatenate((send, self.extra), axis=0)
        self.keep, self.send = keep, send

    def finish(self):
        while self.stride < self.n:
            self.start()
            self.settle()
        return self.total


def after(values, *others):
    return lax.optimization_barrier((values,) + others)[0]


def tied(array, *waits):
    def nothing(*refs):
        pass

    anywhere = pl.BlockSpec(memory_space=pl.ANY)
    out = pl.pallas_call(
        nothing,
        in_specs=[anywhere] * (1 + len(waits)),
        out_specs=anywhere,
        out_shape=jax.ShapeDtypeStruct(array.shape, array.dtype),
        input_output_aliases={0: 0},
        cost_estimate=pl.CostEstimate(flops=1, bytes_accessed=1, transcendentals=0),
    )(array, *waits)
    return out


def swap_tensor(values, n):
    return lax.ppermute(values, "tensor", [(t, t ^ 1) for t in range(n)])


def body(
    block_input,
    norm_gain,
    z_weight,
    x_weight,
    bc_weight,
    dt_weight,
    x_conv,
    x_conv_bias,
    bc_conv,
    bc_conv_bias,
    dt_bias,
    a_log,
    d_skip,
    gated_gain,
    out_weight,
    out_cotangent,
):
    n_dp, n_tensor = lax.axis_size("dp"), lax.axis_size("tensor")
    rows, model = block_input.shape
    inner = x_weight.shape[1]
    head_count = dt_weight.shape[1]
    head_dim = inner // head_count
    states = bc_weight.shape[1] // 2
    taps = x_conv.shape[0]
    heads = 4
    width = heads * head_dim
    blocks = inner // width
    chunks = rows // SPAN
    per_seq = LEN // SPAN
    inner_total = inner * n_tensor
    me = lax.axis_index("dp").astype(jnp.int32).reshape(1)
    lanes = 128
    side_width = 2 * states + lanes

    def tripled(v):
        one = jnp.pad(v, ((0, 0), (0, GROUP - head_count)))
        return jnp.pad(jnp.concatenate((one, one, one), axis=1), ((0, 0), (0, lanes - 3 * GROUP)))

    dt_w = tripled(dt_weight)
    dt_b = tripled(dt_bias[None])
    a_l = tripled(a_log[None])
    skip = jnp.repeat(d_skip, head_dim)[None]
    packed = jnp.concatenate((x_conv, x_conv_bias[None], skip, gated_gain[None]), axis=0)
    packed = jnp.pad(packed, ((0, HALO - packed.shape[0] % HALO), (0, 0)))
    gain_in = norm_gain[None]
    bc_bias = bc_conv_bias[None]

    def whole(array):
        return (array, array.shape, lambda j: (0,) * array.ndim)

    def columns(array):
        return (array, (array.shape[0], width), lambda j: (0, j))

    shared = Named(
        norm_gain=whole(gain_in),
        x_w=columns(x_weight),
        z_w=columns(z_weight),
        bc_w=whole(bc_weight),
        dt_w=whole(dt_w),
        packed=columns(packed),
        bc_conv=whole(bc_conv),
        bc_conv_bias=whole(bc_bias),
        dt_bias=whole(dt_b),
        a_log=whole(a_l),
    )

    residual = block_input.astype(F32)
    inv_rms = lax.rsqrt(jnp.mean(residual * residual, axis=1, keepdims=True) + EPS)
    normed = (residual * inv_rms * gain_in).astype(BF16)
    side_pre = mm(normed, jnp.concatenate((bc_weight, dt_w), axis=1))
    bc_pre, dt_pre = side_pre[:, : 2 * states], side_pre[:, 2 * states :]
    x_pre = mm(normed, x_weight)
    z_pre = mm(normed, z_weight)

    kept = Named()
    shares = []
    shares_other = []
    states_at = []
    for i in range(chunks):
        first = i % per_seq == 0

        def at_rows(j, i=i):
            return (i, 0)

        def at_block(j, i=i):
            return (i, j)

        def at_turned(j, i=i):
            return (0, i)

        operands = Named()
        for name in ("packed", "bc_conv", "bc_conv_bias", "dt_bias", "a_log"):
            operands[name] = shared[name]
        operands.place = (me, None, None)
        operands.cot = (out_cotangent, (SPAN, model), at_rows)
        operands.out_w = (out_weight, (width, model), lambda j: (j, 0))
        operands.normed = (normed, (SPAN, model), at_rows)
        operands.bc_pre = (bc_pre, (SPAN, 2 * states), at_rows)
        operands.dt_pre = (dt_pre, (SPAN, lanes), at_rows)
        operands.x_pre = (x_pre, (SPAN, width), at_block)
        operands.z_pre = (z_pre, (SPAN, width), at_block)
        before = i * (SPAN // HALO) - 1
        if not first:
            operands.x_halo = (x_pre, (HALO, width), lambda j, b=before: (b, j))
            operands.bc_halo = (bc_pre, (HALO, 2 * states), lambda j, b=before: (b, 0))
            operands.state = columns(states_at[-1])
        outs = Named(
            u_out=(shape(SPAN, model), (SPAN, model), lambda j: (0, 0)),
            state_out=(shape(states, inner), (states, width), lambda j: (0, j)),
            sums=(shape(HALO, rows), (HALO, SPAN), lambda j, i=i: (0, i)),
            normed_t=(shape(model, rows, kind=BF16), (model, SPAN), at_turned),
            cot_t=(shape(model, rows, kind=BF16), (model, SPAN), at_turned),
            mixed=(shape(rows, inner), (SPAN, width), at_block),
        )
        waits = []
        scratch = Named(
            cb=((SPAN, 2 * states), BF16),
            bt=((2 * states, SPAN), BF16),
            scores=((SPAN, SPAN), F32),
            cum_t=((lanes, SPAN), F32),
            parts=((2 * SPAN, lanes), BF16),
            acc=((SPAN, width), F32),
        )
        given = run_kernel(
            functools.partial(fwd_kernel, first, heads, head_dim, blocks, n_dp),
            (blocks,),
            operands,
            outs,
            scratch,
            kept,
            waits,
        )
        shares.append(given.pop("u_out"))
        if i == 0:
            shares_other.append(swap_tensor(shares[-1], n_tensor))
        states_at.append(given.pop("state_out"))
        kept = given

    kept.x_pre, kept.z_pre, kept.bc_pre, kept.dt_pre = x_pre, z_pre, bc_pre, dt_pre
    sums = kept.sums
    sums_other = swap_tensor(sums, n_tensor)

    def sums_at(rows_of, at=lambda i: i):
        block = (HALO, rows_of)
        return {
            "sums": (sums, block, lambda i: (0, at(i))),
            "sums_other": (sums_other, block, lambda i: (0, at(i))),
        }

    operands = Named(sums_at(SPAN))
    operands.packed = (packed, packed.shape, lambda i: (0, 0))
    for name, array in dict(z_pre=kept.z_pre, mixed=kept.mixed).items():
        operands[name] = (array, (SPAN, inner), lambda i: (i, 0))
    operands.cot = (out_cotangent, (SPAN, model), lambda i: (i, 0))
    operands.out_w = (out_weight, out_weight.shape, lambda i: (0, 0))
    outs = Named(
        mg=(shape(rows, inner), (SPAN, inner), lambda i: (i, 0)),
        mixer_out=(shape(rows, inner, kind=BF16), (SPAN, inner), lambda i: (i, 0)),
        z_low=(shape(rows, inner, kind=BF16), (SPAN, inner), lambda i: (i, 0)),
    )
    gates = run_kernel(
        functools.partial(gate_kernel, inner_total, taps, width),
        (chunks,),
        operands,
        outs,
        Named(),
        Named(),
        shares_other[:1],
    )
    for share in shares[1:]:
        shares_other.append(swap_tensor(after(share, sums_other), n_tensor))

    def finished(body, given, out, ours, theirs, at):
        operands = Named(given)
        for name, array in dict(share=ours, share_other=theirs).items():
            operands[name] = (array, (part, model), lambda k: (k, 0))
        outs = Named(out=(shape(rows, model, kind=BF16), (part, model), lambda k: (at + k, 0)))
        carried = Named() if out is None else Named(out=out)
        return run_kernel(body, (ours.shape[0] // part,), operands, outs, Named(), carried).out

    def with_output(out, piece):
        at = piece * SPAN // part
        given = sums_at(part, lambda k: at + k)
        given["xin"] = (block_input, (part, model), lambda k: (at + k, 0))
        kernel = functools.partial(output_kernel, inner_total)
        return finished(kernel, given, out, shares[piece], shares_other[piece], at)

    part = SPAN // 2
    block_output = with_output(None, 0)

    out_product = product(kept.cot_t, 0, model, gates.mixer_out)
    z_low = tied(gates.z_low, *shares_other[1:2], out_product, *([block_output] if chunks > 1 else []))
    kept.z_low, kept.mg = z_low, gates.mg
    normed_left = arranged(kept.normed_t, n_dp)
    z_sum = ScatteredProduct(normed_left, z_low, n_dp)
    if n_dp > 1:
        z_sum.start()
        z_sum.settle()
    y_waits = {0: [out_product], 2: shares_other[2:3]}
    if n_dp > 2:
        z_sum.start()
        y_waits[0] = [out_product, z_sum.send]


    lows = Named()
    carry = Named()
    in_parts = [None] * chunks
    in_other = [None] * chunks
    queue = [sums_other] * 3
    for i in reversed(range(chunks)):
        first = i % per_seq == 0
        last_chunk = i % per_seq == per_seq - 1
        start = i == chunks - 1

        def at_rows(j, i=i):
            return (i, 0)

        def at_block(j, i=i):
            return (i, j)

        operands = Named(shared)
        operands.xin = (block_input, (SPAN, model), at_rows)
        for name in ("bc_pre", "dt_pre"):
            operands[name] = (kept[name], (SPAN, kept[name].shape[1]), at_rows)
        operands.x_w = (x_weight, (model, width), lambda j: (0, jnp.maximum(j - 1, 0)))
        operands.x_w_last = (x_weight, (model, width), lambda j: (0, blocks - 1))
        for name in ("x_pre", "z_pre", "mg", "mixed", "z_low"):
            operands[name] = (kept[name], (SPAN, width), at_block)
        operands.sums = (sums, (HALO, SPAN), lambda j, i=i: (0, i))
        operands.sums_other = (sums_other, (HALO, SPAN), lambda j, i=i: (0, i))
        before = i * (SPAN // HALO) - 1
        if not first:
            operands.x_halo = (kept.x_pre, (HALO, width), lambda j, b=before: (b, j))
            operands.bc_halo = (kept.bc_pre, (HALO, 2 * states), lambda j, b=before: (b, 0))
            operands.state = columns(states_at[i - 1])
        if not last_chunk:
            operands.d_state = columns(carry.d_state_out)
            operands.du_halo = columns(carry.du_halo_out)
            operands.du_bc_halo = whole(carry.du_bc_halo_out)
            operands.x_sums_in = columns(carry.x_sums)
            for name in ("head_sums", "bc_sums", "gain_sums"):
                operands[name + "_in"] = whole(carry[name])
        outs = Named(
            in_part=(shape(SPAN, model), (SPAN, model), lambda j: (0, 0)),
            du_halo_out=(shape(HALO, inner), (HALO, width), lambda j: (0, j)),
            du_bc_halo_out=(shape(HALO, 2 * states), (HALO, 2 * states), lambda j: (0, 0)),
            x_sums=(shape(HALO, inner), (HALO, width), lambda j: (0, j)),
            head_sums=(shape(HALO, lanes), (HALO, lanes), lambda j: (0, 0)),
            bc_sums=(shape(HALO, 2 * states), (HALO, 2 * states), lambda j: (0, 0)),
            gain_sums=(shape(HALO, model), (HALO, model), lambda j: (0, 0)),
            x_low=(shape(rows, inner, kind=BF16), (SPAN, width), at_block),
            side_low=(shape(rows, side_width, kind=BF16), (SPAN, side_width), at_rows),
        )
        waits = y_waits.get(chunks - 1 - i, [])
        if i == 0:
            waits = waits + queue[3:4]
        if not first:
            outs.d_state_out = (shape(states, inner), (states, width), lambda j: (0, j))
        scratch = Named(
            bc_slope=((SPAN, 2 * states), F32),
            bb=((SPAN, 2 * states), BF16),
            cb=((SPAN, 2 * states), BF16),
            ct=((2 * states, SPAN), BF16),
            scores=((SPAN, SPAN), F32),
            d_scores=((SPAN, SPAN), F32),
            dt=((SPAN, lanes), F32),
            cum_t=((lanes, SPAN), F32),
            parts=((2 * SPAN, lanes), BF16),
            db=((SPAN, states), F32),
            dc=((SPAN, states), F32),
            d_cum=((SPAN, lanes), F32),
            d_dt=((SPAN, lanes), F32),
            ng=((SPAN, model), F32),
            x_low_before=((SPAN, width), BF16),
            rows=((SPAN, lanes), F32),
        )
        given = run_kernel(
            functools.partial(bwd_kernel, first, last_chunk, heads, head_dim, inner_total),
            (blocks,),
            operands,
            outs,
            scratch,
            lows,
            waits,
        )
        lows = Named(x_low=given.x_low, side_low=given.side_low)
        in_parts[i] = given.in_part
        queue.append(swap_tensor(in_parts[i], n_tensor))
        in_other[i] = queue[-1]
        if last_chunk and not start:
            for name in ("x_sums", "head_sums", "bc_sums", "gain_sums"):
                given[name] = given[name] + carry[name]
        carry = given

    cut = inner // 2
    z_wait = []
    if n_dp > 4:
        z_sum.settle(carry.head_sums)
        z_sum.start()
        z_wait = [z_sum.send]
    x_low = tied(lows.x_low, *queue[4:5], *z_wait)
    small = jnp.concatenate(
        (
            carry.x_sums[: taps + 3].reshape(-1),
            carry.head_sums[:2, :head_count].reshape(-1),
            carry.gain_sums[0],
            carry.bc_sums[: taps + 1].reshape(-1),
        )
    )
    near_width = cut + side_width
    extra = jnp.pad(small, (0, -small.shape[0] % (16 * near_width))).reshape(-1, near_width)
    near_low = jnp.concatenate((x_low[:, :cut], lows.side_low), axis=1)
    near = ScatteredProduct(normed_left, near_low, n_dp, extra)
    far = ScatteredProduct(normed_left, x_low[:, cut:], n_dp)
    out_part = lax.psum_scatter(out_product, "dp", scatter_dimension=0, tiled=True)
    order = []
    for i in range(1, len(shares)):
        block_output = with_output(block_output, i)

    def with_grad(out, i):
        given = dict(cot=(out_cotangent, (part, model), lambda k: (i * 2 + k, 0)))
        return finished(grad_kernel, given, out, in_parts[i], in_other[i], i * 2)

    input_grads = []
    for i in reversed(range(2, chunks)):
        input_grads.append(with_grad(input_grads[-1] if input_grads else None, i))
    input_grad = input_grads[-1] if input_grads else None
    starts = {(True, 2): [out_part]}
    starts[False, 4] = input_grads[-1:] + queue[5:6]
    if n_dp > 4:
        z_sum.settle(x_low)
        z_sum.start()
        starts[False, 2] = [z_sum.send]

    def step(sum_of):
        if sum_of.stride < n_dp:
            sum_of.settle(*order)
            done = sum_of.stride == n_dp
            order[:] = [sum_of.total if done else sum_of.send]
            if not done:
                sum_of.start(*starts.get((sum_of is near, sum_of.stride), []))

    for one in (near, far):
        if n_dp > 1:
            one.start()
    for one in (near, far, near):
        step(one)
    while z_sum.stride < n_dp:
        step(z_sum)
    starts[False, 4].append(z_sum.total)
    for one in (far, near) * 8:
        step(one)
    z_weight_grad = z_sum.total
    near_part, far = near.total, far.total
    small = near.extra.reshape(-1)
    side_part = near_part[:, cut:]
    x_weight_grad = jnp.concatenate((near_part[:, :cut], far), axis=1)
    bc_part = side_part[:, : 2 * states]
    dt_weight_grad = side_part[:, 2 * states : 2 * states + head_count]

    bc_part = bc_part.reshape(n_tensor, -1, 2 * states)
    mine = lax.axis_index("tensor")
    theirs = lax.dynamic_index_in_dim(bc_part, 1 - mine, 0, keepdims=False)
    shared_at = (taps + 3) * inner + 2 * head_count
    shared_sums = small[shared_at : shared_at + model + (taps + 1) * 2 * states]
    shared_sums = jnp.pad(shared_sums, (0, -shared_sums.shape[0] % (HALO * 2 * states)))
    shared_sums = shared_sums.reshape(-1, 2 * states)
    ours = lax.dynamic_index_in_dim(bc_part, mine, 0, keepdims=False)
    mixed_rows = jnp.concatenate((theirs, shared_sums), axis=0)
    came = swap_tensor(after(mixed_rows, block_output), n_tensor)
    bc_weight_grad = ours + came[: ours.shape[0]]
    shared_sums = (shared_sums + came[ours.shape[0] :]).reshape(-1)

    x_end = (taps + 3) * inner
    x_sums = small[:x_end].reshape(taps + 3, inner)
    gated_gain_grad = x_sums[0]
    d_skip_grad = x_sums[1].reshape(head_count, head_dim).sum(axis=1)
    x_conv_grad = x_sums[2 : taps + 2]
    x_conv_bias_grad = x_sums[taps + 2]
    dt_bias_grad = small[x_end : x_end + head_count]
    a_log_grad = small[x_end + head_count : x_end + 2 * head_count]
    gain_total = shared_sums[:model]
    bc_total = shared_sums[model : model + (taps + 1) * 2 * states].reshape(taps + 1, 2 * states)
    place = lax.axis_index("dp") * n_tensor + lax.axis_index("tensor")
    places = n_dp * n_tensor

    def own(values, axis):
        size = values.shape[axis] // places
        return lax.dynamic_slice_in_dim(values, place * size, size, axis)

    norm_gain_grad = own(gain_total, 0)
    bc_conv_grad = own(bc_total[:taps], 1)
    bc_conv_bias_grad = own(bc_total[taps], 0)

    out_weight_grad = out_part.T

    if chunks > 1:
        input_grad = with_grad(input_grad, 1)
    in_other[0] = after(in_other[0], far)
    input_grad = with_grad(input_grad, 0)
    return (
        block_output,
        input_grad,
        norm_gain_grad,
        z_weight_grad,
        x_weight_grad,
        bc_weight_grad,
        dt_weight_grad,
        x_conv_grad,
        x_conv_bias_grad,
        bc_conv_grad,
        bc_conv_bias_grad,
        dt_bias_grad,
        a_log_grad,
        d_skip_grad,
        gated_gain_grad,
        out_weight_grad,
    )


def solution(mesh):
    in_specs = (
        P("dp", None),
        P(),
        P(None, "tensor"),
        P(None, "tensor"),
        P(),
        P(None, "tensor"),
        P(None, "tensor"),
        P("tensor"),
        P(),
        P(),
        P("tensor"),
        P("tensor"),
        P("tensor"),
        P("tensor"),
        P("tensor", None),
        P("dp", None),
    )
    out_specs = (
        P("dp", None),
        P("dp", None),
        P(("dp", "tensor")),
        P("dp", "tensor"),
        P("dp", "tensor"),
        P(("dp", "tensor"), None),
        P("dp", "tensor"),
        P(None, "tensor"),
        P("tensor"),
        P(None, ("dp", "tensor")),
        P(("dp", "tensor")),
        P("tensor"),
        P("tensor"),
        P("tensor"),
        P("tensor"),
        P("tensor", "dp"),
    )
    return jax.shard_map(body, mesh=mesh, in_specs=in_specs, out_specs=out_specs, check_vma=False)
```

```python
import functools
import math

import jax
import jax.numpy as jnp
from jax import lax
from jax.experimental import pallas as pl
from jax.experimental.pallas import tpu as pltpu
from jax.sharding import PartitionSpec as P

SPAN = 256
LEN = 1024
EPS = 1e-05
HIGH = lax.Precision.HIGHEST
LOG2E = math.log2(math.e)
F32 = jnp.float32
BF16 = jnp.bfloat16
HALO = 8
GROUP = 32
VMEM = 56 * 1024 * 1024


class Named(dict):
    __getattr__ = dict.get
    __setattr__ = dict.__setitem__


def mm(a, b):
    return lax.dot_general(a, b, (((1,), (0,)), ((), ())), preferred_element_type=F32)


def mm_nt(a, b):
    return lax.dot_general(a, b, (((1,), (1,)), ((), ())), preferred_element_type=F32)


def mm_tn(a, b):
    return lax.dot_general(a, b, (((0,), (0,)), ((), ())), preferred_element_type=F32)


def split3(x):
    hi = x.astype(BF16)
    rest = x - hi.astype(F32)
    mid = rest.astype(BF16)
    low = (rest - mid.astype(F32)).astype(BF16)
    return hi, mid, low


def split2(x):
    hi = x.astype(BF16)
    return hi, (x - hi.astype(F32)).astype(BF16)


def side(a, b):
    return jnp.concatenate((a, b), axis=1)


def folded(x):
    half = x.shape[1] // 2
    return x[:, :half] + x[:, half:]


def fine_nn(left_pair, b):
    bh, bl = split2(b)
    depth = b.shape[0]
    return mm(left_pair, jnp.concatenate((bh, bh), axis=0)) + mm(left_pair[:, :depth], bl)


def fine_rows(left_stack, b):
    bh, bl = split2(b)
    rows = left_stack.shape[0] // 2
    both = mm(left_stack, bh)
    return both[:rows] + both[rows:] + mm(left_stack[:rows], bl)


def fine_nt(a, b):
    ah, al = split2(a)
    bh, bl = split2(b)
    return folded(mm_nt(ah, jnp.concatenate((bh, bl), axis=0))) + mm_nt(al, bh)


def iota(shape, axis):
    return lax.broadcasted_iota(jnp.int32, shape, axis)


def times_transposed(left, right):
    return lax.dot_general(left, right, (((1,), (1,)), ((), ())), preferred_element_type=F32)


def softplus(v):
    return jnp.maximum(v, 0.0) + jnp.log1p(jnp.exp(-jnp.abs(v)))


def three_parts(x):
    hi, mid, low = split3(x)
    lane = iota(x.shape, 1)
    parts = jnp.where(
        lane < GROUP, hi.astype(F32), jnp.where(lane < 2 * GROUP, mid.astype(F32), low.astype(F32))
    )
    return parts.astype(BF16)


def spread_matrix(block, heads, head_dim, lanes):
    shape = (lanes, heads * head_dim)
    row, col = iota(shape, 0), iota(shape, 1)
    head = block * heads + col // head_dim
    hit = (row == head) | (row == head + GROUP) | (row == head + 2 * GROUP)
    return jnp.where(hit, 1.0, 0.0).astype(BF16)


def gather_matrix(block, heads, head_dim, lanes):
    shape = (heads * head_dim, lanes)
    row, col = iota(shape, 0), iota(shape, 1)
    return jnp.where(col == block * heads + row // head_dim, 1.0, 0.0).astype(BF16)


def triangle(n, lower):
    row, col = iota((n, n), 0), iota((n, n), 1)
    return jnp.where(row >= col if lower else row <= col, 1.0, 0.0)


def pair_masks(head_dim):
    lane = iota((1, 4 * head_dim), 1) // head_dim % 2
    return [jnp.where(lane == k, 1.0, 0.0).astype(BF16) for k in range(2)]


def pair_parts(parts, head_dim, pair):
    at = slice(2 * pair * head_dim, 2 * (pair + 1) * head_dim)
    return side(parts[0][:, at], parts[1][:, at])


def earlier(x, halo, by):
    if by == 0:
        return x
    rolled = pltpu.roll(x, by, 0)
    head = iota((HALO, x.shape[1]), 0) < by
    front = pltpu.roll(halo, by, 0) if halo is not None else 0.0
    return jnp.concatenate((jnp.where(head, front, rolled[:HALO]), rolled[HALO:]), axis=0)


def later(x, halo, by):
    if by == 0:
        return x
    rows = x.shape[0]
    rolled = pltpu.roll(x, rows - by, 0)
    tail = iota((HALO, x.shape[1]), 0) >= HALO - by
    back = pltpu.roll(halo, HALO - by, 0) if halo is not None else 0.0
    end = jnp.where(tail, back, rolled[rows - HALO :])
    return jnp.concatenate((rolled[: rows - HALO], end), axis=0)


def conv_of(x, halo, taps, bias):
    count = taps.shape[0]
    shifted = [earlier(x, halo, count - 1 - k) for k in range(count)]
    total = bias + taps[0:1] * shifted[0]
    for k in range(1, count):
        total = total + taps[k : k + 1] * shifted[k]
    return total, shifted


def conv_back(grad, halo, taps):
    count = taps.shape[0]
    total = taps[count - 1 : count] * grad
    for k in range(count - 1):
        total = total + taps[k : k + 1] * later(grad, halo, count - 1 - k)
    return total


def unpacked(ref, taps):
    return ref[:taps], ref[taps : taps + 1], ref[taps + 1 : taps + 2], ref[taps + 2 : taps + 3]


def maybe(ref):
    return None if ref is None else ref[...]


def silu_slope(v, s):
    return s + v * s * (1.0 - s)


def triangle_sum(x, lower):
    lanes = x.shape[1]
    parts = mm(triangle(x.shape[0], lower).astype(BF16), jnp.concatenate(split3(x), axis=1))
    return parts[:, :lanes] + parts[:, lanes : 2 * lanes] + parts[:, 2 * lanes :]


def steps_of(dt_pre, dt_bias_ref, a_log_ref):
    dt = softplus(dt_pre + dt_bias_ref[...])
    decay = -jnp.exp(a_log_ref[...])
    rates = dt * (decay * LOG2E)
    cum = triangle_sum(rates, True)
    return dt, decay, cum


def row_sums(x):
    lanes = 128
    part = x[:, :lanes]
    for at in range(lanes, x.shape[1], lanes):
        part = part + x[:, at : at + lanes]
    return jnp.sum(part.T, axis=0, keepdims=True)


PIECE = 32


def slot_of(rel, n):
    bits = n.bit_length() - 1
    p = sum((rel >> b & 1) << (bits - 1 - b) for b in range(1, bits))
    first, half, quarter = rel & 1, n // 2, n // 4
    return jnp.where(first == 1, p, jnp.where(p >= quarter, half + p - quarter, n - quarter + p))


def arrange_rows(start, n, place, turned, target):
    block = target.shape[0] // n
    if n == 1 or block % PIECE:
        target[pl.ds(pl.multiple_of(start, PIECE), turned.shape[0]), :] = turned
        return
    for at in range(0, turned.shape[0], PIECE):
        begin = start + at
        owner = lax.div(begin, block)
        slot = slot_of(owner ^ place[0], n)
        to = pl.multiple_of(slot * block + begin - owner * block, PIECE)
        target[pl.ds(to, PIECE), :] = turned[at : at + PIECE]


def fwd_kernel(first, heads, head_dim, blocks, n_dp, refs):
    j = pl.program_id(0)
    r = refs
    rows = r.normed.shape[0]
    half = rows // 2
    states = r.bc_pre.shape[1] // 2
    lanes = r.dt_pre.shape[1]

    @pl.when(j == 0)
    def _():
        bc_pre = r.bc_pre[...]
        u, _ = conv_of(bc_pre, maybe(r.bc_halo), r.bc_conv[...], r.bc_conv_bias[...])
        act = u * jax.nn.sigmoid(u)
        b, c = act[:, :states], act[:, states:]
        r.cb[...] = side(*split2(c))
        r.bt[...] = jnp.concatenate(split2(b.T), axis=0)
        r.scores[...] = fine_nt(c, b) * triangle(rows, True)
        dt, decay, cum = steps_of(r.dt_pre[...], r.dt_bias, r.a_log)
        r.cum_t[...] = cum.T
        r.parts[0:rows, :] = three_parts(cum)
        r.parts[rows : 2 * rows, :] = three_parts(dt)
        r.u_out[...] = jnp.zeros_like(r.u_out)
        r.acc[...] = jnp.zeros_like(r.acc)

    width = heads * head_dim
    xp, zp = r.x_pre[...], r.z_pre[...]
    gate = zp * jax.nn.sigmoid(zp)
    columns = r.normed.shape[1] // blocks
    here = pl.ds(pl.multiple_of(j * columns, columns), columns)
    turned = r.normed[:, here].T
    arrange_rows(j * columns, n_dp, r.place, turned, r.normed_t)
    r.cot_t[here, :] = r.cot[:, here].T
    taps = r.bc_conv.shape[0]
    conv, conv_bias, d_skip, gated_gain = unpacked(r.packed, taps)
    u, _ = conv_of(xp, maybe(r.x_halo), conv, conv_bias)
    xa = u * jax.nn.sigmoid(u)
    spread = mm(r.parts[...], spread_matrix(j, heads, head_dim, lanes))
    cum_e, dt_e = spread[:rows], spread[rows:]
    w = xa * dt_e
    last = cum_e[rows - 1 : rows, :]
    scaled = w * jnp.exp2(last - cum_e)
    masks = pair_masks(head_dim)
    parts = split2(w)
    empty = jnp.zeros((half, half), BF16)
    cols = []
    for pair in range(heads // 2):
        both = pair_parts(parts, head_dim, pair)
        total = 0.0
        for k in range(2):
            head = 2 * pair + k
            row = r.cum_t[pl.ds(j * heads + head, 1), :]
            col = cum_e[:, head * head_dim : head * head_dim + 1]
            m = jnp.exp2(jnp.minimum(col[:half] - row[:, :half], 0.0)) * r.scores[:half, :half]
            top = [side(part, empty) for part in split2(m)]
            m = jnp.exp2(jnp.minimum(col[half:] - row, 0.0)) * r.scores[half:, :]
            bot = split2(m)
            stack = jnp.concatenate((top[0], bot[0], top[1], bot[1]), axis=0)
            total = total + mm(stack, both * masks[k])
        cols.append(folded(total[:rows] + total[rows:]))
    y = side(*cols)
    if first:
        r.state_out[...] = fine_rows(r.bt[...], scaled)
    else:
        state = r.state[...]
        y = y + jnp.exp2(cum_e) * fine_nn(r.cb[...], state)
        r.state_out[...] = jnp.exp2(last) * state + fine_rows(r.bt[...], scaled)
    mixed = y + d_skip * xa
    r.mixed[...] = mixed
    gated = mixed * gate
    gain = gated * gated_gain
    r.u_out[...] += mm(gain.astype(BF16), r.out_w[...])
    r.acc[...] += gated * gated

    @pl.when(j == pl.num_programs(0) - 1)
    def _():
        r.sums[0:1, :] = row_sums(r.acc[...])
        r.sums[1:2, :] = row_sums(r.cot[...].astype(F32) * r.u_out[...])
        r.sums[2:HALO, :] = jnp.zeros((HALO - 2, rows), F32)


def row_scales(r, inner_total):
    sums = (r.sums[...] + r.sums_other[...]).T
    rms = lax.rsqrt(sums[:, 0:1] / inner_total + EPS)
    return rms, sums[:, 1:2] * rms / inner_total


def gate_kernel(inner_total, taps, width, r):
    rms, row_dot = row_scales(r, inner_total)
    for start in range(0, r.z_pre.shape[1], width):
        at = slice(start, start + width)
        mg = mm_nt(r.cot[...], r.out_w[at, :])
        r.mg[:, at] = mg
        zp, mixed = r.z_pre[:, at], r.mixed[:, at]
        gain = r.packed[taps + 2 : taps + 3, at]
        sz = jax.nn.sigmoid(zp)
        gated_unit = mixed * (zp * sz) * rms
        r.mixer_out[:, at] = (gated_unit * gain).astype(BF16)
        gg = rms * (mg * gain - gated_unit * row_dot)
        r.z_low[:, at] = (gg * mixed * silu_slope(zp, sz)).astype(BF16)


def output_kernel(inner_total, r):
    rms, _ = row_scales(r, inner_total)
    total = (r.share[...] + r.share_other[...]) * rms
    r.out[...] = (r.xin[...].astype(F32) + total).astype(BF16)


def grad_kernel(r):
    total = r.share[...] + r.share_other[...]
    r.out[...] = (r.cot[...].astype(F32) + total).astype(BF16)


def bwd_kernel(first, last_chunk, heads, head_dim, inner_total, refs):
    j = pl.program_id(0)
    r = refs
    rows = r.xin.shape[0]
    half = rows // 2
    states = r.bc_w.shape[1] // 2
    lanes = r.dt_w.shape[1]
    width = heads * head_dim
    taps = r.bc_conv.shape[0]
    conv, conv_bias, d_skip, gated_gain = unpacked(r.packed, taps)

    def column_sum(v):
        return jnp.sum(v, axis=0, keepdims=True)

    @pl.when(j == 0)
    def _():
        bc_pre = r.bc_pre[...]
        u, _ = conv_of(bc_pre, maybe(r.bc_halo), r.bc_conv[...], r.bc_conv_bias[...])
        s = jax.nn.sigmoid(u)
        act = u * s
        r.bc_slope[...] = silu_slope(u, s)
        b, c = act[:, :states], act[:, states:]
        r.bb[...] = side(*split2(b))
        r.cb[...] = side(*split2(c))
        r.ct[...] = jnp.concatenate(split2(c.T), axis=0)
        r.scores[...] = fine_nt(b, c) * triangle(rows, False)
        dt, decay, cum = steps_of(r.dt_pre[...], r.dt_bias, r.a_log)
        r.dt[...] = dt
        r.cum_t[...] = cum.T
        r.parts[0:rows, :] = three_parts(cum)
        r.parts[rows : 2 * rows, :] = three_parts(dt)
        r.x_low_before[...] = jnp.zeros_like(r.x_low_before)
        for ref in (r.d_scores, r.db, r.dc, r.d_cum, r.d_dt, r.ng):
            ref[...] = jnp.zeros_like(ref)
        rms, row_dot = row_scales(r, inner_total)
        r.rows[:, 0:1] = rms
        r.rows[:, 1:2] = row_dot

    xp = r.x_pre[...]
    u, shifted = conv_of(xp, maybe(r.x_halo), conv, conv_bias)
    su = jax.nn.sigmoid(u)
    xa = u * su
    spread = mm(r.parts[...], spread_matrix(j, heads, head_dim, lanes))
    cum_e, dt_e = spread[:rows], spread[rows:]
    w = xa * dt_e
    last = cum_e[rows - 1 : rows, :]
    rms, row_dot = r.rows[:, 0:1], r.rows[:, 1:2]
    zp, mg, mixed = r.z_pre[...], r.mg[...], r.mixed[...]
    sz = jax.nn.sigmoid(zp)
    gate = zp * sz
    y = mixed - d_skip * xa
    gated_unit = mixed * gate * rms
    gg = rms * (mg * gated_gain - gated_unit * row_dot)
    dy = gg * gate
    sums = [column_sum(mg * gated_unit), column_sum(dy * xa)]
    masks = pair_masks(head_dim)
    w_parts = split2(w)
    dy_parts = split2(dy)
    empty = jnp.zeros((half, half), BF16)
    cols = []
    for pair in range(heads // 2):
        at = slice(2 * pair * head_dim, 2 * (pair + 1) * head_dim)
        w_both = pair_parts(w_parts, head_dim, pair)
        w_high = w_parts[0][:, at]
        dy_both = pair_parts(dy_parts, head_dim, pair)
        dy_high = side(dy_parts[0][:, at], dy_parts[0][:, at])
        dy_low = dy_parts[1][:, at]
        total = 0.0
        for k in range(2):
            head = 2 * pair + k
            row = r.cum_t[pl.ds(j * heads + head, 1), :]
            col = cum_e[:, head * head_dim : head * head_dim + 1]
            dk, dk_high = dy_both * masks[k], dy_high * masks[k]
            dk_low = dy_low * masks[k][:, : 2 * head_dim]
            grad = mm_nt(w_both, dk_high) + mm_nt(w_high, dk_low)
            decay = jnp.exp2(jnp.minimum(row - col[:half], 0.0))
            r.d_scores[:half, :] += grad[:half] * decay
            top = split2(decay * r.scores[:half, :])
            decay = jnp.exp2(jnp.minimum(row[:, half:] - col[half:], 0.0))
            r.d_scores[half:, half:] += grad[half:, half:] * decay
            bot = [side(empty, part) for part in split2(decay * r.scores[half:, half:])]
            stack = jnp.concatenate((top[0], bot[0], top[1], bot[1]), axis=0)
            total = total + mm(stack, dk)
        cols.append(folded(total[:rows] + total[rows:]))
    dw = side(*cols)
    extra = None
    if not last_chunk:
        to_end = jnp.exp2(last - cum_e)
        d_state = r.d_state[...]
        ds = fine_nn(r.bb[...], d_state) * to_end
        r.db[...] += fine_nt(w * to_end, d_state)
        dw = dw + ds
        extra = column_sum(w * ds)
    if not first:
        state = r.state[...]
        g = jnp.exp2(cum_e) * dy
        r.dc[...] += fine_nt(g, state)
        d_state_out = fine_rows(r.ct[...], g)
        if not last_chunk:
            kept = jnp.exp2(last) * d_state
            extra = extra + column_sum(kept * state)
            d_state_out = d_state_out + kept
        r.d_state_out[...] = d_state_out
    q = dy * y - w * dw
    if extra is not None:
        q = q + jnp.where(iota((rows, 1), 0) == rows - 1, 1.0, 0.0) * extra
    gather = gather_matrix(j, heads, head_dim, lanes)
    stack = split3(q) + split2(dw * xa)
    given = mm(jnp.concatenate(stack, axis=0), gather)
    given = [given[at * rows : (at + 1) * rows] for at in range(5)]
    r.d_cum[...] += given[0] + given[1] + given[2]
    r.d_dt[...] += given[3] + given[4]
    du = (d_skip * dy + dw * dt_e) * silu_slope(u, su)
    xg = conv_back(du, maybe(r.du_halo), conv)
    r.du_halo_out[...] = du[:HALO, :]
    for k in range(taps):
        sums.append(column_sum(du * shifted[k]))
    sums.append(column_sum(du))
    for at, value in enumerate(sums):
        before = 0.0 if last_chunk else r.x_sums_in[at : at + 1, :]
        r.x_sums[at : at + 1, :] = value + before
    r.x_sums[len(sums) : HALO, :] = jnp.zeros((HALO - len(sums), width), F32)
    xl = xg.astype(BF16)
    r.x_low[...] = xl
    r.ng[...] += mm_nt(r.z_low[...], r.z_w[...]) + mm_nt(r.x_low_before[...], r.x_w[...])
    r.x_low_before[...] = xl

    @pl.when(j == pl.num_programs(0) - 1)
    def _():
        hi, low = split2(r.d_scores[...] * triangle(rows, False))
        cb, bb = r.cb[...], r.bb[...]
        db = r.db[...] + folded(mm(hi, cb)) + mm(low, cb[:, :states])
        dc = r.dc[...] + folded(mm_tn(hi, bb)) + mm_tn(low, bb[:, :states])
        d_rates = triangle_sum(r.d_cum[...], False)
        dt = r.dt[...]
        decay = -jnp.exp(r.a_log[...])
        d_dt = d_rates * decay + r.d_dt[...]
        dtg = d_dt * jax.nn.sigmoid(r.dt_pre[...] + r.dt_bias[...])
        dtl = jnp.where(iota(dtg.shape, 1) < GROUP, dtg, 0.0).astype(BF16)
        r.side_low[:, 2 * states :] = dtl
        head_sums = [column_sum(dtg), column_sum(d_rates * dt) * decay]
        for at, value in enumerate(head_sums):
            before = 0.0 if last_chunk else r.head_sums_in[at : at + 1, :]
            r.head_sums[at : at + 1, :] = value + before
        r.head_sums[2:HALO, :] = jnp.zeros((HALO - 2, lanes), F32)
        du_bc = jnp.concatenate((db, dc), axis=1) * r.bc_slope[...]
        bg = conv_back(du_bc, maybe(r.du_bc_halo), r.bc_conv[...])
        r.du_bc_halo_out[...] = du_bc[:HALO, :]
        bc_sums = []
        for k in range(taps):
            near = earlier(r.bc_pre[...], maybe(r.bc_halo), taps - 1 - k)
            bc_sums.append(column_sum(du_bc * near))
        bc_sums.append(column_sum(du_bc))
        for at, value in enumerate(bc_sums):
            before = 0.0 if last_chunk else r.bc_sums_in[at : at + 1, :]
            r.bc_sums[at : at + 1, :] = value + before
        r.bc_sums[len(bc_sums) : HALO, :] = jnp.zeros((HALO - len(bc_sums), 2 * states), F32)
        bl = bg.astype(BF16)
        r.side_low[:, : 2 * states] = bl
        ng = r.ng[...] + mm_nt(bl, r.bc_w[...]) + mm_nt(dtl, r.dt_w[...])
        ng = ng + mm_nt(xl, r.x_w_last[...])
        res = r.xin[...].astype(F32)
        inv = lax.rsqrt(jnp.mean(res * res, axis=1, keepdims=True) + EPS)
        unit = res * inv
        gain_sum = column_sum(ng * unit)
        r.gain_sums[0:1, :] = gain_sum if last_chunk else gain_sum + r.gain_sums_in[0:1, :]
        r.gain_sums[1:HALO, :] = jnp.zeros((HALO - 1, gain_sum.shape[1]), F32)
        iu = ng * r.norm_gain[...]
        r.in_part[...] = inv * (iu - unit * jnp.mean(iu * unit, axis=1, keepdims=True))


def run_kernel(body, grid, operands, outs, scratch, carried, waits=(), flops=1):
    names, arrays, specs = [], [], []
    for name, (array, block, index) in operands.items():
        names.append(name)
        arrays.append(array)
        whole = pl.BlockSpec(memory_space=pltpu.SMEM)
        specs.append(whole if block is None else pl.BlockSpec(block, index))
    aliases = {}
    out_names = list(outs)
    for at, name in enumerate(out_names):
        if name in carried:
            aliases[len(arrays)] = at
            names.append(name + "_old")
            arrays.append(carried[name])
            specs.append(pl.BlockSpec(memory_space=pl.ANY))
    for at, array in enumerate(waits):
        names.append(at)
        arrays.append(array)
        specs.append(pl.BlockSpec(memory_space=pl.ANY))
    scratch_names = list(scratch)

    def kernel(*refs):
        body(Named(zip(names + out_names + scratch_names, refs)))

    given = pl.pallas_call(
        kernel,
        grid=grid,
        in_specs=specs,
        out_specs=[pl.BlockSpec(block, index) for _, block, index in outs.values()],
        out_shape=[shape for shape, _, _ in outs.values()],
        scratch_shapes=[pltpu.VMEM(shape, kind) for shape, kind in scratch.values()],
        input_output_aliases=aliases,
        compiler_params=pltpu.CompilerParams(
            dimension_semantics=("arbitrary",) * len(grid), vmem_limit_bytes=VMEM
        ),
        cost_estimate=pl.CostEstimate(flops=flops, bytes_accessed=1, transcendentals=0),
    )(*arrays)
    return Named(zip(out_names, given))


def shape(*dims, kind=F32):
    return jax.ShapeDtypeStruct(dims, kind)


def relative_masks(n, flip):
    bits = n.bit_length() - 1
    masks = []
    for p in range(n // 2):
        masks.append(flip + sum((p >> (bits - 1 - b) & 1) << b for b in range(1, bits)))
    return masks


def arranged(left, n):
    if n == 1:
        return None, left, left[:0]
    block = left.shape[0] // n
    me = lax.axis_index("dp")
    if block % PIECE == 0:
        half, quarter = left.shape[0] // 2, left.shape[0] // 4
        return left[:half], left[half : half + quarter], left[half + quarter :]

    def pick(masks):
        rows = [lax.dynamic_slice_in_dim(left, (me ^ mask) * block, block, 0) for mask in masks]
        return jnp.concatenate(rows, axis=0)

    kept = relative_masks(n, 0)
    half = len(kept) // 2
    if not half:
        return pick(relative_masks(n, 1)), pick(kept), left[:0]
    return pick(relative_masks(n, 1)), pick(kept[half:]), pick(kept[:half])


def product(left, at, rows, right, came=None, came_at=0):
    depth, columns = right.shape
    step = next(size for size in (512, 384, 256, 128) if columns % size == 0)
    arrays, specs = [left, right], [
        pl.BlockSpec((rows, depth), lambda j: (at, 0)),
        pl.BlockSpec((depth, step), lambda j: (0, j)),
    ]
    if came is not None:
        arrays.append(came)
        specs.append(pl.BlockSpec((rows, step), lambda j: (came_at, j)))

    def kernel(*refs):
        given = mm(refs[0][...], refs[1][...])
        refs[-1][...] = given if came is None else given + refs[2][...]

    return pl.pallas_call(
        kernel,
        grid=(columns // step,),
        in_specs=specs,
        out_specs=pl.BlockSpec((rows, step), lambda j: (0, j)),
        out_shape=shape(rows, columns),
        compiler_params=pltpu.CompilerParams(
            dimension_semantics=("arbitrary",), vmem_limit_bytes=VMEM
        ),
        cost_estimate=pl.CostEstimate(flops=1, bytes_accessed=1, transcendentals=0),
    )(*arrays)


class ScatteredProduct:
    def __init__(self, left, right, n, extra=None):
        self.n, self.stride, self.left, self.right, self.extra = n, 1, left, right, extra
        if n == 1:
            self.total = mm(left[1], right)
        else:
            self.send = mm(left[0], right)

    def start(self, *others):
        pairs = [(p, p ^ self.stride) for p in range(self.n)]
        if self.stride == 1 and self.extra is not None:
            self.extra = self.extra + lax.ppermute(self.extra, "dp", pairs)
        self.came = lax.ppermute(after(self.send, *others), "dp", pairs)

    def settle(self, *others):
        came = after(self.came, *others)
        if self.stride == 1:
            rows = self.left[2].shape[0]
            keep = mm(self.left[2], self.right) + came[:rows]
            send = mm(self.left[1], self.right) + came[rows:]
        else:
            size = self.keep.shape[0]
            rows = size // 2 if 2 * self.stride < self.n else 0
            if self.extra is not None:
                self.extra = self.extra + came[size:]
            keep, send = self.keep[:rows] + came[:rows], self.keep[rows:] + came[rows:size]
        self.stride *= 2
        if self.stride == self.n:
            self.total = send
            return
        if self.extra is not None:
            send = jnp.concatenate((send, self.extra), axis=0)
        self.keep, self.send = keep, send

    def finish(self):
        while self.stride < self.n:
            self.start()
            self.settle()
        return self.total


def after(values, *others):
    return lax.optimization_barrier((values,) + others)[0]


def tied(array, *waits):
    def nothing(*refs):
        pass

    anywhere = pl.BlockSpec(memory_space=pl.ANY)
    out = pl.pallas_call(
        nothing,
        in_specs=[anywhere] * (1 + len(waits)),
        out_specs=anywhere,
        out_shape=jax.ShapeDtypeStruct(array.shape, array.dtype),
        input_output_aliases={0: 0},
        cost_estimate=pl.CostEstimate(flops=1, bytes_accessed=1, transcendentals=0),
    )(array, *waits)
    return out


def swap_tensor(values, n):
    return lax.ppermute(values, "tensor", [(t, t ^ 1) for t in range(n)])


def body(
    block_input,
    norm_gain,
    z_weight,
    x_weight,
    bc_weight,
    dt_weight,
    x_conv,
    x_conv_bias,
    bc_conv,
    bc_conv_bias,
    dt_bias,
    a_log,
    d_skip,
    gated_gain,
    out_weight,
    out_cotangent,
):
    n_dp, n_tensor = lax.axis_size("dp"), lax.axis_size("tensor")
    rows, model = block_input.shape
    inner = x_weight.shape[1]
    head_count = dt_weight.shape[1]
    head_dim = inner // head_count
    states = bc_weight.shape[1] // 2
    taps = x_conv.shape[0]
    heads = 4
    width = heads * head_dim
    blocks = inner // width
    chunks = rows // SPAN
    per_seq = LEN // SPAN
    inner_total = inner * n_tensor
    me = lax.axis_index("dp").astype(jnp.int32).reshape(1)
    lanes = 128
    side_width = 2 * states + lanes

    def tripled(v):
        one = jnp.pad(v, ((0, 0), (0, GROUP - head_count)))
        return jnp.pad(jnp.concatenate((one, one, one), axis=1), ((0, 0), (0, lanes - 3 * GROUP)))

    dt_w = tripled(dt_weight)
    dt_b = tripled(dt_bias[None])
    a_l = tripled(a_log[None])
    skip = jnp.repeat(d_skip, head_dim)[None]
    packed = jnp.concatenate((x_conv, x_conv_bias[None], skip, gated_gain[None]), axis=0)
    packed = jnp.pad(packed, ((0, HALO - packed.shape[0] % HALO), (0, 0)))
    gain_in = norm_gain[None]
    bc_bias = bc_conv_bias[None]

    def whole(array):
        return (array, array.shape, lambda j: (0,) * array.ndim)

    def columns(array):
        return (array, (array.shape[0], width), lambda j: (0, j))

    shared = Named(
        norm_gain=whole(gain_in),
        x_w=columns(x_weight),
        z_w=columns(z_weight),
        bc_w=whole(bc_weight),
        dt_w=whole(dt_w),
        packed=columns(packed),
        bc_conv=whole(bc_conv),
        bc_conv_bias=whole(bc_bias),
        dt_bias=whole(dt_b),
        a_log=whole(a_l),
    )

    residual = block_input.astype(F32)
    inv_rms = lax.rsqrt(jnp.mean(residual * residual, axis=1, keepdims=True) + EPS)
    normed = (residual * inv_rms * gain_in).astype(BF16)
    side_pre = mm(normed, jnp.concatenate((bc_weight, dt_w), axis=1))
    bc_pre, dt_pre = side_pre[:, : 2 * states], side_pre[:, 2 * states :]
    x_pre = mm(normed, x_weight)
    z_pre = mm(normed, z_weight)

    kept = Named()
    shares = []
    shares_other = []
    states_at = []
    for i in range(chunks):
        first = i % per_seq == 0

        def at_rows(j, i=i):
            return (i, 0)

        def at_block(j, i=i):
            return (i, j)

        def at_turned(j, i=i):
            return (0, i)

        operands = Named()
        for name in ("packed", "bc_conv", "bc_conv_bias", "dt_bias", "a_log"):
            operands[name] = shared[name]
        operands.place = (me, None, None)
        operands.cot = (out_cotangent, (SPAN, model), at_rows)
        operands.out_w = (out_weight, (width, model), lambda j: (j, 0))
        operands.normed = (normed, (SPAN, model), at_rows)
        operands.bc_pre = (bc_pre, (SPAN, 2 * states), at_rows)
        operands.dt_pre = (dt_pre, (SPAN, lanes), at_rows)
        operands.x_pre = (x_pre, (SPAN, width), at_block)
        operands.z_pre = (z_pre, (SPAN, width), at_block)
        before = i * (SPAN // HALO) - 1
        if not first:
            operands.x_halo = (x_pre, (HALO, width), lambda j, b=before: (b, j))
            operands.bc_halo = (bc_pre, (HALO, 2 * states), lambda j, b=before: (b, 0))
            operands.state = columns(states_at[-1])
        outs = Named(
            u_out=(shape(SPAN, model), (SPAN, model), lambda j: (0, 0)),
            state_out=(shape(states, inner), (states, width), lambda j: (0, j)),
            sums=(shape(HALO, rows), (HALO, SPAN), lambda j, i=i: (0, i)),
            normed_t=(shape(model, rows, kind=BF16), (model, SPAN), at_turned),
            cot_t=(shape(model, rows, kind=BF16), (model, SPAN), at_turned),
            mixed=(shape(rows, inner), (SPAN, width), at_block),
        )
        waits = []
        scratch = Named(
            cb=((SPAN, 2 * states), BF16),
            bt=((2 * states, SPAN), BF16),
            scores=((SPAN, SPAN), F32),
            cum_t=((lanes, SPAN), F32),
            parts=((2 * SPAN, lanes), BF16),
            acc=((SPAN, width), F32),
        )
        given = run_kernel(
            functools.partial(fwd_kernel, first, heads, head_dim, blocks, n_dp),
            (blocks,),
            operands,
            outs,
            scratch,
            kept,
            waits,
        )
        shares.append(given.pop("u_out"))
        if i == 0:
            shares_other.append(swap_tensor(shares[-1], n_tensor))
        states_at.append(given.pop("state_out"))
        kept = given

    kept.x_pre, kept.z_pre, kept.bc_pre, kept.dt_pre = x_pre, z_pre, bc_pre, dt_pre
    sums = kept.sums
    sums_other = swap_tensor(sums, n_tensor)

    def sums_at(rows_of, at=lambda i: i):
        block = (HALO, rows_of)
        return {
            "sums": (sums, block, lambda i: (0, at(i))),
            "sums_other": (sums_other, block, lambda i: (0, at(i))),
        }

    operands = Named(sums_at(SPAN))
    operands.packed = (packed, packed.shape, lambda i: (0, 0))
    for name, array in dict(z_pre=kept.z_pre, mixed=kept.mixed).items():
        operands[name] = (array, (SPAN, inner), lambda i: (i, 0))
    operands.cot = (out_cotangent, (SPAN, model), lambda i: (i, 0))
    operands.out_w = (out_weight, out_weight.shape, lambda i: (0, 0))
    outs = Named(
        mg=(shape(rows, inner), (SPAN, inner), lambda i: (i, 0)),
        mixer_out=(shape(rows, inner, kind=BF16), (SPAN, inner), lambda i: (i, 0)),
        z_low=(shape(rows, inner, kind=BF16), (SPAN, inner), lambda i: (i, 0)),
    )
    gates = run_kernel(
        functools.partial(gate_kernel, inner_total, taps, width),
        (chunks,),
        operands,
        outs,
        Named(),
        Named(),
        shares_other[:1],
    )
    for share in shares[1:]:
        shares_other.append(swap_tensor(after(share, sums_other), n_tensor))

    def finished(body, given, out, ours, theirs, at):
        operands = Named(given)
        for name, array in dict(share=ours, share_other=theirs).items():
            operands[name] = (array, (part, model), lambda k: (k, 0))
        outs = Named(out=(shape(rows, model, kind=BF16), (part, model), lambda k: (at + k, 0)))
        carried = Named() if out is None else Named(out=out)
        return run_kernel(body, (ours.shape[0] // part,), operands, outs, Named(), carried).out

    def with_output(out, piece):
        at = piece * SPAN // part
        given = sums_at(part, lambda k: at + k)
        given["xin"] = (block_input, (part, model), lambda k: (at + k, 0))
        kernel = functools.partial(output_kernel, inner_total)
        return finished(kernel, given, out, shares[piece], shares_other[piece], at)

    part = SPAN // 2
    block_output = with_output(None, 0)

    out_product = product(kept.cot_t, 0, model, gates.mixer_out)
    z_low = tied(gates.z_low, *shares_other[1:2], out_product, *([block_output] if chunks > 1 else []))
    kept.z_low, kept.mg = z_low, gates.mg
    normed_left = arranged(kept.normed_t, n_dp)
    z_sum = ScatteredProduct(normed_left, z_low, n_dp)
    if n_dp > 1:
        z_sum.start()
        z_sum.settle()
    y_waits = {0: [out_product], 2: shares_other[2:3]}
    if n_dp > 2:
        z_sum.start()
        y_waits[0] = [out_product, z_sum.send]


    lows = Named()
    carry = Named()
    in_parts = [None] * chunks
    in_other = [None] * chunks
    queue = [sums_other] * 3
    for i in reversed(range(chunks)):
        first = i % per_seq == 0
        last_chunk = i % per_seq == per_seq - 1
        start = i == chunks - 1

        def at_rows(j, i=i):
            return (i, 0)

        def at_block(j, i=i):
            return (i, j)

        operands = Named(shared)
        operands.xin = (block_input, (SPAN, model), at_rows)
        for name in ("bc_pre", "dt_pre"):
            operands[name] = (kept[name], (SPAN, kept[name].shape[1]), at_rows)
        operands.x_w = (x_weight, (model, width), lambda j: (0, jnp.maximum(j - 1, 0)))
        operands.x_w_last = (x_weight, (model, width), lambda j: (0, blocks - 1))
        for name in ("x_pre", "z_pre", "mg", "mixed", "z_low"):
            operands[name] = (kept[name], (SPAN, width), at_block)
        operands.sums = (sums, (HALO, SPAN), lambda j, i=i: (0, i))
        operands.sums_other = (sums_other, (HALO, SPAN), lambda j, i=i: (0, i))
        before = i * (SPAN // HALO) - 1
        if not first:
            operands.x_halo = (kept.x_pre, (HALO, width), lambda j, b=before: (b, j))
            operands.bc_halo = (kept.bc_pre, (HALO, 2 * states), lambda j, b=before: (b, 0))
            operands.state = columns(states_at[i - 1])
        if not last_chunk:
            operands.d_state = columns(carry.d_state_out)
            operands.du_halo = columns(carry.du_halo_out)
            operands.du_bc_halo = whole(carry.du_bc_halo_out)
            operands.x_sums_in = columns(carry.x_sums)
            for name in ("head_sums", "bc_sums", "gain_sums"):
                operands[name + "_in"] = whole(carry[name])
        outs = Named(
            in_part=(shape(SPAN, model), (SPAN, model), lambda j: (0, 0)),
            du_halo_out=(shape(HALO, inner), (HALO, width), lambda j: (0, j)),
            du_bc_halo_out=(shape(HALO, 2 * states), (HALO, 2 * states), lambda j: (0, 0)),
            x_sums=(shape(HALO, inner), (HALO, width), lambda j: (0, j)),
            head_sums=(shape(HALO, lanes), (HALO, lanes), lambda j: (0, 0)),
            bc_sums=(shape(HALO, 2 * states), (HALO, 2 * states), lambda j: (0, 0)),
            gain_sums=(shape(HALO, model), (HALO, model), lambda j: (0, 0)),
            x_low=(shape(rows, inner, kind=BF16), (SPAN, width), at_block),
            side_low=(shape(rows, side_width, kind=BF16), (SPAN, side_width), at_rows),
        )
        waits = y_waits.get(chunks - 1 - i, [])
        if i == 0:
            waits = waits + queue[3:4]
        if not first:
            outs.d_state_out = (shape(states, inner), (states, width), lambda j: (0, j))
        scratch = Named(
            bc_slope=((SPAN, 2 * states), F32),
            bb=((SPAN, 2 * states), BF16),
            cb=((SPAN, 2 * states), BF16),
            ct=((2 * states, SPAN), BF16),
            scores=((SPAN, SPAN), F32),
            d_scores=((SPAN, SPAN), F32),
            dt=((SPAN, lanes), F32),
            cum_t=((lanes, SPAN), F32),
            parts=((2 * SPAN, lanes), BF16),
            db=((SPAN, states), F32),
            dc=((SPAN, states), F32),
            d_cum=((SPAN, lanes), F32),
            d_dt=((SPAN, lanes), F32),
            ng=((SPAN, model), F32),
            x_low_before=((SPAN, width), BF16),
            rows=((SPAN, lanes), F32),
        )
        given = run_kernel(
            functools.partial(bwd_kernel, first, last_chunk, heads, head_dim, inner_total),
            (blocks,),
            operands,
            outs,
            scratch,
            lows,
            waits,
        )
        lows = Named(x_low=given.x_low, side_low=given.side_low)
        in_parts[i] = given.in_part
        queue.append(swap_tensor(in_parts[i], n_tensor))
        in_other[i] = queue[-1]
        if last_chunk and not start:
            for name in ("x_sums", "head_sums", "bc_sums", "gain_sums"):
                given[name] = given[name] + carry[name]
        carry = given

    cut = inner // 2
    z_wait = []
    if n_dp > 4:
        z_sum.settle(carry.head_sums)
        z_sum.start()
        z_wait = [z_sum.send]
    x_low = tied(lows.x_low, *queue[4:5], *z_wait)
    small = jnp.concatenate(
        (
            carry.x_sums[: taps + 3].reshape(-1),
            carry.head_sums[:2, :head_count].reshape(-1),
            carry.gain_sums[0],
            carry.bc_sums[: taps + 1].reshape(-1),
        )
    )
    near_width = cut + side_width
    extra = jnp.pad(small, (0, -small.shape[0] % (16 * near_width))).reshape(-1, near_width)
    near_low = jnp.concatenate((x_low[:, :cut], lows.side_low), axis=1)
    near = ScatteredProduct(normed_left, near_low, n_dp, extra)
    far = ScatteredProduct(normed_left, x_low[:, cut:], n_dp)
    out_part = lax.psum_scatter(out_product, "dp", scatter_dimension=0, tiled=True)
    order = []
    for i in range(1, len(shares)):
        block_output = with_output(block_output, i)

    def with_grad(out, i):
        given = dict(cot=(out_cotangent, (part, model), lambda k: (i * 2 + k, 0)))
        return finished(grad_kernel, given, out, in_parts[i], in_other[i], i * 2)

    input_grads = []
    for i in reversed(range(2, chunks)):
        input_grads.append(with_grad(input_grads[-1] if input_grads else None, i))
    input_grad = input_grads[-1] if input_grads else None
    starts = {(True, 2): [out_part]}
    starts[False, 4] = input_grads[-1:] + queue[5:6]
    if n_dp > 4:
        z_sum.settle(x_low)
        z_sum.start()
        starts[False, 2] = [z_sum.send]

    def step(sum_of):
        if sum_of.stride < n_dp:
            ends = queue[6:7] if sum_of is near and sum_of.stride == 8 else []
            sum_of.settle(*order, *ends)
            done = sum_of.stride == n_dp
            order[:] = [sum_of.total if done else sum_of.send]
            if not done:
                sum_of.start(*starts.get((sum_of is near, sum_of.stride), []))

    for one in (near, far):
        if n_dp > 1:
            one.start()
    for one in (near, far, near):
        step(one)
    while z_sum.stride < n_dp:
        step(z_sum)
    starts[False, 4].append(z_sum.total)
    for one in (far, near) * 8:
        step(one)
    z_weight_grad = z_sum.total
    near_part, far = near.total, far.total
    small = near.extra.reshape(-1)
    side_part = near_part[:, cut:]
    x_weight_grad = jnp.concatenate((near_part[:, :cut], far), axis=1)
    bc_part = side_part[:, : 2 * states]
    dt_weight_grad = side_part[:, 2 * states : 2 * states + head_count]

    bc_part = bc_part.reshape(n_tensor, -1, 2 * states)
    mine = lax.axis_index("tensor")
    theirs = lax.dynamic_index_in_dim(bc_part, 1 - mine, 0, keepdims=False)
    shared_at = (taps + 3) * inner + 2 * head_count
    shared_sums = small[shared_at : shared_at + model + (taps + 1) * 2 * states]
    shared_sums = jnp.pad(shared_sums, (0, -shared_sums.shape[0] % (HALO * 2 * states)))
    shared_sums = shared_sums.reshape(-1, 2 * states)
    ours = lax.dynamic_index_in_dim(bc_part, mine, 0, keepdims=False)
    mixed_rows = jnp.concatenate((theirs, shared_sums), axis=0)
    came = swap_tensor(after(mixed_rows, block_output), n_tensor)
    bc_weight_grad = ours + came[: ours.shape[0]]
    shared_sums = (shared_sums + came[ours.shape[0] :]).reshape(-1)

    x_end = (taps + 3) * inner
    x_sums = small[:x_end].reshape(taps + 3, inner)
    gated_gain_grad = x_sums[0]
    d_skip_grad = x_sums[1].reshape(head_count, head_dim).sum(axis=1)
    x_conv_grad = x_sums[2 : taps + 2]
    x_conv_bias_grad = x_sums[taps + 2]
    dt_bias_grad = small[x_end : x_end + head_count]
    a_log_grad = small[x_end + head_count : x_end + 2 * head_count]
    gain_total = shared_sums[:model]
    bc_total = shared_sums[model : model + (taps + 1) * 2 * states].reshape(taps + 1, 2 * states)
    place = lax.axis_index("dp") * n_tensor + lax.axis_index("tensor")
    places = n_dp * n_tensor

    def own(values, axis):
        size = values.shape[axis] // places
        return lax.dynamic_slice_in_dim(values, place * size, size, axis)

    norm_gain_grad = own(gain_total, 0)
    bc_conv_grad = own(bc_total[:taps], 1)
    bc_conv_bias_grad = own(bc_total[taps], 0)

    out_weight_grad = out_part.T

    if chunks > 1:
        input_grad = with_grad(input_grad, 1)
    in_other[0] = after(in_other[0], far)
    input_grad = with_grad(input_grad, 0)
    return (
        block_output,
        input_grad,
        norm_gain_grad,
        z_weight_grad,
        x_weight_grad,
        bc_weight_grad,
        dt_weight_grad,
        x_conv_grad,
        x_conv_bias_grad,
        bc_conv_grad,
        bc_conv_bias_grad,
        dt_bias_grad,
        a_log_grad,
        d_skip_grad,
        gated_gain_grad,
        out_weight_grad,
    )


def solution(mesh):
    in_specs = (
        P("dp", None),
        P(),
        P(None, "tensor"),
        P(None, "tensor"),
        P(),
        P(None, "tensor"),
        P(None, "tensor"),
        P("tensor"),
        P(),
        P(),
        P("tensor"),
        P("tensor"),
        P("tensor"),
        P("tensor"),
        P("tensor", None),
        P("dp", None),
    )
    out_specs = (
        P("dp", None),
        P("dp", None),
        P(("dp", "tensor")),
        P("dp", "tensor"),
        P("dp", "tensor"),
        P(("dp", "tensor"), None),
        P("dp", "tensor"),
        P(None, "tensor"),
        P("tensor"),
        P(None, ("dp", "tensor")),
        P(("dp", "tensor")),
        P("tensor"),
        P("tensor"),
        P("tensor"),
        P("tensor"),
        P("tensor", "dp"),
    )
    return jax.shard_map(body, mesh=mesh, in_specs=in_specs, out_specs=out_specs, check_vma=False)
```

```python
import functools
import math

import jax
import jax.numpy as jnp
from jax import lax
from jax.experimental import pallas as pl
from jax.experimental.pallas import tpu as pltpu
from jax.sharding import PartitionSpec as P

SPAN = 256
LEN = 1024
EPS = 1e-05
HIGH = lax.Precision.HIGHEST
LOG2E = math.log2(math.e)
F32 = jnp.float32
BF16 = jnp.bfloat16
HALO = 8
GROUP = 32
VMEM = 56 * 1024 * 1024


class Named(dict):
    __getattr__ = dict.get
    __setattr__ = dict.__setitem__


def mm(a, b):
    return lax.dot_general(a, b, (((1,), (0,)), ((), ())), preferred_element_type=F32)


def mm_nt(a, b):
    return lax.dot_general(a, b, (((1,), (1,)), ((), ())), preferred_element_type=F32)


def mm_tn(a, b):
    return lax.dot_general(a, b, (((0,), (0,)), ((), ())), preferred_element_type=F32)


def split3(x):
    hi = x.astype(BF16)
    rest = x - hi.astype(F32)
    mid = rest.astype(BF16)
    low = (rest - mid.astype(F32)).astype(BF16)
    return hi, mid, low


def split2(x):
    hi = x.astype(BF16)
    return hi, (x - hi.astype(F32)).astype(BF16)


def side(a, b):
    return jnp.concatenate((a, b), axis=1)


def folded(x):
    half = x.shape[1] // 2
    return x[:, :half] + x[:, half:]


def fine_nn(left_pair, b):
    bh, bl = split2(b)
    depth = b.shape[0]
    return mm(left_pair, jnp.concatenate((bh, bh), axis=0)) + mm(left_pair[:, :depth], bl)


def fine_rows(left_stack, b):
    bh, bl = split2(b)
    rows = left_stack.shape[0] // 2
    both = mm(left_stack, bh)
    return both[:rows] + both[rows:] + mm(left_stack[:rows], bl)


def fine_nt(a, b):
    ah, al = split2(a)
    bh, bl = split2(b)
    return folded(mm_nt(ah, jnp.concatenate((bh, bl), axis=0))) + mm_nt(al, bh)


def iota(shape, axis):
    return lax.broadcasted_iota(jnp.int32, shape, axis)


def times_transposed(left, right):
    return lax.dot_general(left, right, (((1,), (1,)), ((), ())), preferred_element_type=F32)


def softplus(v):
    return jnp.maximum(v, 0.0) + jnp.log1p(jnp.exp(-jnp.abs(v)))


def three_parts(x):
    hi, mid, low = split3(x)
    lane = iota(x.shape, 1)
    parts = jnp.where(
        lane < GROUP, hi.astype(F32), jnp.where(lane < 2 * GROUP, mid.astype(F32), low.astype(F32))
    )
    return parts.astype(BF16)


def spread_matrix(block, heads, head_dim, lanes):
    shape = (lanes, heads * head_dim)
    row, col = iota(shape, 0), iota(shape, 1)
    head = block * heads + col // head_dim
    hit = (row == head) | (row == head + GROUP) | (row == head + 2 * GROUP)
    return jnp.where(hit, 1.0, 0.0).astype(BF16)


def gather_matrix(block, heads, head_dim, lanes):
    shape = (heads * head_dim, lanes)
    row, col = iota(shape, 0), iota(shape, 1)
    return jnp.where(col == block * heads + row // head_dim, 1.0, 0.0).astype(BF16)


def triangle(n, lower):
    row, col = iota((n, n), 0), iota((n, n), 1)
    return jnp.where(row >= col if lower else row <= col, 1.0, 0.0)


def pair_masks(head_dim):
    lane = iota((1, 4 * head_dim), 1) // head_dim % 2
    return [jnp.where(lane == k, 1.0, 0.0).astype(BF16) for k in range(2)]


def pair_parts(parts, head_dim, pair):
    at = slice(2 * pair * head_dim, 2 * (pair + 1) * head_dim)
    return side(parts[0][:, at], parts[1][:, at])


def earlier(x, halo, by):
    if by == 0:
        return x
    rolled = pltpu.roll(x, by, 0)
    head = iota((HALO, x.shape[1]), 0) < by
    front = pltpu.roll(halo, by, 0) if halo is not None else 0.0
    return jnp.concatenate((jnp.where(head, front, rolled[:HALO]), rolled[HALO:]), axis=0)


def later(x, halo, by):
    if by == 0:
        return x
    rows = x.shape[0]
    rolled = pltpu.roll(x, rows - by, 0)
    tail = iota((HALO, x.shape[1]), 0) >= HALO - by
    back = pltpu.roll(halo, HALO - by, 0) if halo is not None else 0.0
    end = jnp.where(tail, back, rolled[rows - HALO :])
    return jnp.concatenate((rolled[: rows - HALO], end), axis=0)


def conv_of(x, halo, taps, bias):
    count = taps.shape[0]
    shifted = [earlier(x, halo, count - 1 - k) for k in range(count)]
    total = bias + taps[0:1] * shifted[0]
    for k in range(1, count):
        total = total + taps[k : k + 1] * shifted[k]
    return total, shifted


def conv_back(grad, halo, taps):
    count = taps.shape[0]
    total = taps[count - 1 : count] * grad
    for k in range(count - 1):
        total = total + taps[k : k + 1] * later(grad, halo, count - 1 - k)
    return total


def unpacked(ref, taps):
    return ref[:taps], ref[taps : taps + 1], ref[taps + 1 : taps + 2], ref[taps + 2 : taps + 3]


def maybe(ref):
    return None if ref is None else ref[...]


def silu_slope(v, s):
    return s + v * s * (1.0 - s)


def triangle_sum(x, lower):
    lanes = x.shape[1]
    parts = mm(triangle(x.shape[0], lower).astype(BF16), jnp.concatenate(split3(x), axis=1))
    return parts[:, :lanes] + parts[:, lanes : 2 * lanes] + parts[:, 2 * lanes :]


def steps_of(dt_pre, dt_bias_ref, a_log_ref):
    dt = softplus(dt_pre + dt_bias_ref[...])
    decay = -jnp.exp(a_log_ref[...])
    rates = dt * (decay * LOG2E)
    cum = triangle_sum(rates, True)
    return dt, decay, cum


def row_sums(x):
    lanes = 128
    part = x[:, :lanes]
    for at in range(lanes, x.shape[1], lanes):
        part = part + x[:, at : at + lanes]
    return jnp.sum(part.T, axis=0, keepdims=True)


PIECE = 32


def slot_of(rel, n):
    bits = n.bit_length() - 1
    p = sum((rel >> b & 1) << (bits - 1 - b) for b in range(1, bits))
    first, half, quarter = rel & 1, n // 2, n // 4
    return jnp.where(first == 1, p, jnp.where(p >= quarter, half + p - quarter, n - quarter + p))


def arrange_rows(start, n, place, turned, target):
    block = target.shape[0] // n
    if n == 1 or block % PIECE:
        target[pl.ds(pl.multiple_of(start, PIECE), turned.shape[0]), :] = turned
        return
    for at in range(0, turned.shape[0], PIECE):
        begin = start + at
        owner = lax.div(begin, block)
        slot = slot_of(owner ^ place[0], n)
        to = pl.multiple_of(slot * block + begin - owner * block, PIECE)
        target[pl.ds(to, PIECE), :] = turned[at : at + PIECE]


def fwd_kernel(first, heads, head_dim, blocks, n_dp, refs):
    j = pl.program_id(0)
    r = refs
    rows = r.normed.shape[0]
    half = rows // 2
    states = r.bc_pre.shape[1] // 2
    lanes = r.dt_pre.shape[1]

    @pl.when(j == 0)
    def _():
        bc_pre = r.bc_pre[...]
        u, _ = conv_of(bc_pre, maybe(r.bc_halo), r.bc_conv[...], r.bc_conv_bias[...])
        act = u * jax.nn.sigmoid(u)
        b, c = act[:, :states], act[:, states:]
        r.cb[...] = side(*split2(c))
        r.bt[...] = jnp.concatenate(split2(b.T), axis=0)
        r.scores[...] = fine_nt(c, b) * triangle(rows, True)
        dt, decay, cum = steps_of(r.dt_pre[...], r.dt_bias, r.a_log)
        r.cum_t[...] = cum.T
        r.parts[0:rows, :] = three_parts(cum)
        r.parts[rows : 2 * rows, :] = three_parts(dt)
        r.u_out[...] = jnp.zeros_like(r.u_out)
        r.acc[...] = jnp.zeros_like(r.acc)

    width = heads * head_dim
    xp, zp = r.x_pre[...], r.z_pre[...]
    gate = zp * jax.nn.sigmoid(zp)
    columns = r.normed.shape[1] // blocks
    here = pl.ds(pl.multiple_of(j * columns, columns), columns)
    turned = r.normed[:, here].T
    arrange_rows(j * columns, n_dp, r.place, turned, r.normed_t)
    r.cot_t[here, :] = r.cot[:, here].T
    taps = r.bc_conv.shape[0]
    conv, conv_bias, d_skip, gated_gain = unpacked(r.packed, taps)
    u, _ = conv_of(xp, maybe(r.x_halo), conv, conv_bias)
    xa = u * jax.nn.sigmoid(u)
    spread = mm(r.parts[...], spread_matrix(j, heads, head_dim, lanes))
    cum_e, dt_e = spread[:rows], spread[rows:]
    w = xa * dt_e
    last = cum_e[rows - 1 : rows, :]
    scaled = w * jnp.exp2(last - cum_e)
    masks = pair_masks(head_dim)
    parts = split2(w)
    empty = jnp.zeros((half, half), BF16)
    cols = []
    for pair in range(heads // 2):
        both = pair_parts(parts, head_dim, pair)
        total = 0.0
        for k in range(2):
            head = 2 * pair + k
            row = r.cum_t[pl.ds(j * heads + head, 1), :]
            col = cum_e[:, head * head_dim : head * head_dim + 1]
            m = jnp.exp2(jnp.minimum(col[:half] - row[:, :half], 0.0)) * r.scores[:half, :half]
            top = [side(part, empty) for part in split2(m)]
            m = jnp.exp2(jnp.minimum(col[half:] - row, 0.0)) * r.scores[half:, :]
            bot = split2(m)
            stack = jnp.concatenate((top[0], bot[0], top[1], bot[1]), axis=0)
            total = total + mm(stack, both * masks[k])
        cols.append(folded(total[:rows] + total[rows:]))
    y = side(*cols)
    if first:
        r.state_out[...] = fine_rows(r.bt[...], scaled)
    else:
        state = r.state[...]
        y = y + jnp.exp2(cum_e) * fine_nn(r.cb[...], state)
        r.state_out[...] = jnp.exp2(last) * state + fine_rows(r.bt[...], scaled)
    mixed = y + d_skip * xa
    r.mixed[...] = mixed
    gated = mixed * gate
    gain = gated * gated_gain
    r.u_out[...] += mm(gain.astype(BF16), r.out_w[...])
    r.acc[...] += gated * gated

    @pl.when(j == pl.num_programs(0) - 1)
    def _():
        r.sums[0:1, :] = row_sums(r.acc[...])
        r.sums[1:2, :] = row_sums(r.cot[...].astype(F32) * r.u_out[...])
        r.sums[2:HALO, :] = jnp.zeros((HALO - 2, rows), F32)


def row_scales(r, inner_total):
    sums = (r.sums[...] + r.sums_other[...]).T
    rms = lax.rsqrt(sums[:, 0:1] / inner_total + EPS)
    return rms, sums[:, 1:2] * rms / inner_total


def gate_kernel(inner_total, taps, width, r):
    rms, row_dot = row_scales(r, inner_total)
    for start in range(0, r.z_pre.shape[1], width):
        at = slice(start, start + width)
        mg = mm_nt(r.cot[...], r.out_w[at, :])
        r.mg[:, at] = mg
        zp, mixed = r.z_pre[:, at], r.mixed[:, at]
        gain = r.packed[taps + 2 : taps + 3, at]
        sz = jax.nn.sigmoid(zp)
        gated_unit = mixed * (zp * sz) * rms
        r.mixer_out[:, at] = (gated_unit * gain).astype(BF16)
        gg = rms * (mg * gain - gated_unit * row_dot)
        r.z_low[:, at] = (gg * mixed * silu_slope(zp, sz)).astype(BF16)


def output_kernel(inner_total, r):
    rms, _ = row_scales(r, inner_total)
    total = (r.share[...] + r.share_other[...]) * rms
    r.out[...] = (r.xin[...].astype(F32) + total).astype(BF16)


def grad_kernel(r):
    total = r.share[...] + r.share_other[...]
    r.out[...] = (r.cot[...].astype(F32) + total).astype(BF16)


def bwd_kernel(first, last_chunk, heads, head_dim, inner_total, refs):
    j = pl.program_id(0)
    r = refs
    rows = r.xin.shape[0]
    half = rows // 2
    states = r.bc_w.shape[1] // 2
    lanes = r.dt_w.shape[1]
    width = heads * head_dim
    taps = r.bc_conv.shape[0]
    conv, conv_bias, d_skip, gated_gain = unpacked(r.packed, taps)

    def column_sum(v):
        return jnp.sum(v, axis=0, keepdims=True)

    @pl.when(j == 0)
    def _():
        bc_pre = r.bc_pre[...]
        u, _ = conv_of(bc_pre, maybe(r.bc_halo), r.bc_conv[...], r.bc_conv_bias[...])
        s = jax.nn.sigmoid(u)
        act = u * s
        r.bc_slope[...] = silu_slope(u, s)
        b, c = act[:, :states], act[:, states:]
        r.bb[...] = side(*split2(b))
        r.cb[...] = side(*split2(c))
        r.ct[...] = jnp.concatenate(split2(c.T), axis=0)
        r.scores[...] = fine_nt(b, c) * triangle(rows, False)
        dt, decay, cum = steps_of(r.dt_pre[...], r.dt_bias, r.a_log)
        r.dt[...] = dt
        r.cum_t[...] = cum.T
        r.parts[0:rows, :] = three_parts(cum)
        r.parts[rows : 2 * rows, :] = three_parts(dt)
        r.x_low_before[...] = jnp.zeros_like(r.x_low_before)
        for ref in (r.d_scores, r.db, r.dc, r.d_cum, r.d_dt, r.ng):
            ref[...] = jnp.zeros_like(ref)
        rms, row_dot = row_scales(r, inner_total)
        r.rows[:, 0:1] = rms
        r.rows[:, 1:2] = row_dot

    xp = r.x_pre[...]
    u, shifted = conv_of(xp, maybe(r.x_halo), conv, conv_bias)
    su = jax.nn.sigmoid(u)
    xa = u * su
    spread = mm(r.parts[...], spread_matrix(j, heads, head_dim, lanes))
    cum_e, dt_e = spread[:rows], spread[rows:]
    w = xa * dt_e
    last = cum_e[rows - 1 : rows, :]
    rms, row_dot = r.rows[:, 0:1], r.rows[:, 1:2]
    zp, mg, mixed = r.z_pre[...], r.mg[...], r.mixed[...]
    sz = jax.nn.sigmoid(zp)
    gate = zp * sz
    y = mixed - d_skip * xa
    gated_unit = mixed * gate * rms
    gg = rms * (mg * gated_gain - gated_unit * row_dot)
    dy = gg * gate
    sums = [column_sum(mg * gated_unit), column_sum(dy * xa)]
    masks = pair_masks(head_dim)
    w_parts = split2(w)
    dy_parts = split2(dy)
    empty = jnp.zeros((half, half), BF16)
    cols = []
    for pair in range(heads // 2):
        at = slice(2 * pair * head_dim, 2 * (pair + 1) * head_dim)
        w_both = pair_parts(w_parts, head_dim, pair)
        w_high = w_parts[0][:, at]
        dy_both = pair_parts(dy_parts, head_dim, pair)
        dy_high = side(dy_parts[0][:, at], dy_parts[0][:, at])
        dy_low = dy_parts[1][:, at]
        total = 0.0
        for k in range(2):
            head = 2 * pair + k
            row = r.cum_t[pl.ds(j * heads + head, 1), :]
            col = cum_e[:, head * head_dim : head * head_dim + 1]
            dk, dk_high = dy_both * masks[k], dy_high * masks[k]
            dk_low = dy_low * masks[k][:, : 2 * head_dim]
            grad = mm_nt(w_both, dk_high) + mm_nt(w_high, dk_low)
            decay = jnp.exp2(jnp.minimum(row - col[:half], 0.0))
            r.d_scores[:half, :] += grad[:half] * decay
            top = split2(decay * r.scores[:half, :])
            decay = jnp.exp2(jnp.minimum(row[:, half:] - col[half:], 0.0))
            r.d_scores[half:, half:] += grad[half:, half:] * decay
            bot = [side(empty, part) for part in split2(decay * r.scores[half:, half:])]
            stack = jnp.concatenate((top[0], bot[0], top[1], bot[1]), axis=0)
            total = total + mm(stack, dk)
        cols.append(folded(total[:rows] + total[rows:]))
    dw = side(*cols)
    extra = None
    if not last_chunk:
        to_end = jnp.exp2(last - cum_e)
        d_state = r.d_state[...]
        ds = fine_nn(r.bb[...], d_state) * to_end
        r.db[...] += fine_nt(w * to_end, d_state)
        dw = dw + ds
        extra = column_sum(w * ds)
    if not first:
        state = r.state[...]
        g = jnp.exp2(cum_e) * dy
        r.dc[...] += fine_nt(g, state)
        d_state_out = fine_rows(r.ct[...], g)
        if not last_chunk:
            kept = jnp.exp2(last) * d_state
            extra = extra + column_sum(kept * state)
            d_state_out = d_state_out + kept
        r.d_state_out[...] = d_state_out
    q = dy * y - w * dw
    if extra is not None:
        q = q + jnp.where(iota((rows, 1), 0) == rows - 1, 1.0, 0.0) * extra
    gather = gather_matrix(j, heads, head_dim, lanes)
    stack = split3(q) + split2(dw * xa)
    given = mm(jnp.concatenate(stack, axis=0), gather)
    given = [given[at * rows : (at + 1) * rows] for at in range(5)]
    r.d_cum[...] += given[0] + given[1] + given[2]
    r.d_dt[...] += given[3] + given[4]
    du = (d_skip * dy + dw * dt_e) * silu_slope(u, su)
    xg = conv_back(du, maybe(r.du_halo), conv)
    r.du_halo_out[...] = du[:HALO, :]
    for k in range(taps):
        sums.append(column_sum(du * shifted[k]))
    sums.append(column_sum(du))
    for at, value in enumerate(sums):
        before = 0.0 if last_chunk else r.x_sums_in[at : at + 1, :]
        r.x_sums[at : at + 1, :] = value + before
    r.x_sums[len(sums) : HALO, :] = jnp.zeros((HALO - len(sums), width), F32)
    xl = xg.astype(BF16)
    r.x_low[...] = xl
    r.ng[...] += mm_nt(r.z_low[...], r.z_w[...]) + mm_nt(r.x_low_before[...], r.x_w[...])
    r.x_low_before[...] = xl

    @pl.when(j == pl.num_programs(0) - 1)
    def _():
        hi, low = split2(r.d_scores[...] * triangle(rows, False))
        cb, bb = r.cb[...], r.bb[...]
        db = r.db[...] + folded(mm(hi, cb)) + mm(low, cb[:, :states])
        dc = r.dc[...] + folded(mm_tn(hi, bb)) + mm_tn(low, bb[:, :states])
        d_rates = triangle_sum(r.d_cum[...], False)
        dt = r.dt[...]
        decay = -jnp.exp(r.a_log[...])
        d_dt = d_rates * decay + r.d_dt[...]
        dtg = d_dt * jax.nn.sigmoid(r.dt_pre[...] + r.dt_bias[...])
        dtl = jnp.where(iota(dtg.shape, 1) < GROUP, dtg, 0.0).astype(BF16)
        r.side_low[:, 2 * states :] = dtl
        head_sums = [column_sum(dtg), column_sum(d_rates * dt) * decay]
        for at, value in enumerate(head_sums):
            before = 0.0 if last_chunk else r.head_sums_in[at : at + 1, :]
            r.head_sums[at : at + 1, :] = value + before
        r.head_sums[2:HALO, :] = jnp.zeros((HALO - 2, lanes), F32)
        du_bc = jnp.concatenate((db, dc), axis=1) * r.bc_slope[...]
        bg = conv_back(du_bc, maybe(r.du_bc_halo), r.bc_conv[...])
        r.du_bc_halo_out[...] = du_bc[:HALO, :]
        bc_sums = []
        for k in range(taps):
            near = earlier(r.bc_pre[...], maybe(r.bc_halo), taps - 1 - k)
            bc_sums.append(column_sum(du_bc * near))
        bc_sums.append(column_sum(du_bc))
        for at, value in enumerate(bc_sums):
            before = 0.0 if last_chunk else r.bc_sums_in[at : at + 1, :]
            r.bc_sums[at : at + 1, :] = value + before
        r.bc_sums[len(bc_sums) : HALO, :] = jnp.zeros((HALO - len(bc_sums), 2 * states), F32)
        bl = bg.astype(BF16)
        r.side_low[:, : 2 * states] = bl
        ng = r.ng[...] + mm_nt(bl, r.bc_w[...]) + mm_nt(dtl, r.dt_w[...])
        ng = ng + mm_nt(xl, r.x_w_last[...])
        res = r.xin[...].astype(F32)
        inv = lax.rsqrt(jnp.mean(res * res, axis=1, keepdims=True) + EPS)
        unit = res * inv
        gain_sum = column_sum(ng * unit)
        r.gain_sums[0:1, :] = gain_sum if last_chunk else gain_sum + r.gain_sums_in[0:1, :]
        r.gain_sums[1:HALO, :] = jnp.zeros((HALO - 1, gain_sum.shape[1]), F32)
        iu = ng * r.norm_gain[...]
        r.in_part[...] = inv * (iu - unit * jnp.mean(iu * unit, axis=1, keepdims=True))


def run_kernel(body, grid, operands, outs, scratch, carried, waits=(), flops=1):
    names, arrays, specs = [], [], []
    for name, (array, block, index) in operands.items():
        names.append(name)
        arrays.append(array)
        whole = pl.BlockSpec(memory_space=pltpu.SMEM)
        specs.append(whole if block is None else pl.BlockSpec(block, index))
    aliases = {}
    out_names = list(outs)
    for at, name in enumerate(out_names):
        if name in carried:
            aliases[len(arrays)] = at
            names.append(name + "_old")
            arrays.append(carried[name])
            specs.append(pl.BlockSpec(memory_space=pl.ANY))
    for at, array in enumerate(waits):
        names.append(at)
        arrays.append(array)
        specs.append(pl.BlockSpec(memory_space=pl.ANY))
    scratch_names = list(scratch)

    def kernel(*refs):
        body(Named(zip(names + out_names + scratch_names, refs)))

    given = pl.pallas_call(
        kernel,
        grid=grid,
        in_specs=specs,
        out_specs=[pl.BlockSpec(block, index) for _, block, index in outs.values()],
        out_shape=[shape for shape, _, _ in outs.values()],
        scratch_shapes=[pltpu.VMEM(shape, kind) for shape, kind in scratch.values()],
        input_output_aliases=aliases,
        compiler_params=pltpu.CompilerParams(
            dimension_semantics=("arbitrary",) * len(grid), vmem_limit_bytes=VMEM
        ),
        cost_estimate=pl.CostEstimate(flops=flops, bytes_accessed=1, transcendentals=0),
    )(*arrays)
    return Named(zip(out_names, given))


def shape(*dims, kind=F32):
    return jax.ShapeDtypeStruct(dims, kind)


def relative_masks(n, flip):
    bits = n.bit_length() - 1
    masks = []
    for p in range(n // 2):
        masks.append(flip + sum((p >> (bits - 1 - b) & 1) << b for b in range(1, bits)))
    return masks


def arranged(left, n):
    if n == 1:
        return None, left, left[:0]
    block = left.shape[0] // n
    me = lax.axis_index("dp")
    if block % PIECE == 0:
        half, quarter = left.shape[0] // 2, left.shape[0] // 4
        return left[:half], left[half : half + quarter], left[half + quarter :]

    def pick(masks):
        rows = [lax.dynamic_slice_in_dim(left, (me ^ mask) * block, block, 0) for mask in masks]
        return jnp.concatenate(rows, axis=0)

    kept = relative_masks(n, 0)
    half = len(kept) // 2
    if not half:
        return pick(relative_masks(n, 1)), pick(kept), left[:0]
    return pick(relative_masks(n, 1)), pick(kept[half:]), pick(kept[:half])


def product(left, at, rows, right, came=None, came_at=0):
    depth, columns = right.shape
    step = next(size for size in (512, 384, 256, 128) if columns % size == 0)
    arrays, specs = [left, right], [
        pl.BlockSpec((rows, depth), lambda j: (at, 0)),
        pl.BlockSpec((depth, step), lambda j: (0, j)),
    ]
    if came is not None:
        arrays.append(came)
        specs.append(pl.BlockSpec((rows, step), lambda j: (came_at, j)))

    def kernel(*refs):
        given = mm(refs[0][...], refs[1][...])
        refs[-1][...] = given if came is None else given + refs[2][...]

    return pl.pallas_call(
        kernel,
        grid=(columns // step,),
        in_specs=specs,
        out_specs=pl.BlockSpec((rows, step), lambda j: (0, j)),
        out_shape=shape(rows, columns),
        compiler_params=pltpu.CompilerParams(
            dimension_semantics=("arbitrary",), vmem_limit_bytes=VMEM
        ),
        cost_estimate=pl.CostEstimate(flops=1, bytes_accessed=1, transcendentals=0),
    )(*arrays)


class ScatteredProduct:
    def __init__(self, left, right, n, extra=None):
        self.n, self.stride, self.left, self.right, self.extra = n, 1, left, right, extra
        if n == 1:
            self.total = mm(left[1], right)
        else:
            self.send = mm(left[0], right)

    def start(self, *others):
        pairs = [(p, p ^ self.stride) for p in range(self.n)]
        if self.stride == 1 and self.extra is not None:
            self.extra = self.extra + lax.ppermute(self.extra, "dp", pairs)
        self.came = lax.ppermute(after(self.send, *others), "dp", pairs)

    def settle(self, *others):
        came = after(self.came, *others)
        if self.stride == 1:
            rows = self.left[2].shape[0]
            keep = mm(self.left[2], self.right) + came[:rows]
            send = mm(self.left[1], self.right) + came[rows:]
        else:
            size = self.keep.shape[0]
            rows = size // 2 if 2 * self.stride < self.n else 0
            if self.extra is not None:
                self.extra = self.extra + came[size:]
            keep, send = self.keep[:rows] + came[:rows], self.keep[rows:] + came[rows:size]
        self.stride *= 2
        if self.stride == self.n:
            self.total = send
            return
        if self.extra is not None:
            send = jnp.concatenate((send, self.extra), axis=0)
        self.keep, self.send = keep, send

    def finish(self):
        while self.stride < self.n:
            self.start()
            self.settle()
        return self.total


def after(values, *others):
    return lax.optimization_barrier((values,) + others)[0]


def tied(array, *waits):
    def nothing(*refs):
        pass

    anywhere = pl.BlockSpec(memory_space=pl.ANY)
    out = pl.pallas_call(
        nothing,
        in_specs=[anywhere] * (1 + len(waits)),
        out_specs=anywhere,
        out_shape=jax.ShapeDtypeStruct(array.shape, array.dtype),
        input_output_aliases={0: 0},
        cost_estimate=pl.CostEstimate(flops=1, bytes_accessed=1, transcendentals=0),
    )(array, *waits)
    return out


def swap_tensor(values, n):
    return lax.ppermute(values, "tensor", [(t, t ^ 1) for t in range(n)])


def body(
    block_input,
    norm_gain,
    z_weight,
    x_weight,
    bc_weight,
    dt_weight,
    x_conv,
    x_conv_bias,
    bc_conv,
    bc_conv_bias,
    dt_bias,
    a_log,
    d_skip,
    gated_gain,
    out_weight,
    out_cotangent,
):
    n_dp, n_tensor = lax.axis_size("dp"), lax.axis_size("tensor")
    rows, model = block_input.shape
    inner = x_weight.shape[1]
    head_count = dt_weight.shape[1]
    head_dim = inner // head_count
    states = bc_weight.shape[1] // 2
    taps = x_conv.shape[0]
    heads = 4
    width = heads * head_dim
    blocks = inner // width
    chunks = rows // SPAN
    per_seq = LEN // SPAN
    inner_total = inner * n_tensor
    me = lax.axis_index("dp").astype(jnp.int32).reshape(1)
    lanes = 128
    side_width = 2 * states + lanes

    def tripled(v):
        one = jnp.pad(v, ((0, 0), (0, GROUP - head_count)))
        return jnp.pad(jnp.concatenate((one, one, one), axis=1), ((0, 0), (0, lanes - 3 * GROUP)))

    dt_w = tripled(dt_weight)
    dt_b = tripled(dt_bias[None])
    a_l = tripled(a_log[None])
    skip = jnp.repeat(d_skip, head_dim)[None]
    packed = jnp.concatenate((x_conv, x_conv_bias[None], skip, gated_gain[None]), axis=0)
    packed = jnp.pad(packed, ((0, HALO - packed.shape[0] % HALO), (0, 0)))
    gain_in = norm_gain[None]
    bc_bias = bc_conv_bias[None]

    def whole(array):
        return (array, array.shape, lambda j: (0,) * array.ndim)

    def columns(array):
        return (array, (array.shape[0], width), lambda j: (0, j))

    shared = Named(
        norm_gain=whole(gain_in),
        x_w=columns(x_weight),
        z_w=columns(z_weight),
        bc_w=whole(bc_weight),
        dt_w=whole(dt_w),
        packed=columns(packed),
        bc_conv=whole(bc_conv),
        bc_conv_bias=whole(bc_bias),
        dt_bias=whole(dt_b),
        a_log=whole(a_l),
    )

    residual = block_input.astype(F32)
    inv_rms = lax.rsqrt(jnp.mean(residual * residual, axis=1, keepdims=True) + EPS)
    normed = (residual * inv_rms * gain_in).astype(BF16)
    side_pre = mm(normed, jnp.concatenate((bc_weight, dt_w), axis=1))
    bc_pre, dt_pre = side_pre[:, : 2 * states], side_pre[:, 2 * states :]
    x_pre = mm(normed, x_weight)
    z_pre = mm(normed, z_weight)

    kept = Named()
    shares = []
    shares_other = []
    states_at = []
    for i in range(chunks):
        first = i % per_seq == 0

        def at_rows(j, i=i):
            return (i, 0)

        def at_block(j, i=i):
            return (i, j)

        def at_turned(j, i=i):
            return (0, i)

        operands = Named()
        for name in ("packed", "bc_conv", "bc_conv_bias", "dt_bias", "a_log"):
            operands[name] = shared[name]
        operands.place = (me, None, None)
        operands.cot = (out_cotangent, (SPAN, model), at_rows)
        operands.out_w = (out_weight, (width, model), lambda j: (j, 0))
        operands.normed = (normed, (SPAN, model), at_rows)
        operands.bc_pre = (bc_pre, (SPAN, 2 * states), at_rows)
        operands.dt_pre = (dt_pre, (SPAN, lanes), at_rows)
        operands.x_pre = (x_pre, (SPAN, width), at_block)
        operands.z_pre = (z_pre, (SPAN, width), at_block)
        before = i * (SPAN // HALO) - 1
        if not first:
            operands.x_halo = (x_pre, (HALO, width), lambda j, b=before: (b, j))
            operands.bc_halo = (bc_pre, (HALO, 2 * states), lambda j, b=before: (b, 0))
            operands.state = columns(states_at[-1])
        outs = Named(
            u_out=(shape(SPAN, model), (SPAN, model), lambda j: (0, 0)),
            state_out=(shape(states, inner), (states, width), lambda j: (0, j)),
            sums=(shape(HALO, rows), (HALO, SPAN), lambda j, i=i: (0, i)),
            normed_t=(shape(model, rows, kind=BF16), (model, SPAN), at_turned),
            cot_t=(shape(model, rows, kind=BF16), (model, SPAN), at_turned),
            mixed=(shape(rows, inner), (SPAN, width), at_block),
        )
        waits = []
        scratch = Named(
            cb=((SPAN, 2 * states), BF16),
            bt=((2 * states, SPAN), BF16),
            scores=((SPAN, SPAN), F32),
            cum_t=((lanes, SPAN), F32),
            parts=((2 * SPAN, lanes), BF16),
            acc=((SPAN, width), F32),
        )
        given = run_kernel(
            functools.partial(fwd_kernel, first, heads, head_dim, blocks, n_dp),
            (blocks,),
            operands,
            outs,
            scratch,
            kept,
            waits,
        )
        shares.append(given.pop("u_out"))
        if i == 0:
            shares_other.append(swap_tensor(shares[-1], n_tensor))
        states_at.append(given.pop("state_out"))
        kept = given

    kept.x_pre, kept.z_pre, kept.bc_pre, kept.dt_pre = x_pre, z_pre, bc_pre, dt_pre
    sums = kept.sums
    sums_other = swap_tensor(sums, n_tensor)

    def sums_at(rows_of, at=lambda i: i):
        block = (HALO, rows_of)
        return {
            "sums": (sums, block, lambda i: (0, at(i))),
            "sums_other": (sums_other, block, lambda i: (0, at(i))),
        }

    operands = Named(sums_at(SPAN))
    operands.packed = (packed, packed.shape, lambda i: (0, 0))
    for name, array in dict(z_pre=kept.z_pre, mixed=kept.mixed).items():
        operands[name] = (array, (SPAN, inner), lambda i: (i, 0))
    operands.cot = (out_cotangent, (SPAN, model), lambda i: (i, 0))
    operands.out_w = (out_weight, out_weight.shape, lambda i: (0, 0))
    outs = Named(
        mg=(shape(rows, inner), (SPAN, inner), lambda i: (i, 0)),
        mixer_out=(shape(rows, inner, kind=BF16), (SPAN, inner), lambda i: (i, 0)),
        z_low=(shape(rows, inner, kind=BF16), (SPAN, inner), lambda i: (i, 0)),
    )
    gates = run_kernel(
        functools.partial(gate_kernel, inner_total, taps, width),
        (chunks,),
        operands,
        outs,
        Named(),
        Named(),
        shares_other[:1],
    )
    for share in shares[1:]:
        shares_other.append(swap_tensor(after(share, sums_other), n_tensor))

    def finished(body, given, out, ours, theirs, at):
        operands = Named(given)
        for name, array in dict(share=ours, share_other=theirs).items():
            operands[name] = (array, (part, model), lambda k: (k, 0))
        outs = Named(out=(shape(rows, model, kind=BF16), (part, model), lambda k: (at + k, 0)))
        carried = Named() if out is None else Named(out=out)
        return run_kernel(body, (ours.shape[0] // part,), operands, outs, Named(), carried).out

    def with_output(out, piece):
        at = piece * SPAN // part
        given = sums_at(part, lambda k: at + k)
        given["xin"] = (block_input, (part, model), lambda k: (at + k, 0))
        kernel = functools.partial(output_kernel, inner_total)
        return finished(kernel, given, out, shares[piece], shares_other[piece], at)

    part = SPAN // 2
    block_output = with_output(None, 0)

    out_product = product(kept.cot_t, 0, model, gates.mixer_out)
    z_low = tied(gates.z_low, *shares_other[1:2], out_product, *([block_output] if chunks > 1 else []))
    kept.z_low, kept.mg = z_low, gates.mg
    normed_left = arranged(kept.normed_t, n_dp)
    z_sum = ScatteredProduct(normed_left, z_low, n_dp)
    if n_dp > 1:
        z_sum.start()
        z_sum.settle()
    y_waits = {0: [out_product], 2: shares_other[2:3]}
    if n_dp > 2:
        z_sum.start()
        y_waits[0] = [out_product, z_sum.send]


    lows = Named()
    carry = Named()
    in_parts = [None] * chunks
    in_other = [None] * chunks
    queue = [sums_other] * 3
    for i in reversed(range(chunks)):
        first = i % per_seq == 0
        last_chunk = i % per_seq == per_seq - 1
        start = i == chunks - 1

        def at_rows(j, i=i):
            return (i, 0)

        def at_block(j, i=i):
            return (i, j)

        operands = Named(shared)
        operands.xin = (block_input, (SPAN, model), at_rows)
        for name in ("bc_pre", "dt_pre"):
            operands[name] = (kept[name], (SPAN, kept[name].shape[1]), at_rows)
        operands.x_w = (x_weight, (model, width), lambda j: (0, jnp.maximum(j - 1, 0)))
        operands.x_w_last = (x_weight, (model, width), lambda j: (0, blocks - 1))
        for name in ("x_pre", "z_pre", "mg", "mixed", "z_low"):
            operands[name] = (kept[name], (SPAN, width), at_block)
        operands.sums = (sums, (HALO, SPAN), lambda j, i=i: (0, i))
        operands.sums_other = (sums_other, (HALO, SPAN), lambda j, i=i: (0, i))
        before = i * (SPAN // HALO) - 1
        if not first:
            operands.x_halo = (kept.x_pre, (HALO, width), lambda j, b=before: (b, j))
            operands.bc_halo = (kept.bc_pre, (HALO, 2 * states), lambda j, b=before: (b, 0))
            operands.state = columns(states_at[i - 1])
        if not last_chunk:
            operands.d_state = columns(carry.d_state_out)
            operands.du_halo = columns(carry.du_halo_out)
            operands.du_bc_halo = whole(carry.du_bc_halo_out)
            operands.x_sums_in = columns(carry.x_sums)
            for name in ("head_sums", "bc_sums", "gain_sums"):
                operands[name + "_in"] = whole(carry[name])
        outs = Named(
            in_part=(shape(SPAN, model), (SPAN, model), lambda j: (0, 0)),
            du_halo_out=(shape(HALO, inner), (HALO, width), lambda j: (0, j)),
            du_bc_halo_out=(shape(HALO, 2 * states), (HALO, 2 * states), lambda j: (0, 0)),
            x_sums=(shape(HALO, inner), (HALO, width), lambda j: (0, j)),
            head_sums=(shape(HALO, lanes), (HALO, lanes), lambda j: (0, 0)),
            bc_sums=(shape(HALO, 2 * states), (HALO, 2 * states), lambda j: (0, 0)),
            gain_sums=(shape(HALO, model), (HALO, model), lambda j: (0, 0)),
            x_low=(shape(rows, inner, kind=BF16), (SPAN, width), at_block),
            side_low=(shape(rows, side_width, kind=BF16), (SPAN, side_width), at_rows),
        )
        waits = y_waits.get(chunks - 1 - i, [])
        if i == 0:
            waits = waits + queue[3:4]
        if not first:
            outs.d_state_out = (shape(states, inner), (states, width), lambda j: (0, j))
        scratch = Named(
            bc_slope=((SPAN, 2 * states), F32),
            bb=((SPAN, 2 * states), BF16),
            cb=((SPAN, 2 * states), BF16),
            ct=((2 * states, SPAN), BF16),
            scores=((SPAN, SPAN), F32),
            d_scores=((SPAN, SPAN), F32),
            dt=((SPAN, lanes), F32),
            cum_t=((lanes, SPAN), F32),
            parts=((2 * SPAN, lanes), BF16),
            db=((SPAN, states), F32),
            dc=((SPAN, states), F32),
            d_cum=((SPAN, lanes), F32),
            d_dt=((SPAN, lanes), F32),
            ng=((SPAN, model), F32),
            x_low_before=((SPAN, width), BF16),
            rows=((SPAN, lanes), F32),
        )
        given = run_kernel(
            functools.partial(bwd_kernel, first, last_chunk, heads, head_dim, inner_total),
            (blocks,),
            operands,
            outs,
            scratch,
            lows,
            waits,
        )
        lows = Named(x_low=given.x_low, side_low=given.side_low)
        in_parts[i] = given.in_part
        queue.append(swap_tensor(in_parts[i], n_tensor))
        in_other[i] = queue[-1]
        if last_chunk and not start:
            for name in ("x_sums", "head_sums", "bc_sums", "gain_sums"):
                given[name] = given[name] + carry[name]
        carry = given

    cut = inner // 3
    z_wait = []
    if n_dp > 4:
        z_sum.settle(carry.head_sums)
        z_sum.start()
        z_wait = [z_sum.send]
    x_low = tied(lows.x_low, *queue[4:5], *z_wait)
    small = jnp.concatenate(
        (
            carry.x_sums[: taps + 3].reshape(-1),
            carry.head_sums[:2, :head_count].reshape(-1),
            carry.gain_sums[0],
            carry.bc_sums[: taps + 1].reshape(-1),
        )
    )
    near_width = cut + side_width
    extra = jnp.pad(small, (0, -small.shape[0] % (16 * near_width))).reshape(-1, near_width)
    near_low = jnp.concatenate((x_low[:, :cut], lows.side_low), axis=1)
    near = ScatteredProduct(normed_left, near_low, n_dp, extra)
    far = ScatteredProduct(normed_left, x_low[:, cut:], n_dp)
    out_part = lax.psum_scatter(out_product, "dp", scatter_dimension=0, tiled=True)
    order = []
    for i in range(1, len(shares)):
        block_output = with_output(block_output, i)

    def with_grad(out, i):
        given = dict(cot=(out_cotangent, (part, model), lambda k: (i * 2 + k, 0)))
        return finished(grad_kernel, given, out, in_parts[i], in_other[i], i * 2)

    input_grads = []
    for i in reversed(range(2, chunks)):
        input_grads.append(with_grad(input_grads[-1] if input_grads else None, i))
    input_grad = input_grads[-1] if input_grads else None
    starts = {(True, 2): [out_part]}
    starts[False, 4] = input_grads[-1:] + queue[5:6]
    if n_dp > 4:
        z_sum.settle(x_low)
        z_sum.start()
        starts[False, 2] = [z_sum.send]

    def step(sum_of):
        if sum_of.stride < n_dp:
            ends = queue[6:7] if sum_of is near and sum_of.stride == 8 else []
            sum_of.settle(*order, *ends)
            done = sum_of.stride == n_dp
            order[:] = [sum_of.total if done else sum_of.send]
            if not done:
                sum_of.start(*starts.get((sum_of is near, sum_of.stride), []))

    for one in (near, far):
        if n_dp > 1:
            one.start()
    for one in (near, far, near):
        step(one)
    while z_sum.stride < n_dp:
        step(z_sum)
    starts[False, 4].append(z_sum.total)
    for one in (far, near) * 8:
        step(one)
    z_weight_grad = z_sum.total
    near_part, far = near.total, far.total
    small = near.extra.reshape(-1)
    side_part = near_part[:, cut:]
    x_weight_grad = jnp.concatenate((near_part[:, :cut], far), axis=1)
    bc_part = side_part[:, : 2 * states]
    dt_weight_grad = side_part[:, 2 * states : 2 * states + head_count]

    bc_part = bc_part.reshape(n_tensor, -1, 2 * states)
    mine = lax.axis_index("tensor")
    theirs = lax.dynamic_index_in_dim(bc_part, 1 - mine, 0, keepdims=False)
    shared_at = (taps + 3) * inner + 2 * head_count
    shared_sums = small[shared_at : shared_at + model + (taps + 1) * 2 * states]
    shared_sums = jnp.pad(shared_sums, (0, -shared_sums.shape[0] % (HALO * 2 * states)))
    shared_sums = shared_sums.reshape(-1, 2 * states)
    ours = lax.dynamic_index_in_dim(bc_part, mine, 0, keepdims=False)
    mixed_rows = jnp.concatenate((theirs, shared_sums), axis=0)
    came = swap_tensor(after(mixed_rows, block_output), n_tensor)
    bc_weight_grad = ours + came[: ours.shape[0]]
    shared_sums = (shared_sums + came[ours.shape[0] :]).reshape(-1)

    x_end = (taps + 3) * inner
    x_sums = small[:x_end].reshape(taps + 3, inner)
    gated_gain_grad = x_sums[0]
    d_skip_grad = x_sums[1].reshape(head_count, head_dim).sum(axis=1)
    x_conv_grad = x_sums[2 : taps + 2]
    x_conv_bias_grad = x_sums[taps + 2]
    dt_bias_grad = small[x_end : x_end + head_count]
    a_log_grad = small[x_end + head_count : x_end + 2 * head_count]
    gain_total = shared_sums[:model]
    bc_total = shared_sums[model : model + (taps + 1) * 2 * states].reshape(taps + 1, 2 * states)
    place = lax.axis_index("dp") * n_tensor + lax.axis_index("tensor")
    places = n_dp * n_tensor

    def own(values, axis):
        size = values.shape[axis] // places
        return lax.dynamic_slice_in_dim(values, place * size, size, axis)

    norm_gain_grad = own(gain_total, 0)
    bc_conv_grad = own(bc_total[:taps], 1)
    bc_conv_bias_grad = own(bc_total[taps], 0)

    out_weight_grad = out_part.T

    if chunks > 1:
        input_grad = with_grad(input_grad, 1)
    in_other[0] = after(in_other[0], far)
    input_grad = with_grad(input_grad, 0)
    return (
        block_output,
        input_grad,
        norm_gain_grad,
        z_weight_grad,
        x_weight_grad,
        bc_weight_grad,
        dt_weight_grad,
        x_conv_grad,
        x_conv_bias_grad,
        bc_conv_grad,
        bc_conv_bias_grad,
        dt_bias_grad,
        a_log_grad,
        d_skip_grad,
        gated_gain_grad,
        out_weight_grad,
    )


def solution(mesh):
    in_specs = (
        P("dp", None),
        P(),
        P(None, "tensor"),
        P(None, "tensor"),
        P(),
        P(None, "tensor"),
        P(None, "tensor"),
        P("tensor"),
        P(),
        P(),
        P("tensor"),
        P("tensor"),
        P("tensor"),
        P("tensor"),
        P("tensor", None),
        P("dp", None),
    )
    out_specs = (
        P("dp", None),
        P("dp", None),
        P(("dp", "tensor")),
        P("dp", "tensor"),
        P("dp", "tensor"),
        P(("dp", "tensor"), None),
        P("dp", "tensor"),
        P(None, "tensor"),
        P("tensor"),
        P(None, ("dp", "tensor")),
        P(("dp", "tensor")),
        P("tensor"),
        P("tensor"),
        P("tensor"),
        P("tensor"),
        P("tensor", "dp"),
    )
    return jax.shard_map(body, mesh=mesh, in_specs=in_specs, out_specs=out_specs, check_vma=False)
```
